128 devices in a mesh: dp: 64 (over z, x_hi, y, core), tensor: 2 (over x_lo).
Axes of the slice: x: 4 (x_hi: 2, x_lo: 2; x = x_hi * 2 + x_lo), y: 4, z: 4, core: 2. Of those that a mesh axis runs over, the one named last changes fastest.
Arguments:
- tokens: bfloat16 [16384, 2048], P(('dp', 'tensor')), may hold values from -6 to 6
- positions: int32 [16384], P('dp'), may hold values from 0 to 1023, as said below
- norm_in: float32 [2048], replicated, may hold values from 0.5 to 1.5
- query_weight: bfloat16 [2048, 4096], P('dp', 'tensor'), may hold values from -0.125 to 0.125
- key_weight: bfloat16 [2048, 512], P('dp', 'tensor'), may hold values from -0.125 to 0.125
- value_weight: bfloat16 [2048, 512], P('dp', 'tensor'), may hold values from -0.125 to 0.125
- query_gain: float32 [128], replicated, may hold values from 0.5 to 1.5
- key_gain: float32 [128], replicated, may hold values from 0.5 to 1.5
- out_weight: bfloat16 [4096, 2048], P('tensor', 'dp'), may hold values from -0.5 to 0.5
- norm_mid: float32 [2048], replicated, may hold values from 0.5 to 1.5
- routed_experts: int32 [16384, 8], P(('dp', 'tensor')), may hold values from 0 to 63, all different within a row; in each aligned block of 128 rows (0 to 127, 128 to 255, ...) at most 20 rows name the same one
- route_weight: float32 [16384, 8], P(('dp', 'tensor')), may hold values from 0.05 to 0.5
- gate_weight: bfloat16 [64, 2048, 768], P('dp', None, 'tensor'), may hold values from -0.125 to 0.125
- up_weight: bfloat16 [64, 2048, 768], P('dp', None, 'tensor'), may hold values from -0.125 to 0.125
- down_weight: bfloat16 [64, 768, 2048], P('dp', 'tensor'), may hold values from -0.625 to 0.625
- out_grad: bfloat16 [16384, 2048], P(('dp', 'tensor')), may hold values from -6 to 6
Outputs:
- output: bfloat16 [16384, 2048], P(('dp', 'tensor'))
- grad_tokens: bfloat16 [16384, 2048], P(('dp', 'tensor'))
- grad_norm_in: float32 [2048], replicated
- grad_query: float32 [2048, 4096], P('dp', 'tensor')
- grad_key: float32 [2048, 512], P('dp', 'tensor')
- grad_value: float32 [2048, 512], P('dp', 'tensor')
- grad_query_gain: float32 [128], replicated
- grad_key_gain: float32 [128], replicated
- grad_out_proj: float32 [4096, 2048], P('tensor', 'dp')
- grad_norm_mid: float32 [2048], replicated
- grad_route: float32 [16384, 8], P(('dp', 'tensor'))
- grad_gate: float32 [64, 2048, 768], P('dp', None, 'tensor')
- grad_up: float32 [64, 2048, 768], P('dp', None, 'tensor')
- grad_down: float32 [64, 768, 2048], P('dp', 'tensor')
The draws below stay inside these ranges and needn't reach their ends.
Inputs may be any that keep to these rules, and one draw needn't show every extreme that they name: Within each sequence of 256 tokens the positions rise, by one or two from each token to the next. `routed_experts`: each row names 8 different experts; in the rows of one device no expert is named by more than 20 rows.
All inputs are finite; a program needn't handle non-finite values.
Results may differ from the reference program's by a relative error of at most 0.02.
Values may be sent and summed in bfloat16 or wider, within the bound.
A program may use at most 320 MiB of HBM per device.

```python
import math
import jax
import jax.numpy as jnp
import numpy as np
from jax import lax

D = 2048
QH = 32
KVH = 4
HD = 128
FF = 768
TOP = 8
TOK_DEV = 128
SEQ = 256
TOKENS = 16384
EXPERTS = 64
CAP = 20


def draw_positions(key, part):
    count = TOKENS // SEQ
    keys = jax.random.split(key, 4)
    top_offset = 2 * SEQ + 1
    offsets = jax.random.randint(keys[0], (count,), 0, top_offset + 1, dtype=jnp.int32)
    first = jax.random.randint(keys[1], (), 0, count, dtype=jnp.int32)
    second = (first + 1 + jax.random.randint(keys[2], (), 0, count - 1, dtype=jnp.int32)) % count
    offsets = offsets.at[first].set(0).at[second].set(top_offset)
    steps = jax.random.randint(keys[3], (count, SEQ), 1, 3, dtype=jnp.int32)
    longest = jnp.arange(count, dtype=jnp.int32)[:, None] == second
    steps = jnp.where(longest, jnp.full((count, SEQ), 2, jnp.int32), steps)
    steps = steps.at[:, 0].set(0)
    rising = jnp.cumsum(steps, axis=1).astype(jnp.int32)
    return (offsets[:, None] + rising).reshape(-1).astype(jnp.int32)


def block_levels(own_key, extent, pieces, low, high):
    factor_of, own = 1.0, jax.random.fold_in(own_key, 6)
    for axis_at, parts in pieces:
        draws = jnp.exp(jax.random.uniform(jax.random.fold_in(own, axis_at), (parts,), jnp.float32, low / len(pieces), high / len(pieces)))
        factor_of = factor_of * jnp.repeat(draws, extent[axis_at] // parts).reshape([-1 if axis == axis_at else 1 for axis in range(len(extent))])
    return factor_of


def deal_out(own_key, own, number, rows, count, top, bound, slope):
    order = jax.random.permutation(own_key, count)
    packed, common = portions_of(count, rows * top, bound, slope, True), portions_of(count, rows * top, bound, slope, False)
    places = jnp.arange(count)

    def named(tallies, rotation):
        used = int((tallies > 0).sum())
        fixed = max(1, used // 4)
        passed = fixed + (places - fixed + rotation * (used - fixed)) % max(1, count - fixed)
        return jnp.zeros((count,), jnp.int32).at[order[jnp.where(places < fixed, places, passed)]].set(jnp.asarray(tallies, jnp.int32))

    tallies = jnp.where(number % 4 == 0, named(packed, number // 4), named(common, number - number // 4 - 1))
    mixed = jax.random.permutation(jax.random.fold_in(own, 3), count)
    source_of, sink = mixed[0:count // 2 * 2:2], mixed[1:count // 2 * 2:2]
    slack = jnp.minimum(tallies[source_of] - 1, bound - tallies[sink]) // 2
    slack = jnp.where((source_of == order[0]) | (sink == order[0]) | (tallies[sink] == 0), 0, jnp.maximum(slack, 0))
    passed = jax.random.randint(jax.random.fold_in(own, 4), (count // 2,), 0, 1 << 20) % (slack + 1)
    tallies = tallies.at[source_of].add(-passed).at[sink].add(passed)
    labels = jnp.searchsorted(jnp.cumsum(tallies), jnp.arange(rows * top), side="right").astype(jnp.int32)
    listing = labels.reshape(top, rows).T
    listing = listing[jax.random.permutation(jax.random.fold_in(own, 1), rows)]
    rotation = jax.random.randint(jax.random.fold_in(own, 2), (rows, 1), 0, top)
    return jnp.take_along_axis(listing, (jnp.arange(top)[None, :] + rotation) % top, axis=1)


def portions_of(amount, total, bound, lean, full):
    portions = [(1 << 20) // math.isqrt(grade ** lean) + 1 for grade in range(1, amount + 1)]
    largest = bound if full else min(bound, max(-(-total // amount), total * portions[0] // sum(portions)))
    least = 1 if total - largest >= amount - 1 else 0
    given, spare = [largest] + [least] * (amount - 1), total - largest - least * (amount - 1)
    while spare > 0:
        free = [i for i in range(1, amount) if given[i] < largest] or [i for i in range(1, amount) if given[i] < bound]
        whole, remaining = sum([portions[i] for i in free]), spare
        for i in free:
            more = min(bound - given[i], max(1, remaining * portions[i] // whole), spare)
            given[i] = given[i] + more
            spare = spare - more
    return np.array(given)


def scatter_about(rng, shape, scale, reach, cuts=(), kind=jnp.bfloat16):
    array = jax.random.normal(rng, shape, jnp.float32) * scale
    if len(cuts) > 0:
        array = block_levels(rng, shape, cuts, -0.22, 0.18) * array
    return jnp.clip(array, min=-reach, max=reach).astype(kind)


def setup_inputs(seed: int = 0) -> dict:
    key_of = jax.random.split(jax.random.key(seed), 17)
    tokens = scatter_about(key_of[0], (TOKENS, D), 1.0, 6.0, ((0, 128),))
    positions = draw_positions(jax.random.fold_in(key_of[16], 71), 0)
    norm_in = jnp.clip(1.0 + 0.1 * jax.random.normal(key_of[2], (D,), jnp.float32), 0.5, 1.5)
    query_weight = scatter_about(key_of[3], (D, QH * HD), D ** -0.5, 0.125, ((0, 64), (1, 2)))
    key_weight = scatter_about(key_of[4], (D, KVH * HD), D ** -0.5, 0.125, ((0, 64), (1, 2)))
    value_weight = scatter_about(key_of[5], (D, KVH * HD), D ** -0.5, 0.125, ((0, 64), (1, 2)))
    query_gain = jnp.clip(1.0 + 0.1 * jax.random.normal(key_of[6], (HD,), jnp.float32), 0.5, 1.5)
    key_gain = jnp.clip(1.0 + 0.1 * jax.random.normal(key_of[7], (HD,), jnp.float32), 0.5, 1.5)
    out_weight = scatter_about(key_of[8], (QH * HD, D), (QH * HD // 32) ** -0.5, 0.5, ((0, 2), (1, 64)))
    norm_mid = jnp.clip(1.0 + 0.1 * jax.random.normal(key_of[9], (D,), jnp.float32), 0.5, 1.5)
    routed_experts_keys = jax.random.split(jax.random.fold_in(key_of[10], 1), TOKENS // TOK_DEV)
    routed_experts_turns = jax.random.permutation(jax.random.fold_in(key_of[10], 3), TOKENS // TOK_DEV)
    routed_experts = jax.vmap(lambda own, number: deal_out(jax.random.fold_in(key_of[10], 2), own, number, TOK_DEV, EXPERTS, TOP, CAP, 2))(routed_experts_keys, routed_experts_turns).reshape((TOKENS, TOP))
    route_weight = jnp.clip(jnp.exp(math.log(0.5) - 2.3025851 * jax.random.uniform(key_of[11], (TOKENS, TOP), jnp.float32) ** block_levels(key_of[11], (TOKENS, TOP), ((0, 128),), -0.2, 0.2)), 0.05, 0.5)
    gate_weight = scatter_about(key_of[12], (EXPERTS, D, FF), D ** -0.5, 0.125, ((0, 64), (2, 2)))
    up_weight = scatter_about(key_of[13], (EXPERTS, D, FF), D ** -0.5, 0.125, ((0, 64), (2, 2)))
    down_weight = scatter_about(key_of[14], (EXPERTS, FF, D), (FF // 8) ** -0.5, 0.625, ((0, 64), (1, 2)))
    out_grad = scatter_about(key_of[15], (TOKENS, D), 1.0, 6.0, ((0, 128),))
    return dict(tokens=tokens, positions=positions, norm_in=norm_in, query_weight=query_weight, key_weight=key_weight, value_weight=value_weight, query_gain=query_gain, key_gain=key_gain, out_weight=out_weight, norm_mid=norm_mid, routed_experts=routed_experts, route_weight=route_weight, gate_weight=gate_weight, up_weight=up_weight, down_weight=down_weight, out_grad=out_grad)


@jax.custom_vjp
def low(v):
    return lax.optimization_barrier(v.astype(jnp.bfloat16)).astype(jnp.float32)

@jax.custom_vjp
def low_back(v):
    return v

def low_keep(v):
    return (low(v), None)

def low_pass(kept, grad):
    return (grad,)

def back_keep(v):
    return (v, None)

def back_low(kept, grad):
    return (low(grad),)
low.defvjp(low_keep, low_pass)
low_back.defvjp(back_keep, back_low)
EPS = 1e-06
THETA = 1000000.0

def matmul(left, right):
    return jnp.dot(left, right, precision=lax.Precision.HIGHEST, preferred_element_type=jnp.float32)

def rms_norm(values, gain):
    return values * lax.rsqrt(lax.optimization_barrier(jnp.mean(values * values, axis=-1, keepdims=True)) + EPS) * gain

def rope_tables(positions):
    half = HD // 2
    freqs = jnp.exp(jnp.arange(half, dtype=jnp.float32) * (-2.0 * math.log(THETA) / HD))
    angles = positions.astype(jnp.float32)[:, None] * freqs[None, :]
    return (jnp.cos(angles)[:, None, :], jnp.sin(angles)[:, None, :])

def rotate(values, cosine, sine):
    half = values.shape[-1] // 2
    first = values[..., :half]
    second = values[..., half:]
    return jnp.concatenate([first * cosine - second * sine, second * cosine + first * sine], axis=-1)

def attend_blocks(blocks):
    query, key, value = blocks
    repeat = QH // KVH
    key_all = jnp.repeat(key, repeat, axis=2)
    value_all = jnp.repeat(value, repeat, axis=2)
    scores = jnp.einsum('gahd,gbhd->ghab', query, key_all, precision=lax.Precision.HIGHEST) * HD ** (-0.5)
    scores = low_back(scores)
    causal = jnp.arange(SEQ)[:, None] >= jnp.arange(SEQ)[None, :]
    scores = jnp.where(causal, scores, -1e+30)
    probs = low(jax.nn.softmax(scores, axis=-1))
    mixed = jnp.einsum('ghab,gbhd->gahd', probs, value_all, precision=lax.Precision.HIGHEST)
    return low_back(low(mixed))

def reference(tokens, positions, norm_in, query_weight, key_weight, value_weight, query_gain, key_gain, out_weight, norm_mid, routed_experts, route_weight, gate_weight, up_weight, down_weight, out_grad):
    cosine, sine = rope_tables(positions)
    flat_experts = routed_experts.reshape(-1).astype(jnp.int32)
    order = jnp.argsort(flat_experts, stable=True).astype(jnp.int32)
    counts = lax.optimization_barrier(jnp.sum((flat_experts[:, None] == jnp.arange(EXPERTS, dtype=jnp.int32)[None, :]).astype(jnp.int32), axis=0))
    starts = (jnp.cumsum(counts) - counts).astype(jnp.int32)
    most_rows = CAP * (TOKENS // TOK_DEV)
    slots = jnp.arange(most_rows, dtype=jnp.int32)
    group = math.gcd(TOKENS // SEQ, max(1, 4096 // SEQ))
    blocks = TOKENS // (SEQ * group)

    def forward(tokens_f, norm_in_f, query_f, key_f, value_f, query_gain_f, key_gain_f, out_f, norm_mid_f, route_f, gate_f, up_f, down_f):
        normed = low(rms_norm(tokens_f, norm_in_f))
        query_raw = low_back(matmul(normed, query_f)).reshape(TOKENS, QH, HD)
        key_raw = low_back(matmul(normed, key_f)).reshape(TOKENS, KVH, HD)
        value = low_back(low(matmul(normed, value_f))).reshape(TOKENS, KVH, HD)
        query = low(rotate(rms_norm(query_raw, query_gain_f), cosine, sine))
        key = low(rotate(rms_norm(key_raw, key_gain_f), cosine, sine))
        mixed = lax.map(jax.checkpoint(attend_blocks), (query.reshape(blocks, group, SEQ, QH, HD), key.reshape(blocks, group, SEQ, KVH, HD), value.reshape(blocks, group, SEQ, KVH, HD)))
        mixed = mixed.reshape(TOKENS, QH * HD)
        attended = low_back(matmul(mixed, out_f))
        hidden_in = tokens_f + attended
        normed_mid = low(rms_norm(hidden_in, norm_mid_f))
        weights_flat = route_f.reshape(-1)

        def expert_step(total, inputs):
            gate_w, up_w, down_w, index = inputs
            position = starts[index] + slots
            valid = slots < counts[index]
            route = order[jnp.minimum(position, TOKENS * TOP - 1)]
            token = route // TOP
            keep = valid.astype(jnp.float32)
            rows_in = low_back(normed_mid[token]) * keep[:, None]
            gate = low_back(matmul(rows_in, gate_w))
            up = low_back(matmul(rows_in, up_w))
            hidden = low(jax.nn.silu(gate) * up)
            result = low_back(low(matmul(hidden, down_w)))
            weight = weights_flat[route] * keep
            return (total.at[token].add(result * weight[:, None]), None)
        start_total = jnp.zeros((TOKENS, D), jnp.float32)
        moe, unused = lax.scan(jax.checkpoint(expert_step), start_total, (gate_f, up_f, down_f, jnp.arange(EXPERTS, dtype=jnp.int32)))
        return hidden_in + moe
    primals = (tokens.astype(jnp.float32), norm_in.astype(jnp.float32), query_weight.astype(jnp.float32), key_weight.astype(jnp.float32), value_weight.astype(jnp.float32), query_gain.astype(jnp.float32), key_gain.astype(jnp.float32), out_weight.astype(jnp.float32), norm_mid.astype(jnp.float32), route_weight.astype(jnp.float32), gate_weight.astype(jnp.float32), up_weight.astype(jnp.float32), down_weight.astype(jnp.float32))
    output, pullback = jax.vjp(forward, *primals)
    grads = pullback(out_grad.astype(jnp.float32))
    return (output.astype(jnp.bfloat16), grads[0].astype(jnp.bfloat16), grads[1], grads[2], grads[3], grads[4], grads[5], grads[6], grads[7], grads[8], grads[9], grads[10], grads[11], grads[12])
```

```python
import math

import jax
import jax.numpy as jnp
from jax import lax
from jax.sharding import PartitionSpec as P

HD = 128
TOP = 8
EPS = 1e-06
THETA = 1000000.0
BF16 = jnp.bfloat16
F32 = jnp.float32


def dot(left, right, contract):
    return lax.dot_general(left, right, (contract, ((), ())), preferred_element_type=F32)


def rms_scale(values):
    return lax.rsqrt(jnp.mean(values * values, axis=-1, keepdims=True) + EPS)


def norm_back(values, scale, gain, grad):
    scaled = gain * grad
    inner = jnp.mean(scaled * values, axis=-1, keepdims=True)
    d_values = scale * scaled - values * (scale * scale * scale) * inner
    axes = tuple(range(grad.ndim - 1))
    return (d_values, jnp.sum(grad * values * scale, axis=axes))


def rope_tables(positions, head_size):
    half = head_size // 2
    freqs = jnp.exp(jnp.arange(half, dtype=F32) * (-2.0 * math.log(THETA) / head_size))
    angles = positions.astype(F32)[:, None] * freqs[None, :]
    return (jnp.cos(angles)[:, None, :], jnp.sin(angles)[:, None, :])


def rotate(values, cosine, sine):
    half = values.shape[-1] // 2
    first = values[..., :half]
    second = values[..., half:]
    return jnp.concatenate(
        [first * cosine - second * sine, second * cosine + first * sine], axis=-1
    )


def rotate_back(grad, cosine, sine):
    half = grad.shape[-1] // 2
    first = grad[..., :half]
    second = grad[..., half:]
    return jnp.concatenate(
        [first * cosine + second * sine, second * cosine - first * sine], axis=-1
    )


def swap(values):
    return lax.ppermute(values, "tensor", [(0, 1), (1, 0)])


def share_sequence(values):
    other = swap(values)
    first = lax.axis_index("tensor") == 0
    return jnp.concatenate(
        [jnp.where(first, values, other), jnp.where(first, other, values)], axis=0
    )


def sum_sequence(total, rows):
    mine = lax.axis_index("tensor") * rows
    own = lax.dynamic_slice_in_dim(total, mine, rows, 0)
    sent = lax.dynamic_slice_in_dim(total, rows - mine, rows, 0).astype(BF16)
    return own + swap(sent).astype(F32)


def exchange(buffer):
    return lax.all_to_all(buffer, "dp", split_axis=0, concat_axis=0, tiled=True)


def per_device(
    tokens,
    positions,
    norm_in,
    query_weight,
    key_weight,
    value_weight,
    query_gain,
    key_gain,
    out_weight,
    norm_mid,
    routed_experts,
    route_weight,
    gate_weight,
    up_weight,
    down_weight,
    out_grad,
):
    rows, width = tokens.shape
    owners = lax.axis_size("dp")
    experts = owners
    capacity = 5 * rows * TOP // (4 * experts)
    slots = experts * capacity
    scale = HD ** (-0.5)

    shard = jnp.concatenate([query_weight, key_weight, value_weight, out_weight.T], axis=1)
    full = lax.all_gather(shard, "dp", axis=0, tiled=True)
    q_cols, k_cols = query_weight.shape[1], key_weight.shape[1]
    in_cols = q_cols + 2 * k_cols
    in_full, out_full = full[:, :in_cols], full[:, in_cols:]
    query_heads, key_heads = q_cols // HD, k_cols // HD
    group = query_heads // key_heads

    gate_w, up_w, down_w = gate_weight[0], up_weight[0], down_weight[0]
    down_o, gate_o, up_o = swap(down_w), swap(gate_w), swap(up_w)

    names = routed_experts[:, :, None] == jnp.arange(experts, dtype=jnp.int32)
    chosen = jnp.any(names, axis=1)
    weight_of = jnp.sum(jnp.where(names, route_weight[:, :, None], 0.0), axis=1)
    below = jnp.arange(rows)[:, None] > jnp.arange(rows)[None, :]
    rank = dot(below.astype(BF16), chosen.astype(BF16), ((1,), (0,))).astype(jnp.int32)
    rank = jnp.where(chosen, rank, -1)
    place_b = rank.T[:, None, :] == jnp.arange(capacity, dtype=jnp.int32)[None, :, None]
    place = place_b.reshape(slots, rows).astype(BF16)
    slot_weight = jnp.sum(jnp.where(place_b, weight_of.T[:, None, :], 0.0), axis=2).reshape(slots)

    grad = out_grad.astype(F32)
    d_rows = (dot(place, out_grad, ((1,), (0,))) * slot_weight[:, None]).astype(BF16)
    expert_grads = exchange(d_rows.reshape(experts, capacity, width)).reshape(slots, width)

    inputs = tokens.astype(F32)
    in_scale = rms_scale(inputs)
    normed = (inputs * in_scale * norm_in).astype(BF16)
    whole = share_sequence(normed)
    length = whole.shape[0]
    cosine, sine = rope_tables(positions, HD)
    raw = dot(whole, in_full, ((1,), (0,)))
    query_raw = raw[:, :q_cols].reshape(length, query_heads, HD)
    key_raw = raw[:, q_cols : q_cols + k_cols].reshape(length, key_heads, HD)
    value_low = raw[:, q_cols + k_cols :].astype(BF16).reshape(length, key_heads, HD)
    query_scale = rms_scale(query_raw)
    query = (
        rotate(query_raw * query_scale * query_gain, cosine, sine)
        .astype(BF16)
        .reshape(length, key_heads, group, HD)
    )
    key_scale = rms_scale(key_raw)
    key = rotate(key_raw * key_scale * key_gain, cosine, sine).astype(BF16)
    causal = jnp.arange(length)[:, None] >= jnp.arange(length)[None, :]
    scores = jnp.einsum("ahgd,bhd->hgab", query, key, preferred_element_type=F32) * scale
    scores = jnp.where(causal, scores, -1e30)
    peak = jnp.max(scores, axis=-1, keepdims=True)
    log_total = peak + jnp.log(jnp.sum(jnp.exp(scores - peak), axis=-1, keepdims=True))
    probs_low = jnp.exp(scores - log_total).astype(BF16)
    mixed = (
        jnp.einsum("hgab,bhd->ahgd", probs_low, value_low, preferred_element_type=F32)
        .astype(BF16)
        .reshape(length, q_cols)
    )
    attended = sum_sequence(dot(mixed, out_full, ((1,), (1,))), rows)
    hidden_in = inputs + attended
    mid_scale = rms_scale(hidden_in)
    normed_mid = (hidden_in * mid_scale * norm_mid).astype(BF16)

    send_rows = dot(place, normed_mid, ((1,), (0,))).astype(BF16)
    rows_in = exchange(send_rows.reshape(experts, capacity, width)).reshape(slots, width)

    def expert_half(gate_h, up_h, down_h):
        gate = dot(rows_in, gate_h, ((1,), (0,)))
        up = dot(rows_in, up_h, ((1,), (0,)))
        d_hidden = dot(expert_grads, down_h, ((1,), (1,)))
        sigma = jax.nn.sigmoid(gate)
        activated = gate * sigma
        hidden = (activated * up).astype(BF16)
        d_gate = (d_hidden * up * (sigma * (1.0 + gate * (1.0 - sigma)))).astype(BF16)
        d_up = (d_hidden * activated).astype(BF16)
        result = dot(hidden, down_h, ((1,), (0,)))
        d_row = dot(d_gate, gate_h, ((1,), (1,))) + dot(d_up, up_h, ((1,), (1,)))
        return hidden, d_gate, d_up, result, d_row

    hid_m, dg_m, du_m, res_m, dr_m = expert_half(gate_w, up_w, down_w)
    hid_o, dg_o, du_o, res_o, dr_o = expert_half(gate_o, up_o, down_o)
    d_row = (dr_m + dr_o).astype(BF16)
    result = (res_m + res_o).astype(BF16)
    back_rows = exchange(d_row.reshape(experts, capacity, width)).reshape(slots, width)
    returned = exchange(result.reshape(experts, capacity, width)).reshape(slots, width)

    def expert_grad(left_o, right_o, left_m, right_m):
        sent = dot(left_o, right_o, ((0,), (0,))).astype(BF16)
        return (dot(left_m, right_m, ((0,), (0,))) + swap(sent).astype(F32))[None]

    grad_down = expert_grad(hid_o, expert_grads, hid_m, expert_grads)
    grad_gate = expert_grad(rows_in, dg_o, rows_in, dg_m)
    grad_up = expert_grad(rows_in, du_o, rows_in, du_m)

    combine = jnp.where(place_b, weight_of.T[:, None, :], 0.0).reshape(slots, rows)
    combine_high = combine.astype(BF16)
    combine_low = (combine - combine_high.astype(F32)).astype(BF16)
    moe = dot(combine_high, returned, ((0,), (0,))) + dot(combine_low, returned, ((0,), (0,)))
    output = (hidden_in + moe).astype(BF16)
    products = dot(returned, out_grad, ((1,), (1,)))
    of_expert = jnp.sum(
        jnp.where(place_b, products.reshape(experts, capacity, rows), 0.0), axis=1
    ).T
    grad_route = jnp.sum(jnp.where(names, of_expert[:, None, :], 0.0), axis=2)

    d_mid = dot(place, back_rows, ((0,), (0,)))
    d_mid_in, grad_norm_mid = norm_back(hidden_in, mid_scale, norm_mid, d_mid)
    d_hidden_in = grad + d_mid_in
    d_attended = d_hidden_in.astype(BF16)
    d_whole = share_sequence(d_attended)
    d_mixed = (
        dot(d_whole, out_full, ((1,), (0,))).astype(BF16).reshape(length, key_heads, group, HD)
    )
    probs = jnp.exp(scores - log_total)
    d_probs = jnp.einsum("ahgd,bhd->hgab", d_mixed, value_low, preferred_element_type=F32)
    value_grad = jnp.einsum("hgab,ahgd->bhd", probs_low, d_mixed, preferred_element_type=F32)
    delta = jnp.sum(probs * d_probs, axis=-1, keepdims=True)
    d_scores = (probs * (d_probs - delta)).astype(BF16)
    d_query = (
        jnp.einsum("hgab,bhd->ahgd", d_scores, key, preferred_element_type=F32).reshape(
            length, query_heads, HD
        )
        * scale
    )
    d_key = jnp.einsum("hgab,ahgd->bhd", d_scores, query, preferred_element_type=F32) * scale
    d_query_raw, grad_query_gain = norm_back(
        query_raw, query_scale, query_gain, rotate_back(d_query, cosine, sine)
    )
    d_key_raw, grad_key_gain = norm_back(
        key_raw, key_scale, key_gain, rotate_back(d_key, cosine, sine)
    )
    d_raw = jnp.concatenate(
        [
            d_query_raw.astype(BF16).reshape(length, q_cols),
            d_key_raw.astype(BF16).reshape(length, k_cols),
            value_grad.astype(BF16).reshape(length, k_cols),
        ],
        axis=1,
    )
    d_normed = sum_sequence(dot(d_raw, in_full, ((1,), (1,))), rows)
    d_inputs, grad_norm_in = norm_back(inputs, in_scale, norm_in, d_normed)
    grad_tokens = (d_hidden_in + d_inputs).astype(BF16)

    gains = jnp.concatenate([grad_norm_in, grad_norm_mid, grad_query_gain, grad_key_gain])
    gains = lax.psum(gains, ("dp", "tensor"))
    grad_norm_in, grad_norm_mid = gains[:width], gains[width : 2 * width]
    grad_query_gain, grad_key_gain = gains[2 * width : 2 * width + HD], gains[2 * width + HD :]

    in_grads = dot(whole, d_raw, ((0,), (0,))).astype(BF16)
    out_grads = dot(d_whole, mixed, ((0,), (0,))).astype(BF16)
    partial = jnp.concatenate([in_grads, out_grads], axis=1)
    parts = exchange(partial.reshape(owners, -1, partial.shape[1]))
    total = jnp.sum(parts.astype(F32), axis=0)
    return (
        output,
        grad_tokens,
        grad_norm_in,
        total[:, :q_cols],
        total[:, q_cols : q_cols + k_cols],
        total[:, q_cols + k_cols : in_cols],
        grad_query_gain,
        grad_key_gain,
        total[:, in_cols:].T,
        grad_norm_mid,
        grad_route,
        grad_gate,
        grad_up,
        grad_down,
    )


def solution(mesh):
    tokens_spec = P(("dp", "tensor"), None)
    columns, rows = P("dp", None, "tensor"), P("dp", "tensor", None)
    proj = P("dp", "tensor")
    return jax.shard_map(
        per_device,
        mesh=mesh,
        in_specs=(
            tokens_spec,
            P("dp"),
            P(),
            proj,
            proj,
            proj,
            P(),
            P(),
            P("tensor", "dp"),
            P(),
            tokens_spec,
            tokens_spec,
            columns,
            columns,
            rows,
            tokens_spec,
        ),
        out_specs=(
            tokens_spec,
            tokens_spec,
            P(),
            proj,
            proj,
            proj,
            P(),
            P(),
            P("tensor", "dp"),
            P(),
            tokens_spec,
            columns,
            columns,
            rows,
        ),
        check_vma=False,
    )
```

```python
import math

import jax
import jax.numpy as jnp
from jax import lax
from jax.experimental import pallas as pl
from jax.experimental.pallas import tpu as pltpu
from jax.sharding import PartitionSpec as P

HD = 128
TOP = 8
EPS = 1e-06
THETA = 1000000.0
BF16 = jnp.bfloat16
F32 = jnp.float32
MESH_ID = pl.DeviceIdType.MESH
ANY_SPEC = pl.BlockSpec(memory_space=pl.ANY)
VMEM_SPEC = pl.BlockSpec(memory_space=pltpu.VMEM)


def coordinates():
    dp = lax.axis_index("dp")
    return lax.div(dp, 16), lax.rem(lax.div(dp, 8), 2), lax.rem(lax.div(dp, 2), 4), lax.rem(dp, 2)


def device(z, x, y, core, tensor):
    return (((z * 2 + x) * 4 + y) * 2 + core, tensor)


def turn(at, step):
    return lax.rem(at + step, 4)


def send(src, dst, send_sem, recv_sem, to):
    copy = pltpu.make_async_remote_copy(
        src_ref=src,
        dst_ref=dst,
        send_sem=send_sem,
        recv_sem=recv_sem,
        device_id=to,
        device_id_type=MESH_ID,
    )
    copy.start()
    return copy


def greet(peers):
    barrier = pltpu.get_barrier_semaphore()
    for peer in peers:
        pl.semaphore_signal(barrier, inc=1, device_id=peer, device_id_type=MESH_ID)
    pl.semaphore_wait(barrier, len(peers))


STEPS = (1, 3, 2)


def reduce_kernel(
    ga, gb, gain, d_own, d_sent, x_hat, down, gate, up,
    oa, ob, og, d_came, down_c, gate_c, up_c,
    own_a, got_a, one_a, two_a, sum_a, three_a,
    own_b, got_b, one_b, two_b, sum_b, three_b,
    vec, vecs,
    load_sem, core_send, core_recv, one_send, one_recv, two_send, two_recv,
    three_send, three_recv, vec_send, vec_recv, pair_send, pair_recv,
):
    z, x, y, core = coordinates()
    tensor = lax.axis_index("tensor")
    sibling = device(z, x, y, 1 - core, tensor)
    along_z = [device(turn(z, s), x, y, core, tensor) for s in STEPS]
    along_y = [device(z, x, turn(y, s), core, tensor) for s in STEPS]
    across = device(z, 1 - x, y, core, tensor)
    near = [
        device(z, x, y, 1 - core, tensor),
        device(z, x, y, core, 1 - tensor),
        device(z, x, y, 1 - core, 1 - tensor),
    ]
    greet(along_z + along_y + [across] + near)

    vec_groups = (
        (near, core * 2 + tensor, 4),
        (along_z, z, 4),
        (along_y, y, 4),
        ([across], x, 2),
    )
    vec_copies = {}

    def vec_start(stage):
        peers, mine, _ = vec_groups[stage]
        if stage == 0:
            vec[0] = gain[...]
            vec[0, 0:1] = jnp.sum(
                (d_own[...] + d_came[...].astype(F32)) * x_hat[...], axis=0, keepdims=True
            )
        vecs[stage, mine] = vec[stage]
        vec_copies[stage] = [
            send(vec.at[stage], vecs.at[stage, mine], vec_send.at[stage, i], vec_recv.at[stage, i], peer)
            for i, peer in enumerate(peers)
        ]

    def vec_finish(stage):
        for copy in vec_copies[stage]:
            copy.wait()
        count = vec_groups[stage][2]
        total = vecs[stage, 0]
        for i in range(1, count):
            total = total + vecs[stage, i]
        if stage == 3:
            og[...] = total
        else:
            vec[stage + 1] = total

    partner = near[1]
    d_copy = send(d_sent, d_came, pair_send.at[0], pair_recv.at[0], partner)

    loads, swaps = {}, {}
    order = STEPS + (0,)
    for i, s in enumerate(order):
        to = turn(z, s)
        swaps["a", s] = send(ga.at[to, :, :, 1 - core], got_a.at[to], core_send.at[0, i], core_recv.at[0, i], sibling)
        loads["a", s] = pltpu.make_async_copy(ga.at[to, :, :, core], own_a.at[to], load_sem.at[0, i])
        loads["a", s].start()
        to = turn(y, s)
        swaps["b", s] = send(gb.at[:, :, to, 1 - core], got_b.at[to], core_send.at[1, i], core_recv.at[1, i], sibling)
        loads["b", s] = pltpu.make_async_copy(gb.at[:, :, to, core], own_b.at[to], load_sem.at[1, i])
        loads["b", s].start()

    def add_cores(own, got, to):
        shape = own.shape

        @pl.loop(0, shape[1])
        def _(i):
            @pl.loop(0, shape[2])
            def _(j):
                own[to, i, j] = (own[to, i, j].astype(F32) + got[to, i, j].astype(F32)).astype(BF16)

    d_copy.wait_recv()
    vec_start(0)
    expert = [
        send(down, down_c, pair_send.at[1], pair_recv.at[1], partner),
        send(gate, gate_c, pair_send.at[2], pair_recv.at[2], partner),
    ]

    ones = []
    for i, s in enumerate(order):
        loads["a", s].wait()
        swaps["a", s].wait_recv()
        add_cores(own_a, got_a, turn(z, s))
        if s:
            ones.append(send(own_a.at[turn(z, s)], one_a.at[i], one_send.at[0, i], one_recv.at[0, i], along_z[i]))
        loads["b", s].wait()
        swaps["b", s].wait_recv()
        add_cores(own_b, got_b, turn(y, s))
        if s:
            ones.append(send(own_b.at[turn(y, s)], one_b.at[i], one_send.at[1, i], one_recv.at[1, i], along_y[i]))
    vec_finish(0)
    vec_start(1)

    for copy in ones:
        copy.wait_recv()
    vec_finish(1)
    vec_start(2)
    twos = []
    for i, s in enumerate(order):
        to = turn(y, s)
        for k in range(2):
            sum_a[to, k] = (
                own_a[z, k, to].astype(F32) + one_a[0, k, to].astype(F32)
                + one_a[1, k, to].astype(F32) + one_a[2, k, to].astype(F32)
            ).astype(BF16)
        if s:
            twos.append(send(sum_a.at[to], two_a.at[i], two_send.at[0, i], two_recv.at[0, i], along_y[i]))
        to = turn(z, s)
        for k in range(2):
            sum_b[to, k] = (
                own_b[y, to, k].astype(F32) + one_b[0, to, k].astype(F32)
                + one_b[1, to, k].astype(F32) + one_b[2, to, k].astype(F32)
            ).astype(BF16)
        if s:
            twos.append(send(sum_b.at[to], two_b.at[i], two_send.at[1, i], two_recv.at[1, i], along_z[i]))

    for copy in twos:
        copy.wait_recv()
    vec_finish(2)
    vec_start(3)

    def last(sums, two, at, k):
        return (
            sums[at, k].astype(F32) + two[0, k].astype(F32) + two[1, k].astype(F32) + two[2, k].astype(F32)
        )

    three_a[0] = last(sum_a, two_a, y, 1 - x).astype(BF16)
    final_a = send(three_a.at[0], three_a.at[1], three_send.at[0], three_recv.at[0], across)
    three_b[0] = last(sum_b, two_b, z, 1 - x).astype(BF16)
    final_b = send(three_b.at[0], three_b.at[1], three_send.at[1], three_recv.at[1], across)
    expert.append(send(up, up_c, pair_send.at[3], pair_recv.at[3], partner))
    mine_a = last(sum_a, two_a, y, x)
    final_a.wait_recv()
    oa[...] = mine_a + three_a[1].astype(F32)
    mine_b = last(sum_b, two_b, z, x)
    final_b.wait_recv()
    ob[...] = mine_b + three_b[1].astype(F32)
    vec_finish(3)
    for copy in expert:
        copy.wait_recv()
    for copy in list(swaps.values()) + ones + twos + [final_a, final_b, d_copy] + expert:
        copy.wait_send()


def reduce_grads(in_grads, out_grads, gains, d_own, d_sent, x_hat, expert):
    owners = lax.axis_size("dp")
    rows = in_grads.shape[0] // owners
    a_cols, b_cols = in_grads.shape[1], out_grads.shape[1]
    dma = pltpu.SemaphoreType.DMA
    vmem = pltpu.VMEM

    def scratch(cols, inner):
        return [
            vmem((4,) + inner + (rows, cols), BF16),
            vmem((4,) + inner + (rows, cols), BF16),
            vmem((3,) + inner + (rows, cols), BF16),
            vmem((3, 2, rows, cols), BF16),
            vmem((4, 2, rows, cols), BF16),
            vmem((2, rows, cols), BF16),
        ]

    return pl.pallas_call(
        reduce_kernel,
        out_shape=(
            jax.ShapeDtypeStruct((rows, a_cols), F32),
            jax.ShapeDtypeStruct((rows, b_cols), F32),
            jax.ShapeDtypeStruct(gains.shape, F32),
            jax.ShapeDtypeStruct(d_sent.shape, BF16),
            *[jax.ShapeDtypeStruct(half.shape, BF16) for half in expert],
        ),
        in_specs=[ANY_SPEC] * 2 + [VMEM_SPEC] * 4 + [ANY_SPEC] * 3,
        out_specs=[VMEM_SPEC] * 4 + [ANY_SPEC] * 3,
        scratch_shapes=scratch(a_cols, (2, 4))
        + scratch(b_cols, (4, 2))
        + [
            vmem((4,) + gains.shape, F32),
            vmem((4, 4) + gains.shape, F32),
            dma((2, 4)),
            dma((2, 4)),
            dma((2, 4)),
            dma((2, 3)),
            dma((2, 3)),
            dma((2, 3)),
            dma((2, 3)),
            dma((2,)),
            dma((2,)),
            dma((4, 3)),
            dma((4, 3)),
            dma((4,)),
            dma((4,)),
        ],
        compiler_params=pltpu.CompilerParams(
            collective_id=1, has_side_effects=True, vmem_limit_bytes=56 * 1024 * 1024
        ),
        cost_estimate=pl.CostEstimate(flops=10_000_000, bytes_accessed=300_000_000, transcendentals=0),
    )(
        in_grads.reshape(4, 2, 4, 2, rows, a_cols),
        out_grads.reshape(4, 2, 4, 2, rows, b_cols),
        gains,
        d_own,
        d_sent,
        x_hat,
        *expert,
    )


def ring(view, at, up, down, sends, recvs, arrived):
    both = pl.ds(0, 2)

    def start(place, half, i, to):
        block = view(place, half)
        return send(block, block, sends.at[i], recvs.at[i], to)

    copies = [start(at, both, 0, up), start(at, both, 1, down)]
    yield copies
    copies[0].wait_recv()
    copies.append(start(turn(at, 3), 0, 2, up))
    arrived(turn(at, 3))
    yield
    copies[1].wait_recv()
    copies.append(start(turn(at, 1), 1, 3, down))
    arrived(turn(at, 1))
    yield
    copies[2].wait_recv()
    copies[3].wait_recv()
    arrived(turn(at, 2))
    yield


def together(*rings):
    copies = [next(r) for r in rings]
    for _ in range(3):
        for r in rings:
            next(r)
    return [c for group in copies for c in group]


def gather_kernel(
    sa, sb, part, down, gate, up, fa, fb, whole, down_o, gate_o, up_o,
    keep_sem, x_send, x_recv, one_send, one_recv, two_send, two_recv, core_send, core_recv, pair_send, pair_recv,
):
    z, x, y, core = coordinates()
    tensor = lax.axis_index("tensor")
    sibling = device(z, x, y, 1 - core, tensor)
    across = device(z, 1 - x, y, core, tensor)
    partner = device(z, x, y, core, 1 - tensor)
    around_z = device(turn(z, 1), x, y, core, tensor), device(turn(z, 3), x, y, core, tensor)
    around_y = device(z, x, turn(y, 1), core, tensor), device(z, x, turn(y, 3), core, tensor)
    greet([sibling, across, partner, *around_z, *around_y])

    pair = send(part, whole.at[tensor], pair_send.at[0], pair_recv.at[0], partner)
    a_own, b_own = fa.at[z, x, y, core], fb.at[z, x, y, core]
    over = [
        send(sa, a_own, x_send.at[0], x_recv.at[0], across),
        send(sb, b_own, x_send.at[1], x_recv.at[1], across),
    ]
    expert = [
        send(src, dst, pair_send.at[i], pair_recv.at[i], partner)
        for i, (src, dst) in enumerate(((down, down_o), (gate, gate_o), (up, up_o)), 1)
    ]
    keep = [
        pltpu.make_async_copy(part, whole.at[tensor], keep_sem.at[0]),
        pltpu.make_async_copy(sa, a_own, keep_sem.at[1]),
        pltpu.make_async_copy(sb, b_own, keep_sem.at[2]),
    ]
    for copy in keep:
        copy.start()
    keep[1].wait()
    keep[2].wait()
    over[0].wait_recv()
    over[1].wait_recv()

    def skip(place):
        return None

    small = together(
        ring(lambda i, h: fa.at[z, h, i, core], y, *around_y, one_send.at[0], one_recv.at[0], skip),
        ring(lambda i, h: fb.at[i, h, y, core], z, *around_z, one_send.at[1], one_recv.at[1], skip),
    )
    cores = []

    def hand_on(view):
        def arrived(place):
            block, k = view(place, pl.ds(0, 2)), len(cores)
            cores.append(send(block, block, core_send.at[k], core_recv.at[k], sibling))

        return arrived

    def view_a(i, h):
        return fa.at[i, h, :, core]

    def view_b(i, h):
        return fb.at[:, h, i, core]

    large = [
        ring(view_a, z, *around_z, two_send.at[0], two_recv.at[0], hand_on(view_a)),
        ring(view_b, y, *around_y, two_send.at[1], two_recv.at[1], hand_on(view_b)),
    ]
    copies = [next(r) for r in large]
    hand_on(view_a)(z)
    hand_on(view_b)(y)
    for _ in range(3):
        for r in large:
            next(r)
    keep[0].wait()
    pair.wait_recv()
    for copy in cores + expert:
        copy.wait_recv()
    for copy in expert + [pair] + over + small + copies[0] + copies[1] + cores:
        copy.wait_send()


def gather_weights(in_shard, out_shard, part, expert):
    owners = lax.axis_size("dp")
    (rows, a_cols), b_cols = in_shard.shape, out_shard.shape[1]
    dma = pltpu.SemaphoreType.DMA
    in_full, out_full, whole, *other = pl.pallas_call(
        gather_kernel,
        out_shape=(
            jax.ShapeDtypeStruct((4, 2, 4, 2, rows, a_cols), BF16),
            jax.ShapeDtypeStruct((4, 2, 4, 2, rows, b_cols), BF16),
            jax.ShapeDtypeStruct((2,) + part.shape, BF16),
            *[jax.ShapeDtypeStruct(w.shape, BF16) for w in expert],
        ),
        in_specs=[ANY_SPEC] * 6,
        out_specs=[ANY_SPEC] * 6,
        scratch_shapes=[
            dma((3,)),
            dma((2,)),
            dma((2,)),
            dma((2, 4)),
            dma((2, 4)),
            dma((2, 4)),
            dma((2, 4)),
            dma((8,)),
            dma((8,)),
            dma((4,)),
            dma((4,)),
        ],
        compiler_params=pltpu.CompilerParams(collective_id=2, has_side_effects=True),
        cost_estimate=pl.CostEstimate(flops=0, bytes_accessed=250_000_000, transcendentals=0),
    )(in_shard, out_shard, part, *expert)
    return (
        in_full.reshape(owners * rows, a_cols),
        out_full.reshape(owners * rows, b_cols),
        whole.reshape(-1, part.shape[1]),
        other,
    )


def dot(left, right, contract):
    return lax.dot_general(left, right, (contract, ((), ())), preferred_element_type=F32)


def rms_scale(values):
    return lax.rsqrt(jnp.mean(values * values, axis=-1, keepdims=True) + EPS)


def norm_back(values, scale, gain, grad):
    scaled = gain * grad
    inner = jnp.mean(scaled * values, axis=-1, keepdims=True)
    d_values = scale * scaled - values * (scale * scale * scale) * inner
    axes = tuple(range(grad.ndim - 1))
    return (d_values, jnp.sum(grad * values * scale, axis=axes))


def rope_tables(positions, head_size):
    half = head_size // 2
    freqs = jnp.exp(jnp.arange(half, dtype=F32) * (-2.0 * math.log(THETA) / head_size))
    angles = positions.astype(F32)[:, None] * freqs[None, :]
    return (jnp.cos(angles)[:, None, :], jnp.sin(angles)[:, None, :])


def rotate(values, cosine, sine):
    half = values.shape[-1] // 2
    first = values[..., :half]
    second = values[..., half:]
    return jnp.concatenate(
        [first * cosine - second * sine, second * cosine + first * sine], axis=-1
    )


def rotate_back(grad, cosine, sine):
    half = grad.shape[-1] // 2
    first = grad[..., :half]
    second = grad[..., half:]
    return jnp.concatenate(
        [first * cosine + second * sine, second * cosine - first * sine], axis=-1
    )


def swap(values):
    return lax.ppermute(values, "tensor", [(0, 1), (1, 0)])


def share_sequence(values):
    other = swap(values)
    first = lax.axis_index("tensor") == 0
    return jnp.concatenate(
        [jnp.where(first, values, other), jnp.where(first, other, values)], axis=0
    )


def halves_of(total, rows):
    mine = lax.axis_index("tensor") * rows
    return (
        lax.dynamic_slice_in_dim(total, mine, rows, 0),
        lax.dynamic_slice_in_dim(total, rows - mine, rows, 0),
    )


def sum_sequence(total, rows):
    own, sent = halves_of(total, rows)
    return own + swap(sent.astype(BF16)).astype(F32)


def exchange(buffer):
    return lax.all_to_all(buffer, "dp", split_axis=0, concat_axis=0, tiled=True)


def per_device(
    tokens,
    positions,
    norm_in,
    query_weight,
    key_weight,
    value_weight,
    query_gain,
    key_gain,
    out_weight,
    norm_mid,
    routed_experts,
    route_weight,
    gate_weight,
    up_weight,
    down_weight,
    out_grad,
):
    rows, width = tokens.shape
    owners = lax.axis_size("dp")
    experts = owners
    capacity = 5 * rows * TOP // (4 * experts)
    slots = experts * capacity
    scale = HD ** (-0.5)

    inputs = tokens.astype(F32)
    in_scale = rms_scale(inputs)
    normed = (inputs * in_scale * norm_in).astype(BF16)
    gate_w, up_w, down_w = gate_weight[0], up_weight[0], down_weight[0]
    in_full, out_full, whole, (down_o, gate_o, up_o) = gather_weights(
        jnp.concatenate([query_weight, key_weight, value_weight], axis=1),
        out_weight.T,
        normed,
        (down_w, gate_w, up_w),
    )
    q_cols, k_cols = query_weight.shape[1], key_weight.shape[1]
    query_heads, key_heads = q_cols // HD, k_cols // HD
    group = query_heads // key_heads

    names = routed_experts[:, :, None] == jnp.arange(experts, dtype=jnp.int32)
    chosen = jnp.any(names, axis=1)
    weight_of = jnp.sum(jnp.where(names, route_weight[:, :, None], 0.0), axis=1)
    below = jnp.arange(rows)[:, None] > jnp.arange(rows)[None, :]
    rank = dot(below.astype(BF16), chosen.astype(BF16), ((1,), (0,))).astype(jnp.int32)
    rank = jnp.where(chosen, rank, -1)
    place_b = rank.T[:, None, :] == jnp.arange(capacity, dtype=jnp.int32)[None, :, None]
    place = place_b.reshape(slots, rows).astype(BF16)
    slot_weight = jnp.sum(jnp.where(place_b, weight_of.T[:, None, :], 0.0), axis=2).reshape(slots)

    grad = out_grad.astype(F32)
    d_rows = (dot(place, out_grad, ((1,), (0,))) * slot_weight[:, None]).astype(BF16)
    d_rows, whole = lax.optimization_barrier((d_rows, whole))
    expert_grads = exchange(d_rows.reshape(experts, capacity, width)).reshape(slots, width)

    length = whole.shape[0]
    cosine, sine = rope_tables(positions, HD)
    raw = dot(whole, in_full, ((1,), (0,)))
    query_raw = raw[:, :q_cols].reshape(length, query_heads, HD)
    key_raw = raw[:, q_cols : q_cols + k_cols].reshape(length, key_heads, HD)
    value_low = raw[:, q_cols + k_cols :].astype(BF16).reshape(length, key_heads, HD)
    query_scale = rms_scale(query_raw)
    query = (
        rotate(query_raw * query_scale * query_gain, cosine, sine)
        .astype(BF16)
        .reshape(length, key_heads, group, HD)
    )
    key_scale = rms_scale(key_raw)
    key = rotate(key_raw * key_scale * key_gain, cosine, sine).astype(BF16)
    causal = jnp.arange(length)[:, None] >= jnp.arange(length)[None, :]
    scores = jnp.einsum("ahgd,bhd->hgab", query, key, preferred_element_type=F32) * scale
    scores = jnp.where(causal, scores, -1e30)
    peak = jnp.max(scores, axis=-1, keepdims=True)
    log_total = peak + jnp.log(jnp.sum(jnp.exp(scores - peak), axis=-1, keepdims=True))
    probs_low = jnp.exp(scores - log_total).astype(BF16)
    mixed = (
        jnp.einsum("hgab,bhd->ahgd", probs_low, value_low, preferred_element_type=F32)
        .astype(BF16)
        .reshape(length, q_cols)
    )
    attended = sum_sequence(dot(mixed, out_full, ((1,), (1,))), rows)
    hidden_in = inputs + attended
    mid_scale = rms_scale(hidden_in)
    normed_mid = (hidden_in * mid_scale * norm_mid).astype(BF16)

    send_rows = dot(place, normed_mid, ((1,), (0,))).astype(BF16)
    send_rows, expert_grads = lax.optimization_barrier((send_rows, expert_grads))
    rows_in = exchange(send_rows.reshape(experts, capacity, width)).reshape(slots, width)

    def expert_half(gate_h, up_h, down_h):
        gate = dot(rows_in, gate_h, ((1,), (0,)))
        up = dot(rows_in, up_h, ((1,), (0,)))
        d_hidden = dot(expert_grads, down_h, ((1,), (1,)))
        sigma = jax.nn.sigmoid(gate)
        activated = gate * sigma
        hidden = (activated * up).astype(BF16)
        d_gate = (d_hidden * up * (sigma * (1.0 + gate * (1.0 - sigma)))).astype(BF16)
        d_up = (d_hidden * activated).astype(BF16)
        result = dot(hidden, down_h, ((1,), (0,)))
        d_row = dot(d_gate, gate_h, ((1,), (1,))) + dot(d_up, up_h, ((1,), (1,)))
        return hidden, d_gate, d_up, result, d_row

    hid_m, dg_m, du_m, res_m, dr_m = expert_half(gate_w, up_w, down_w)
    hid_o, dg_o, du_o, res_o, dr_o = expert_half(gate_o, up_o, down_o)
    d_row = (dr_m + dr_o).astype(BF16)
    result = (res_m + res_o).astype(BF16)
    back_rows = exchange(d_row.reshape(experts, capacity, width)).reshape(slots, width)
    halves = ((hid_m, expert_grads), (rows_in, dg_m), (rows_in, du_m))
    sent = [
        dot(left, right, ((0,), (0,))).astype(BF16)
        for left, right in ((hid_o, expert_grads), (rows_in, dg_o), (rows_in, du_o))
    ]

    d_mid = dot(place, back_rows, ((0,), (0,)))
    d_mid_in, grad_norm_mid = norm_back(hidden_in, mid_scale, norm_mid, d_mid)
    d_hidden_in = grad + d_mid_in
    d_attended = d_hidden_in.astype(BF16)
    d_whole = share_sequence(d_attended)
    d_whole, result = lax.optimization_barrier((d_whole, result))
    d_mixed = (
        dot(d_whole, out_full, ((1,), (0,))).astype(BF16).reshape(length, key_heads, group, HD)
    )
    probs = jnp.exp(scores - log_total)
    d_probs = jnp.einsum("ahgd,bhd->hgab", d_mixed, value_low, preferred_element_type=F32)
    value_grad = jnp.einsum("hgab,ahgd->bhd", probs_low, d_mixed, preferred_element_type=F32)
    delta = jnp.sum(probs * d_probs, axis=-1, keepdims=True)
    d_scores = (probs * (d_probs - delta)).astype(BF16)
    d_query = (
        jnp.einsum("hgab,bhd->ahgd", d_scores, key, preferred_element_type=F32).reshape(
            length, query_heads, HD
        )
        * scale
    )
    d_key = jnp.einsum("hgab,ahgd->bhd", d_scores, query, preferred_element_type=F32) * scale
    d_query_raw, grad_query_gain = norm_back(
        query_raw, query_scale, query_gain, rotate_back(d_query, cosine, sine)
    )
    d_key_raw, grad_key_gain = norm_back(
        key_raw, key_scale, key_gain, rotate_back(d_key, cosine, sine)
    )
    d_raw = jnp.concatenate(
        [
            d_query_raw.astype(BF16).reshape(length, q_cols),
            d_key_raw.astype(BF16).reshape(length, k_cols),
            value_grad.astype(BF16).reshape(length, k_cols),
        ],
        axis=1,
    )
    d_total = dot(d_raw, in_full, ((1,), (1,)))
    d_own, d_sent = halves_of(d_total, rows)

    returned = exchange(result.reshape(experts, capacity, width)).reshape(slots, width)
    combine = jnp.where(place_b, weight_of.T[:, None, :], 0.0).reshape(slots, rows)
    combine_high = combine.astype(BF16)
    combine_low = (combine - combine_high.astype(F32)).astype(BF16)
    moe = dot(combine_high, returned, ((0,), (0,))) + dot(combine_low, returned, ((0,), (0,)))
    output = (hidden_in + moe).astype(BF16)
    products = dot(returned, out_grad, ((1,), (1,)))
    of_expert = jnp.sum(
        jnp.where(place_b, products.reshape(experts, capacity, rows), 0.0), axis=1
    ).T
    grad_route = jnp.sum(jnp.where(names, of_expert[:, None, :], 0.0), axis=2)

    in_grads = dot(whole, d_raw, ((0,), (0,))).astype(BF16)
    out_grads = dot(d_whole, mixed, ((0,), (0,))).astype(BF16)
    gains = jnp.pad(
        jnp.stack([grad_norm_mid, jnp.pad(jnp.concatenate([grad_query_gain, grad_key_gain]), (0, width - 2 * HD))]),
        ((1, 5), (0, 0)),
    )
    in_total, out_total, gains, d_came, *came = reduce_grads(
        in_grads, out_grads, gains, d_own, d_sent.astype(BF16), inputs * in_scale, sent
    )
    d_normed = d_own + d_came.astype(F32)
    d_inputs, _ = norm_back(inputs, in_scale, norm_in, d_normed)
    grad_tokens = (d_hidden_in + d_inputs).astype(BF16)
    grad_down, grad_gate, grad_up = [
        (dot(left, right, ((0,), (0,))) + half.astype(F32))[None]
        for (left, right), half in zip(halves, came)
    ]
    grad_norm_in, grad_norm_mid = gains[0], gains[1]
    grad_query_gain, grad_key_gain = gains[2, :HD], gains[2, HD : 2 * HD]
    return (
        output,
        grad_tokens,
        grad_norm_in,
        in_total[:, :q_cols],
        in_total[:, q_cols : q_cols + k_cols],
        in_total[:, q_cols + k_cols :],
        grad_query_gain,
        grad_key_gain,
        out_total.T,
        grad_norm_mid,
        grad_route,
        grad_gate,
        grad_up,
        grad_down,
    )


def solution(mesh):
    tokens_spec = P(("dp", "tensor"), None)
    columns, rows = P("dp", None, "tensor"), P("dp", "tensor", None)
    proj = P("dp", "tensor")
    return jax.shard_map(
        per_device,
        mesh=mesh,
        in_specs=(
            tokens_spec,
            P("dp"),
            P(),
            proj,
            proj,
            proj,
            P(),
            P(),
            P("tensor", "dp"),
            P(),
            tokens_spec,
            tokens_spec,
            columns,
            columns,
            rows,
            tokens_spec,
        ),
        out_specs=(
            tokens_spec,
            tokens_spec,
            P(),
            proj,
            proj,
            proj,
            P(),
            P(),
            P("tensor", "dp"),
            P(),
            tokens_spec,
            columns,
            columns,
            rows,
        ),
        check_vma=False,
    )
```

```python
import functools
import math

import jax
import jax.numpy as jnp
from jax import lax
from jax.experimental import pallas as pl
from jax.experimental.pallas import tpu as pltpu
from jax.sharding import PartitionSpec as P

HD = 128
TOP = 8
EPS = 1e-06
THETA = 1000000.0
BF16 = jnp.bfloat16
F32 = jnp.float32
MESH_ID = pl.DeviceIdType.MESH
ANY_SPEC = pl.BlockSpec(memory_space=pl.ANY)
VMEM_SPEC = pl.BlockSpec(memory_space=pltpu.VMEM)


def coordinates():
    dp = lax.axis_index("dp")
    return lax.div(dp, 16), lax.rem(lax.div(dp, 8), 2), lax.rem(lax.div(dp, 2), 4), lax.rem(dp, 2)


def device(z, x, y, core, tensor):
    return (((z * 2 + x) * 4 + y) * 2 + core, tensor)


def turn(at, step):
    return lax.rem(at + step, 4)


def send(src, dst, send_sem, recv_sem, to):
    copy = pltpu.make_async_remote_copy(
        src_ref=src,
        dst_ref=dst,
        send_sem=send_sem,
        recv_sem=recv_sem,
        device_id=to,
        device_id_type=MESH_ID,
    )
    copy.start()
    return copy


def greet(peers):
    barrier = pltpu.get_barrier_semaphore()
    for peer in peers:
        pl.semaphore_signal(barrier, inc=1, device_id=peer, device_id_type=MESH_ID)
    pl.semaphore_wait(barrier, len(peers))


STEPS = (1, 3, 2)


def reduce_kernel(
    ga, gb, gain, d_own, d_sent, x_hat, down, gate,
    oa, ob, og, d_came, down_c, gate_c,
    own_a, got_a, one_a, two_a, sum_a, three_a,
    own_b, got_b, one_b, two_b, sum_b, three_b,
    vec, vecs,
    load_sem, core_send, core_recv, one_send, one_recv, two_send, two_recv,
    three_send, three_recv, vec_send, vec_recv, pair_send, pair_recv,
):
    z, x, y, core = coordinates()
    tensor = lax.axis_index("tensor")
    sibling = device(z, x, y, 1 - core, tensor)
    along_z = [device(turn(z, s), x, y, core, tensor) for s in STEPS]
    along_y = [device(z, x, turn(y, s), core, tensor) for s in STEPS]
    across = device(z, 1 - x, y, core, tensor)
    near = [
        device(z, x, y, 1 - core, tensor),
        device(z, x, y, core, 1 - tensor),
        device(z, x, y, 1 - core, 1 - tensor),
    ]
    greet(along_z + along_y + [across] + near)

    vec_groups = (
        (near, core * 2 + tensor, 4),
        (along_z, z, 4),
        (along_y, y, 4),
        ([across], x, 2),
    )
    vec_copies = {}

    def vec_start(stage):
        peers, mine, _ = vec_groups[stage]
        if stage == 0:
            vec[0] = gain[...]
            vec[0, 0:1] = jnp.sum(
                (d_own[...] + d_came[...].astype(F32)) * x_hat[...], axis=0, keepdims=True
            )
        vecs[stage, mine] = vec[stage]
        vec_copies[stage] = [
            send(vec.at[stage], vecs.at[stage, mine], vec_send.at[stage, i], vec_recv.at[stage, i], peer)
            for i, peer in enumerate(peers)
        ]

    def vec_finish(stage):
        for copy in vec_copies[stage]:
            copy.wait()
        count = vec_groups[stage][2]
        total = vecs[stage, 0]
        for i in range(1, count):
            total = total + vecs[stage, i]
        if stage == 3:
            og[...] = total
        else:
            vec[stage + 1] = total

    partner = near[1]
    d_copy = send(d_sent, d_came, pair_send.at[0], pair_recv.at[0], partner)

    loads, swaps = {}, {}
    order = STEPS + (0,)
    for i, s in enumerate(order):
        to = turn(z, s)
        swaps["a", s] = send(ga.at[to, :, :, 1 - core], got_a.at[to], core_send.at[0, i], core_recv.at[0, i], sibling)
        loads["a", s] = pltpu.make_async_copy(ga.at[to, :, :, core], own_a.at[to], load_sem.at[0, i])
        loads["a", s].start()
        to = turn(y, s)
        swaps["b", s] = send(gb.at[:, :, to, 1 - core], got_b.at[to], core_send.at[1, i], core_recv.at[1, i], sibling)
        loads["b", s] = pltpu.make_async_copy(gb.at[:, :, to, core], own_b.at[to], load_sem.at[1, i])
        loads["b", s].start()

    def add_cores(own, got, to):
        shape = own.shape

        @pl.loop(0, shape[1])
        def _(i):
            @pl.loop(0, shape[2])
            def _(j):
                own[to, i, j] = (own[to, i, j].astype(F32) + got[to, i, j].astype(F32)).astype(BF16)

    ones = []
    expert = []
    for i, s in enumerate(order):
        if i == 1:
            d_copy.wait_recv()
            vec_start(0)
            expert.append(send(down, down_c, pair_send.at[1], pair_recv.at[1], partner))
            expert.append(send(gate, gate_c, pair_send.at[2], pair_recv.at[2], partner))
        loads["a", s].wait()
        swaps["a", s].wait_recv()
        add_cores(own_a, got_a, turn(z, s))
        if s:
            ones.append(send(own_a.at[turn(z, s)], one_a.at[i], one_send.at[0, i], one_recv.at[0, i], along_z[i]))
        loads["b", s].wait()
        swaps["b", s].wait_recv()
        add_cores(own_b, got_b, turn(y, s))
        if s:
            ones.append(send(own_b.at[turn(y, s)], one_b.at[i], one_send.at[1, i], one_recv.at[1, i], along_y[i]))
    vec_finish(0)
    vec_start(1)

    for copy in ones:
        copy.wait_recv()
    vec_finish(1)
    vec_start(2)
    twos = []
    for i, s in enumerate(order):
        to = turn(y, s)
        for k in range(2):
            sum_a[to, k] = (
                own_a[z, k, to].astype(F32) + one_a[0, k, to].astype(F32)
                + one_a[1, k, to].astype(F32) + one_a[2, k, to].astype(F32)
            ).astype(BF16)
        if s:
            twos.append(send(sum_a.at[to], two_a.at[i], two_send.at[0, i], two_recv.at[0, i], along_y[i]))
        to = turn(z, s)
        for k in range(2):
            sum_b[to, k] = (
                own_b[y, to, k].astype(F32) + one_b[0, to, k].astype(F32)
                + one_b[1, to, k].astype(F32) + one_b[2, to, k].astype(F32)
            ).astype(BF16)
        if s:
            twos.append(send(sum_b.at[to], two_b.at[i], two_send.at[1, i], two_recv.at[1, i], along_z[i]))

    for copy in twos:
        copy.wait_recv()
    vec_finish(2)
    vec_start(3)

    def last(sums, two, at, k):
        return (
            sums[at, k].astype(F32) + two[0, k].astype(F32) + two[1, k].astype(F32) + two[2, k].astype(F32)
        )

    three_a[0] = last(sum_a, two_a, y, 1 - x).astype(BF16)
    final_a = send(three_a.at[0], three_a.at[1], three_send.at[0], three_recv.at[0], across)
    three_b[0] = last(sum_b, two_b, z, 1 - x).astype(BF16)
    final_b = send(three_b.at[0], three_b.at[1], three_send.at[1], three_recv.at[1], across)
    mine_a = last(sum_a, two_a, y, x)
    final_a.wait_recv()
    oa[...] = mine_a + three_a[1].astype(F32)
    mine_b = last(sum_b, two_b, z, x)
    final_b.wait_recv()
    ob[...] = mine_b + three_b[1].astype(F32)
    vec_finish(3)
    for copy in expert:
        copy.wait_recv()
    for copy in list(swaps.values()) + ones + twos + [final_a, final_b, d_copy] + expert:
        copy.wait_send()


def reduce_grads(in_grads, out_grads, gains, d_own, d_sent, x_hat, expert):
    owners = lax.axis_size("dp")
    rows = in_grads.shape[0] // owners
    a_cols, b_cols = in_grads.shape[1], out_grads.shape[1]
    dma = pltpu.SemaphoreType.DMA
    vmem = pltpu.VMEM

    def scratch(cols, inner):
        return [
            vmem((4,) + inner + (rows, cols), BF16),
            vmem((4,) + inner + (rows, cols), BF16),
            vmem((3,) + inner + (rows, cols), BF16),
            vmem((3, 2, rows, cols), BF16),
            vmem((4, 2, rows, cols), BF16),
            vmem((2, rows, cols), BF16),
        ]

    return pl.pallas_call(
        reduce_kernel,
        out_shape=(
            jax.ShapeDtypeStruct((rows, a_cols), F32),
            jax.ShapeDtypeStruct((rows, b_cols), F32),
            jax.ShapeDtypeStruct(gains.shape, F32),
            jax.ShapeDtypeStruct(d_sent.shape, BF16),
            *[jax.ShapeDtypeStruct(half.shape, BF16) for half in expert],
        ),
        in_specs=[ANY_SPEC] * 2 + [VMEM_SPEC] * 4 + [ANY_SPEC] * 2,
        out_specs=[VMEM_SPEC] * 4 + [ANY_SPEC] * 2,
        scratch_shapes=scratch(a_cols, (2, 4))
        + scratch(b_cols, (4, 2))
        + [
            vmem((4,) + gains.shape, F32),
            vmem((4, 4) + gains.shape, F32),
            dma((2, 4)),
            dma((2, 4)),
            dma((2, 4)),
            dma((2, 3)),
            dma((2, 3)),
            dma((2, 3)),
            dma((2, 3)),
            dma((2,)),
            dma((2,)),
            dma((4, 3)),
            dma((4, 3)),
            dma((3,)),
            dma((3,)),
        ],
        compiler_params=pltpu.CompilerParams(
            collective_id=1, has_side_effects=True, vmem_limit_bytes=56 * 1024 * 1024
        ),
        cost_estimate=pl.CostEstimate(flops=10_000_000, bytes_accessed=300_000_000, transcendentals=0),
    )(
        in_grads.reshape(4, 2, 4, 2, rows, a_cols),
        out_grads.reshape(4, 2, 4, 2, rows, b_cols),
        gains,
        d_own,
        d_sent,
        x_hat,
        *expert,
    )


def ring(view, at, up, down, sends, recvs, arrived):
    both = pl.ds(0, 2)

    def start(place, half, i, to):
        block = view(place, half)
        return send(block, block, sends.at[i], recvs.at[i], to)

    copies = [start(at, both, 0, up), start(at, both, 1, down)]
    yield copies
    copies[0].wait_recv()
    copies.append(start(turn(at, 3), 0, 2, up))
    arrived(turn(at, 3))
    yield
    copies[1].wait_recv()
    copies.append(start(turn(at, 1), 1, 3, down))
    arrived(turn(at, 1))
    yield
    copies[2].wait_recv()
    copies[3].wait_recv()
    arrived(turn(at, 2))
    yield


def together(*rings):
    copies = [next(r) for r in rings]
    for _ in range(3):
        for r in rings:
            next(r)
    return [c for group in copies for c in group]


def gather_kernel(
    sa, sb, part, down, gate, fa, fb, whole, down_o, gate_o,
    keep_sem, x_send, x_recv, one_send, one_recv, two_send, two_recv, core_send, core_recv, pair_send, pair_recv,
):
    z, x, y, core = coordinates()
    tensor = lax.axis_index("tensor")
    sibling = device(z, x, y, 1 - core, tensor)
    across = device(z, 1 - x, y, core, tensor)
    partner = device(z, x, y, core, 1 - tensor)
    around_z = device(turn(z, 1), x, y, core, tensor), device(turn(z, 3), x, y, core, tensor)
    around_y = device(z, x, turn(y, 1), core, tensor), device(z, x, turn(y, 3), core, tensor)
    greet([sibling, across, partner, *around_z, *around_y])

    pair = send(part, whole.at[tensor], pair_send.at[0], pair_recv.at[0], partner)
    a_own, b_own = fa.at[z, x, y, core], fb.at[z, x, y, core]
    over = [
        send(sa, a_own, x_send.at[0], x_recv.at[0], across),
        send(sb, b_own, x_send.at[1], x_recv.at[1], across),
    ]
    expert = [
        send(src, dst, pair_send.at[i], pair_recv.at[i], partner)
        for i, (src, dst) in enumerate(((down, down_o), (gate, gate_o)), 1)
    ]
    keep = [
        pltpu.make_async_copy(part, whole.at[tensor], keep_sem.at[0]),
        pltpu.make_async_copy(sa, a_own, keep_sem.at[1]),
        pltpu.make_async_copy(sb, b_own, keep_sem.at[2]),
    ]
    for copy in keep:
        copy.start()
    keep[1].wait()
    keep[2].wait()
    over[0].wait_recv()
    over[1].wait_recv()

    def skip(place):
        return None

    small = together(
        ring(lambda i, h: fa.at[z, h, i, core], y, *around_y, one_send.at[0], one_recv.at[0], skip),
        ring(lambda i, h: fb.at[i, h, y, core], z, *around_z, one_send.at[1], one_recv.at[1], skip),
    )
    cores = []

    def hand_on(view):
        def arrived(place):
            block, k = view(place, pl.ds(0, 2)), len(cores)
            cores.append(send(block, block, core_send.at[k], core_recv.at[k], sibling))

        return arrived

    def view_a(i, h):
        return fa.at[i, h, :, core]

    def view_b(i, h):
        return fb.at[:, h, i, core]

    large = [
        ring(view_a, z, *around_z, two_send.at[0], two_recv.at[0], hand_on(view_a)),
        ring(view_b, y, *around_y, two_send.at[1], two_recv.at[1], hand_on(view_b)),
    ]
    copies = [next(r) for r in large]
    hand_on(view_a)(z)
    hand_on(view_b)(y)
    for _ in range(3):
        for r in large:
            next(r)
    keep[0].wait()
    pair.wait_recv()
    for copy in cores + expert:
        copy.wait_recv()
    for copy in expert + [pair] + over + small + copies[0] + copies[1] + cores:
        copy.wait_send()


def gather_weights(in_shard, out_shard, part, expert):
    owners = lax.axis_size("dp")
    (rows, a_cols), b_cols = in_shard.shape, out_shard.shape[1]
    dma = pltpu.SemaphoreType.DMA
    in_full, out_full, whole, *other = pl.pallas_call(
        gather_kernel,
        out_shape=(
            jax.ShapeDtypeStruct((4, 2, 4, 2, rows, a_cols), BF16),
            jax.ShapeDtypeStruct((4, 2, 4, 2, rows, b_cols), BF16),
            jax.ShapeDtypeStruct((2,) + part.shape, BF16),
            *[jax.ShapeDtypeStruct(w.shape, BF16) for w in expert],
        ),
        in_specs=[ANY_SPEC] * 5,
        out_specs=[ANY_SPEC] * 5,
        scratch_shapes=[
            dma((3,)),
            dma((2,)),
            dma((2,)),
            dma((2, 4)),
            dma((2, 4)),
            dma((2, 4)),
            dma((2, 4)),
            dma((8,)),
            dma((8,)),
            dma((4,)),
            dma((4,)),
        ],
        compiler_params=pltpu.CompilerParams(collective_id=2, has_side_effects=True),
        cost_estimate=pl.CostEstimate(flops=0, bytes_accessed=250_000_000, transcendentals=0),
    )(in_shard, out_shard, part, *expert)
    return (
        in_full.reshape(owners * rows, a_cols),
        out_full.reshape(owners * rows, b_cols),
        whole.reshape(-1, part.shape[1]),
        other,
    )


ROWS_FULL, ROWS_PART, CHUNKS = 16, 4, 4


def pack_kernel(weighted, values, place, part, *refs):
    out = refs[-1]
    width = values.shape[1]
    step = width // CHUNKS
    tokens = values.shape[0]
    main = jnp.dot(place[...], values[...], preferred_element_type=F32)
    rest = jnp.zeros((place.shape[0], step), F32)
    for j in range(CHUNKS):
        rest += jnp.dot(
            part[:, j * tokens : (j + 1) * tokens],
            values[:, j * step : (j + 1) * step],
            preferred_element_type=F32,
        )
    if weighted:
        main, rest = main * refs[0][...], rest * refs[1][...]
    out[:, :width] = main.astype(BF16)
    out[:, width:] = rest.astype(BF16)


def pack(values, place, part, weights=()):
    total, tokens = place.shape
    width = values.shape[1]
    block = total // 4
    return pl.pallas_call(
        functools.partial(pack_kernel, bool(weights)),
        grid=(4,),
        out_shape=jax.ShapeDtypeStruct((total, width + width // CHUNKS), BF16),
        in_specs=[
            pl.BlockSpec((tokens, width), lambda g: (0, 0)),
            pl.BlockSpec((block, tokens), lambda g: (g, 0)),
            pl.BlockSpec((block, CHUNKS * tokens), lambda g: (g, 0)),
        ]
        + [pl.BlockSpec((block, 1), lambda g: (g, 0))] * len(weights),
        out_specs=pl.BlockSpec((block, width + width // CHUNKS), lambda g: (g, 0)),
        cost_estimate=pl.CostEstimate(flops=1_000_000_000, bytes_accessed=8_000_000, transcendentals=0),
    )(values, place, part, *weights)


def expert_kernel(
    rows, grads, gate_m, gate_o, up_m, up_o, down_m, down_o,
    result, d_row, rows_out, grads_out, hidden, d_gate, d_up,
    gate_w, up_w, down_w,
):
    units = down_m.shape[0]

    @pl.when(pl.program_id(0) == 0)
    def _():
        gate_w[:, :units] = gate_m[...]
        gate_w[:, units:] = gate_o[...]
        up_w[:, :units] = up_m[...]
        up_w[:, units:] = up_o[...]
        down_w[:units] = down_m[...]
        down_w[units:] = down_o[...]

    block = rows.shape[0]
    width = down_w.shape[1]
    step = width // CHUNKS
    more = block // ROWS_FULL * ROWS_PART

    def picks(shape, axis, j):
        extra = lax.broadcasted_iota(jnp.int32, shape, axis)
        packed = lax.broadcasted_iota(jnp.int32, shape, 1 - axis)
        return (packed == (extra >> 2) * 16 + j * 4 + (extra & 3)).astype(F32).astype(BF16)

    def spread(src, dst):
        dst[:block] = src[:, :width]
        for j in range(CHUNKS):
            dst[block:, j * step : (j + 1) * step] = jnp.dot(
                picks((more, block), 0, j), src[:, width:], preferred_element_type=F32
            ).astype(BF16)

    def repack(dst, parts):
        rest = jnp.zeros((block, step), F32)
        for j in range(CHUNKS):
            full = parts(j).astype(BF16)
            dst[:, j * step : (j + 1) * step] = full[:block]
            rest += jnp.dot(picks((block, more), 1, j), full[block:], preferred_element_type=F32)
        dst[:, width:] = rest.astype(BF16)

    spread(rows, rows_out)
    gate = jnp.dot(rows_out[...], gate_w[...], preferred_element_type=F32)
    up = jnp.dot(rows_out[...], up_w[...], preferred_element_type=F32)
    sigma = jax.nn.sigmoid(gate)
    activated = gate * sigma
    hidden[...] = (activated * up).astype(BF16)
    spread(grads, grads_out)
    d_hidden = dot(grads_out[...], down_w[...], ((1,), (1,)))
    d_gate[...] = (d_hidden * up * (sigma * (1.0 + gate * (1.0 - sigma)))).astype(BF16)
    d_up[...] = (d_hidden * activated).astype(BF16)
    repack(
        d_row,
        lambda j: dot(d_gate[...], gate_w[j * step : (j + 1) * step], ((1,), (1,)))
        + dot(d_up[...], up_w[j * step : (j + 1) * step], ((1,), (1,))),
    )
    repack(
        result,
        lambda j: jnp.dot(hidden[...], down_w[:, j * step : (j + 1) * step], preferred_element_type=F32),
    )


def run_expert(rows, grads, gate_w, up_w, down_w):
    total, packed = rows.shape
    units, width = 2 * down_w[0].shape[0], down_w[0].shape[1]
    groups = 4
    block = total // groups
    full = block // ROWS_FULL * (ROWS_FULL + ROWS_PART)

    def whole_of(w):
        return pl.BlockSpec(w.shape, lambda g: (0, 0), pipeline_mode=pl.Buffered(1))

    def cut(rows, cols):
        return pl.BlockSpec((rows, cols), lambda g: (g, 0))

    def shape(cols):
        return jax.ShapeDtypeStruct((full * groups, cols), BF16)

    return pl.pallas_call(
        expert_kernel,
        grid=(groups,),
        out_shape=(
            jax.ShapeDtypeStruct((total, packed), BF16),
            jax.ShapeDtypeStruct((total, packed), BF16),
            shape(width),
            shape(width),
            shape(units),
            shape(units),
            shape(units),
        ),
        in_specs=[cut(block, packed)] * 2 + [whole_of(w) for w in (*gate_w, *up_w, *down_w)],
        out_specs=[cut(block, packed)] * 2 + [cut(full, width)] * 2 + [cut(full, units)] * 3,
        scratch_shapes=[
            pltpu.VMEM((width, units), BF16),
            pltpu.VMEM((width, units), BF16),
            pltpu.VMEM((units, width), BF16),
        ],
        compiler_params=pltpu.CompilerParams(vmem_limit_bytes=56 * 1024 * 1024),
        cost_estimate=pl.CostEstimate(
            flops=12 * full * groups * width * units, bytes_accessed=45_000_000, transcendentals=full * groups * units
        ),
    )(rows, grads, *gate_w, *up_w, *down_w)


def dot(left, right, contract):
    return lax.dot_general(left, right, (contract, ((), ())), preferred_element_type=F32)


def rms_scale(values):
    return lax.rsqrt(jnp.mean(values * values, axis=-1, keepdims=True) + EPS)


def norm_back(values, scale, gain, grad):
    scaled = gain * grad
    inner = jnp.mean(scaled * values, axis=-1, keepdims=True)
    d_values = scale * scaled - values * (scale * scale * scale) * inner
    axes = tuple(range(grad.ndim - 1))
    return (d_values, jnp.sum(grad * values * scale, axis=axes))


def rope_tables(positions, head_size):
    half = head_size // 2
    freqs = jnp.exp(jnp.arange(half, dtype=F32) * (-2.0 * math.log(THETA) / head_size))
    angles = positions.astype(F32)[:, None] * freqs[None, :]
    return (jnp.cos(angles)[:, None, :], jnp.sin(angles)[:, None, :])


def rotate(values, cosine, sine):
    half = values.shape[-1] // 2
    first = values[..., :half]
    second = values[..., half:]
    return jnp.concatenate(
        [first * cosine - second * sine, second * cosine + first * sine], axis=-1
    )


def rotate_back(grad, cosine, sine):
    half = grad.shape[-1] // 2
    first = grad[..., :half]
    second = grad[..., half:]
    return jnp.concatenate(
        [first * cosine + second * sine, second * cosine - first * sine], axis=-1
    )


def swap(values):
    return lax.ppermute(values, "tensor", [(0, 1), (1, 0)])


def share_sequence(values):
    other = swap(values)
    first = lax.axis_index("tensor") == 0
    return jnp.concatenate(
        [jnp.where(first, values, other), jnp.where(first, other, values)], axis=0
    )


def halves_of(total, rows):
    mine = lax.axis_index("tensor") * rows
    return (
        lax.dynamic_slice_in_dim(total, mine, rows, 0),
        lax.dynamic_slice_in_dim(total, rows - mine, rows, 0),
    )


def sum_sequence(total, rows):
    own, sent = halves_of(total, rows)
    return own + swap(sent.astype(BF16)).astype(F32)


def exchange(buffer):
    groups = [[dp * 2 + (dp // 8 % 2 ^ g) for dp in range(64)] for g in range(2)]
    return lax.all_to_all(
        buffer, ("dp", "tensor"), split_axis=0, concat_axis=0, tiled=True, axis_index_groups=groups
    )


def per_device(
    tokens,
    positions,
    norm_in,
    query_weight,
    key_weight,
    value_weight,
    query_gain,
    key_gain,
    out_weight,
    norm_mid,
    routed_experts,
    route_weight,
    gate_weight,
    up_weight,
    down_weight,
    out_grad,
):
    rows, width = tokens.shape
    owners = lax.axis_size("dp")
    experts = owners
    scale = HD ** (-0.5)

    inputs = tokens.astype(F32)
    in_scale = rms_scale(inputs)
    normed = (inputs * in_scale * norm_in).astype(BF16)
    gate_w, up_w, down_w = gate_weight[0], up_weight[0], down_weight[0]
    in_full, out_full, whole, (down_o, gate_o) = gather_weights(
        jnp.concatenate([query_weight, key_weight, value_weight], axis=1),
        out_weight.T,
        normed,
        (down_w, gate_w),
    )
    q_cols, k_cols = query_weight.shape[1], key_weight.shape[1]
    query_heads, key_heads = q_cols // HD, k_cols // HD
    group = query_heads // key_heads

    names = routed_experts[:, :, None] == jnp.arange(experts, dtype=jnp.int32)
    chosen = jnp.any(names, axis=1)
    weight_of = jnp.sum(jnp.where(names, route_weight[:, :, None], 0.0), axis=1)
    below = jnp.arange(rows)[:, None] > jnp.arange(rows)[None, :]
    rank = dot(below.astype(BF16), chosen.astype(BF16), ((1,), (0,))).astype(jnp.int32)
    rank = jnp.where(chosen, rank, -1).T
    spot = jnp.arange(ROWS_FULL, dtype=jnp.int32)
    in_place = rank[:, None, :] == spot[None, :, None]
    extra = rank[:, None, :] == ROWS_FULL + (spot % ROWS_PART)[None, :, None]
    quarter = jnp.arange(CHUNKS, dtype=jnp.int32)
    in_part = extra[:, :, None, :] & (
        (spot // ROWS_PART)[None, :, None, None] == quarter[None, None, :, None]
    )
    packed_rows = experts * ROWS_FULL
    place = in_place.reshape(packed_rows, rows).astype(BF16)
    part = in_part.reshape(packed_rows, CHUNKS * rows).astype(BF16)
    weight_t = weight_of.T
    place_weight = jnp.sum(jnp.where(in_place, weight_t[:, None, :], 0.0), axis=2).reshape(packed_rows, 1)
    part_weight = jnp.sum(jnp.where(extra, weight_t[:, None, :], 0.0), axis=2).reshape(packed_rows, 1)

    def to_experts(packed):
        return exchange(packed.reshape(experts, ROWS_FULL, -1)).reshape(packed_rows, -1)

    def quarters(values):
        return values.reshape(rows, CHUNKS, -1).transpose(1, 0, 2).reshape(CHUNKS * rows, -1)

    def to_tokens(packed, place, part):
        first = dot(place, packed[:, :width], ((0,), (0,)))
        rest = dot(part, packed[:, width:], ((0,), (0,)))
        return first + rest.reshape(CHUNKS, rows, -1).transpose(1, 0, 2).reshape(rows, width)

    grad = out_grad.astype(F32)
    d_rows = pack(out_grad, place, part, (place_weight, part_weight))
    d_rows, whole = lax.optimization_barrier((d_rows, whole))
    expert_grads = to_experts(d_rows)

    length = whole.shape[0]
    cosine, sine = rope_tables(positions, HD)
    raw = dot(whole, in_full, ((1,), (0,)))
    query_raw = raw[:, :q_cols].reshape(length, query_heads, HD)
    key_raw = raw[:, q_cols : q_cols + k_cols].reshape(length, key_heads, HD)
    value_low = raw[:, q_cols + k_cols :].astype(BF16).reshape(length, key_heads, HD)
    query_scale = rms_scale(query_raw)
    query = (
        rotate(query_raw * query_scale * query_gain, cosine, sine)
        .astype(BF16)
        .reshape(length, key_heads, group, HD)
    )
    key_scale = rms_scale(key_raw)
    key = rotate(key_raw * key_scale * key_gain, cosine, sine).astype(BF16)
    causal = jnp.arange(length)[:, None] >= jnp.arange(length)[None, :]
    scores = jnp.einsum("ahgd,bhd->hgab", query, key, preferred_element_type=F32) * scale
    scores = jnp.where(causal, scores, -1e30)
    peak = jnp.max(scores, axis=-1, keepdims=True)
    log_total = peak + jnp.log(jnp.sum(jnp.exp(scores - peak), axis=-1, keepdims=True))
    probs_low = jnp.exp(scores - log_total).astype(BF16)
    mixed = (
        jnp.einsum("hgab,bhd->ahgd", probs_low, value_low, preferred_element_type=F32)
        .astype(BF16)
        .reshape(length, q_cols)
    )
    attended = sum_sequence(dot(mixed, out_full, ((1,), (1,))), rows)
    hidden_in = inputs + attended
    mid_scale = rms_scale(hidden_in)
    normed_mid = (hidden_in * mid_scale * norm_mid).astype(BF16)

    send_rows = pack(normed_mid, place, part)
    send_rows, expert_grads, up_s = lax.optimization_barrier((send_rows, expert_grads, up_w))
    up_o = swap(up_s)
    result, d_row, rows_in, grads_in, hidden, d_gate, d_up = run_expert(
        to_experts(send_rows), expert_grads, (gate_w, gate_o), (up_w, up_o), (down_w, down_o)
    )
    back_rows = to_experts(d_row)
    units = down_w.shape[0]
    halves, others = [
        ((hidden[:, of], grads_in), (rows_in, d_gate[:, of]), (rows_in, d_up[:, of]))
        for of in (slice(0, units), slice(units, 2 * units))
    ]
    sent = [dot(left, right, ((0,), (0,))).astype(BF16) for left, right in others]

    d_mid = to_tokens(back_rows, place, part)
    d_mid_in, grad_norm_mid = norm_back(hidden_in, mid_scale, norm_mid, d_mid)
    d_hidden_in = grad + d_mid_in
    d_attended = d_hidden_in.astype(BF16)
    d_whole = share_sequence(d_attended)
    d_whole, result, up_sent = lax.optimization_barrier((d_whole, result, sent[2]))
    up_came = swap(up_sent)
    d_mixed = (
        dot(d_whole, out_full, ((1,), (0,))).astype(BF16).reshape(length, key_heads, group, HD)
    )
    probs = jnp.exp(scores - log_total)
    d_probs = jnp.einsum("ahgd,bhd->hgab", d_mixed, value_low, preferred_element_type=F32)
    value_grad = jnp.einsum("hgab,ahgd->bhd", probs_low, d_mixed, preferred_element_type=F32)
    delta = jnp.sum(probs * d_probs, axis=-1, keepdims=True)
    d_scores = (probs * (d_probs - delta)).astype(BF16)
    d_query = (
        jnp.einsum("hgab,bhd->ahgd", d_scores, key, preferred_element_type=F32).reshape(
            length, query_heads, HD
        )
        * scale
    )
    d_key = jnp.einsum("hgab,ahgd->bhd", d_scores, query, preferred_element_type=F32) * scale
    d_query_raw, grad_query_gain = norm_back(
        query_raw, query_scale, query_gain, rotate_back(d_query, cosine, sine)
    )
    d_key_raw, grad_key_gain = norm_back(
        key_raw, key_scale, key_gain, rotate_back(d_key, cosine, sine)
    )
    d_raw = jnp.concatenate(
        [
            d_query_raw.astype(BF16).reshape(length, q_cols),
            d_key_raw.astype(BF16).reshape(length, k_cols),
            value_grad.astype(BF16).reshape(length, k_cols),
        ],
        axis=1,
    )
    d_total = dot(d_raw, in_full, ((1,), (1,)))
    d_own, d_sent = halves_of(d_total, rows)

    returned = to_experts(result)
    in_grads = dot(whole, d_raw, ((0,), (0,))).astype(BF16)
    out_grads = dot(d_whole, mixed, ((0,), (0,))).astype(BF16)
    gains = jnp.pad(
        jnp.stack([grad_norm_mid, jnp.pad(jnp.concatenate([grad_query_gain, grad_key_gain]), (0, width - 2 * HD))]),
        ((1, 5), (0, 0)),
    )
    in_grads, returned, up_came = lax.optimization_barrier((in_grads, returned, up_came))
    in_total, out_total, gains, d_came, *came = reduce_grads(
        in_grads, out_grads, gains, d_own, d_sent.astype(BF16), inputs * in_scale, sent[:2]
    )
    place_high = (place * place_weight).astype(BF16)
    part_high = (part * part_weight).astype(BF16)
    place_low = (place * place_weight - place_high.astype(F32)).astype(BF16)
    part_low = (part * part_weight - part_high.astype(F32)).astype(BF16)
    moe = to_tokens(returned, place_high, part_high) + to_tokens(returned, place_low, part_low)
    output = (hidden_in + moe).astype(BF16)
    products = dot(returned[:, :width], out_grad, ((1,), (1,))) * place
    rest = dot(returned[:, width:], quarters(out_grad), ((1,), (1,))) * part
    of_row = products + jnp.sum(rest.reshape(packed_rows, CHUNKS, rows), axis=1)
    of_expert = jnp.sum(of_row.reshape(experts, ROWS_FULL, rows), axis=1).T
    grad_route = jnp.sum(jnp.where(names, of_expert[:, None, :], 0.0), axis=2)
    d_normed = d_own + d_came.astype(F32)
    d_inputs, _ = norm_back(inputs, in_scale, norm_in, d_normed)
    grad_tokens = (d_hidden_in + d_inputs).astype(BF16)
    grad_down, grad_gate, grad_up = [
        (dot(left, right, ((0,), (0,))) + half.astype(F32))[None]
        for (left, right), half in zip(halves, (*came, up_came))
    ]
    grad_norm_in, grad_norm_mid = gains[0], gains[1]
    grad_query_gain, grad_key_gain = gains[2, :HD], gains[2, HD : 2 * HD]
    return (
        output,
        grad_tokens,
        grad_norm_in,
        in_total[:, :q_cols],
        in_total[:, q_cols : q_cols + k_cols],
        in_total[:, q_cols + k_cols :],
        grad_query_gain,
        grad_key_gain,
        out_total.T,
        grad_norm_mid,
        grad_route,
        grad_gate,
        grad_up,
        grad_down,
    )


def solution(mesh):
    tokens_spec = P(("dp", "tensor"), None)
    columns, rows = P("dp", None, "tensor"), P("dp", "tensor", None)
    proj = P("dp", "tensor")
    return jax.shard_map(
        per_device,
        mesh=mesh,
        in_specs=(
            tokens_spec,
            P("dp"),
            P(),
            proj,
            proj,
            proj,
            P(),
            P(),
            P("tensor", "dp"),
            P(),
            tokens_spec,
            tokens_spec,
            columns,
            columns,
            rows,
            tokens_spec,
        ),
        out_specs=(
            tokens_spec,
            tokens_spec,
            P(),
            proj,
            proj,
            proj,
            P(),
            P(),
            P("tensor", "dp"),
            P(),
            tokens_spec,
            columns,
            columns,
            rows,
        ),
        check_vma=False,
    )
```

```python
import functools
import math

import jax
import jax.numpy as jnp
from jax import lax
from jax.experimental import pallas as pl
from jax.experimental.pallas import tpu as pltpu
from jax.sharding import PartitionSpec as P

HD = 128
TOP = 8
EPS = 1e-06
THETA = 1000000.0
BF16 = jnp.bfloat16
F32 = jnp.float32
MESH_ID = pl.DeviceIdType.MESH
ANY_SPEC = pl.BlockSpec(memory_space=pl.ANY)
VMEM_SPEC = pl.BlockSpec(memory_space=pltpu.VMEM)


def coordinates():
    dp = lax.axis_index("dp")
    return lax.div(dp, 16), lax.rem(lax.div(dp, 8), 2), lax.rem(lax.div(dp, 2), 4), lax.rem(dp, 2)


def device(z, x, y, core, tensor):
    return (((z * 2 + x) * 4 + y) * 2 + core, tensor)


def turn(at, step):
    return lax.rem(at + step, 4)


def send(src, dst, send_sem, recv_sem, to):
    copy = pltpu.make_async_remote_copy(
        src_ref=src,
        dst_ref=dst,
        send_sem=send_sem,
        recv_sem=recv_sem,
        device_id=to,
        device_id_type=MESH_ID,
    )
    copy.start()
    return copy


def greet(peers):
    barrier = pltpu.get_barrier_semaphore()
    for peer in peers:
        pl.semaphore_signal(barrier, inc=1, device_id=peer, device_id_type=MESH_ID)
    pl.semaphore_wait(barrier, len(peers))


STEPS = (1, 3, 2)


def reduce_kernel(
    ga, gb, gain, d_own, d_sent, x_hat, down, gate,
    oa, ob, og, d_came, down_c, gate_c,
    own_a, got_a, one_a, via_a, two_a, sum_a, three_a,
    own_b, got_b, one_b, via_b, two_b, sum_b, three_b,
    vec, vecs,
    load_sem, core_send, core_recv, one_send, one_recv, two_send, two_recv,
    three_send, three_recv, vec_send, vec_recv, pair_send, pair_recv,
):
    z, x, y, core = coordinates()
    tensor = lax.axis_index("tensor")
    sibling = device(z, x, y, 1 - core, tensor)
    along_z = [device(turn(z, s), x, y, core, tensor) for s in STEPS]
    along_y = [device(z, x, turn(y, s), core, tensor) for s in STEPS]
    across = device(z, 1 - x, y, core, tensor)
    near = [
        device(z, x, y, 1 - core, tensor),
        device(z, x, y, core, 1 - tensor),
        device(z, x, y, 1 - core, 1 - tensor),
    ]
    greet(along_z + along_y + [across] + near)

    vec_groups = (
        (near, core * 2 + tensor, 4),
        (along_z, z, 4),
        (along_y, y, 4),
        ([across], x, 2),
    )
    vec_copies = {}

    def vec_start(stage):
        peers, mine, _ = vec_groups[stage]
        if stage == 0:
            vec[0] = gain[...]
            vec[0, 0:1] = jnp.sum(
                (d_own[...] + d_came[...].astype(F32)) * x_hat[...], axis=0, keepdims=True
            )
        vecs[stage, mine] = vec[stage]
        vec_copies[stage] = [
            send(vec.at[stage], vecs.at[stage, mine], vec_send.at[stage, i], vec_recv.at[stage, i], peer)
            for i, peer in enumerate(peers)
        ]

    def vec_finish(stage):
        for copy in vec_copies[stage]:
            copy.wait()
        count = vec_groups[stage][2]
        total = vecs[stage, 0]
        for i in range(1, count):
            total = total + vecs[stage, i]
        if stage == 3:
            og[...] = total
        else:
            vec[stage + 1] = total

    partner = near[1]
    d_copy = send(d_sent, d_came, pair_send.at[0], pair_recv.at[0], partner)

    loads, swaps = {}, {}
    order = (2, 1, 3, 0)
    for i, s in enumerate(order):
        to = turn(z, s)
        swaps["a", s] = send(ga.at[to, :, :, 1 - core], got_a.at[to], core_send.at[0, i], core_recv.at[0, i], sibling)
        loads["a", s] = pltpu.make_async_copy(ga.at[to, :, :, core], own_a.at[to], load_sem.at[0, i])
        loads["a", s].start()
        to = turn(y, s)
        swaps["b", s] = send(gb.at[:, :, to, 1 - core], got_b.at[to], core_send.at[1, i], core_recv.at[1, i], sibling)
        loads["b", s] = pltpu.make_async_copy(gb.at[:, :, to, core], own_b.at[to], load_sem.at[1, i])
        loads["b", s].start()

    def add_cores(own, got, to):
        shape = own.shape

        @pl.loop(0, shape[1])
        def _(i):
            @pl.loop(0, shape[2])
            def _(j):
                own[to, i, j] = (own[to, i, j].astype(F32) + got[to, i, j].astype(F32)).astype(BF16)

    def round_ring(own, got, via, one, at, up, down, name, row):
        n = own.shape[1] // 2
        halves = pl.ds(0, n), pl.ds(n, n)
        above, far, below = turn(at, 1), turn(at, 2), turn(at, 3)

        def step(src, dst, i, to):
            return send(src, dst, one_send.at[row, i], one_recv.at[row, i], to)

        def ready(s):
            loads[name, s].wait()
            swaps[name, s].wait_recv()
            add_cores(own, got, turn(at, s))

        def pass_on(k, to):
            first = k * n

            @pl.loop(0, n)
            def _(i):
                @pl.loop(0, own.shape[2])
                def _(j):
                    own[to, first + i, j] = (
                        own[to, first + i, j].astype(F32) + via[k, i, j].astype(F32)
                    ).astype(BF16)

        ready(2)
        copies = [step(own.at[far, halves[0]], via.at[0], 0, up), step(own.at[far, halves[1]], via.at[1], 1, down)]
        yield copies
        ready(1)
        copies.append(step(own.at[above, halves[1]], one.at[0, halves[1]], 2, up))
        yield
        ready(3)
        copies.append(step(own.at[below, halves[0]], one.at[1, halves[0]], 3, down))
        yield
        copies[0].wait_recv()
        pass_on(0, above)
        copies.append(step(own.at[above, halves[0]], one.at[0, halves[0]], 4, up))
        yield
        copies[1].wait_recv()
        pass_on(1, below)
        copies.append(step(own.at[below, halves[1]], one.at[1, halves[1]], 5, down))
        yield
        ready(0)
        yield

    rings = [
        round_ring(own_a, got_a, via_a, one_a, z, along_z[0], along_z[1], "a", 0),
        round_ring(own_b, got_b, via_b, one_b, y, along_y[0], along_y[1], "b", 1),
    ]
    firsts = [next(r) for r in rings]
    d_copy.wait_recv()
    vec_start(0)
    expert = [
        send(down, down_c, pair_send.at[1], pair_recv.at[1], partner),
        send(gate, gate_c, pair_send.at[2], pair_recv.at[2], partner),
    ]
    for _ in range(5):
        for r in rings:
            next(r)
    ones = firsts[0] + firsts[1]
    vec_finish(0)
    vec_start(1)

    for copy in firsts[0][2:] + firsts[1][2:]:
        copy.wait_recv()
    vec_finish(1)
    vec_start(2)
    twos = []
    for i, s in enumerate(STEPS + (0,)):
        to = turn(y, s)
        for k in range(2):
            sum_a[to, k] = (
                own_a[z, k, to].astype(F32) + one_a[0, k, to].astype(F32) + one_a[1, k, to].astype(F32)
            ).astype(BF16)
        if s:
            twos.append(send(sum_a.at[to], two_a.at[i], two_send.at[0, i], two_recv.at[0, i], along_y[i]))
        to = turn(z, s)
        for k in range(2):
            sum_b[to, k] = (
                own_b[y, to, k].astype(F32) + one_b[0, to, k].astype(F32) + one_b[1, to, k].astype(F32)
            ).astype(BF16)
        if s:
            twos.append(send(sum_b.at[to], two_b.at[i], two_send.at[1, i], two_recv.at[1, i], along_z[i]))

    for copy in twos:
        copy.wait_recv()
    vec_finish(2)
    vec_start(3)

    def last(sums, two, at, k):
        return (
            sums[at, k].astype(F32) + two[0, k].astype(F32) + two[1, k].astype(F32) + two[2, k].astype(F32)
        )

    three_a[0] = last(sum_a, two_a, y, 1 - x).astype(BF16)
    final_a = send(three_a.at[0], three_a.at[1], three_send.at[0], three_recv.at[0], across)
    three_b[0] = last(sum_b, two_b, z, 1 - x).astype(BF16)
    final_b = send(three_b.at[0], three_b.at[1], three_send.at[1], three_recv.at[1], across)
    mine_a = last(sum_a, two_a, y, x)
    final_a.wait_recv()
    oa[...] = mine_a + three_a[1].astype(F32)
    mine_b = last(sum_b, two_b, z, x)
    final_b.wait_recv()
    ob[...] = mine_b + three_b[1].astype(F32)
    vec_finish(3)
    for copy in expert:
        copy.wait_recv()
    for copy in list(swaps.values()) + ones + twos + [final_a, final_b, d_copy] + expert:
        copy.wait_send()


def reduce_grads(in_grads, out_grads, gains, d_own, d_sent, x_hat, expert):
    owners = lax.axis_size("dp")
    rows = in_grads.shape[0] // owners
    a_cols, b_cols = in_grads.shape[1], out_grads.shape[1]
    dma = pltpu.SemaphoreType.DMA
    vmem = pltpu.VMEM

    def scratch(cols, inner):
        return [
            vmem((4,) + inner + (rows, cols), BF16),
            vmem((4,) + inner + (rows, cols), BF16),
            vmem((2,) + inner + (rows, cols), BF16),
            vmem((2, inner[0] // 2, inner[1], rows, cols), BF16),
            vmem((3, 2, rows, cols), BF16),
            vmem((4, 2, rows, cols), BF16),
            vmem((2, rows, cols), BF16),
        ]

    return pl.pallas_call(
        reduce_kernel,
        out_shape=(
            jax.ShapeDtypeStruct((rows, a_cols), F32),
            jax.ShapeDtypeStruct((rows, b_cols), F32),
            jax.ShapeDtypeStruct(gains.shape, F32),
            jax.ShapeDtypeStruct(d_sent.shape, BF16),
            *[jax.ShapeDtypeStruct(half.shape, BF16) for half in expert],
        ),
        in_specs=[ANY_SPEC] * 2 + [VMEM_SPEC] * 4 + [ANY_SPEC] * 2,
        out_specs=[VMEM_SPEC] * 4 + [ANY_SPEC] * 2,
        scratch_shapes=scratch(a_cols, (2, 4))
        + scratch(b_cols, (4, 2))
        + [
            vmem((4,) + gains.shape, F32),
            vmem((4, 4) + gains.shape, F32),
            dma((2, 4)),
            dma((2, 4)),
            dma((2, 4)),
            dma((2, 6)),
            dma((2, 6)),
            dma((2, 3)),
            dma((2, 3)),
            dma((2,)),
            dma((2,)),
            dma((4, 3)),
            dma((4, 3)),
            dma((3,)),
            dma((3,)),
        ],
        compiler_params=pltpu.CompilerParams(
            collective_id=1, has_side_effects=True, vmem_limit_bytes=56 * 1024 * 1024
        ),
        cost_estimate=pl.CostEstimate(flops=10_000_000, bytes_accessed=300_000_000, transcendentals=0),
    )(
        in_grads.reshape(4, 2, 4, 2, rows, a_cols),
        out_grads.reshape(4, 2, 4, 2, rows, b_cols),
        gains,
        d_own,
        d_sent,
        x_hat,
        *expert,
    )


def ring(view, at, up, down, sends, recvs, arrived):
    both = pl.ds(0, 2)

    def start(place, half, i, to):
        block = view(place, half)
        return send(block, block, sends.at[i], recvs.at[i], to)

    copies = [start(at, both, 0, up), start(at, both, 1, down)]
    yield copies
    copies[0].wait_recv()
    copies.append(start(turn(at, 3), 0, 2, up))
    arrived(turn(at, 3))
    yield
    copies[1].wait_recv()
    copies.append(start(turn(at, 1), 1, 3, down))
    arrived(turn(at, 1))
    yield
    copies[2].wait_recv()
    copies[3].wait_recv()
    arrived(turn(at, 2))
    yield


def together(*rings):
    copies = [next(r) for r in rings]
    for _ in range(3):
        for r in rings:
            next(r)
    return [c for group in copies for c in group]


def gather_kernel(
    sa, sb, part, down, gate, fa, fb, whole, down_o, gate_o,
    keep_sem, x_send, x_recv, one_send, one_recv, two_send, two_recv, core_send, core_recv, pair_send, pair_recv,
):
    z, x, y, core = coordinates()
    tensor = lax.axis_index("tensor")
    sibling = device(z, x, y, 1 - core, tensor)
    across = device(z, 1 - x, y, core, tensor)
    partner = device(z, x, y, core, 1 - tensor)
    around_z = device(turn(z, 1), x, y, core, tensor), device(turn(z, 3), x, y, core, tensor)
    around_y = device(z, x, turn(y, 1), core, tensor), device(z, x, turn(y, 3), core, tensor)
    greet([sibling, across, partner, *around_z, *around_y])

    pair = send(part, whole.at[tensor], pair_send.at[0], pair_recv.at[0], partner)
    a_own, b_own = fa.at[z, x, y, core], fb.at[z, x, y, core]
    over = [
        send(sa, a_own, x_send.at[0], x_recv.at[0], across),
        send(sb, b_own, x_send.at[1], x_recv.at[1], across),
    ]
    expert = [
        send(src, dst, pair_send.at[i], pair_recv.at[i], partner)
        for i, (src, dst) in enumerate(((down, down_o), (gate, gate_o)), 1)
    ]
    keep = [
        pltpu.make_async_copy(part, whole.at[tensor], keep_sem.at[0]),
        pltpu.make_async_copy(sa, a_own, keep_sem.at[1]),
        pltpu.make_async_copy(sb, b_own, keep_sem.at[2]),
    ]
    for copy in keep:
        copy.start()
    keep[1].wait()
    keep[2].wait()
    over[0].wait_recv()
    over[1].wait_recv()

    def skip(place):
        return None

    small = together(
        ring(lambda i, h: fa.at[z, h, i, core], y, *around_y, one_send.at[0], one_recv.at[0], skip),
        ring(lambda i, h: fb.at[i, h, y, core], z, *around_z, one_send.at[1], one_recv.at[1], skip),
    )
    cores = []

    def hand_on(view):
        def arrived(place):
            block, k = view(place, pl.ds(0, 2)), len(cores)
            cores.append(send(block, block, core_send.at[k], core_recv.at[k], sibling))

        return arrived

    def view_a(i, h):
        return fa.at[i, h, :, core]

    def view_b(i, h):
        return fb.at[:, h, i, core]

    large = [
        ring(view_a, z, *around_z, two_send.at[0], two_recv.at[0], hand_on(view_a)),
        ring(view_b, y, *around_y, two_send.at[1], two_recv.at[1], hand_on(view_b)),
    ]
    copies = [next(r) for r in large]
    hand_on(view_a)(z)
    hand_on(view_b)(y)
    for _ in range(3):
        for r in large:
            next(r)
    keep[0].wait()
    pair.wait_recv()
    for copy in cores + expert:
        copy.wait_recv()
    for copy in expert + [pair] + over + small + copies[0] + copies[1] + cores:
        copy.wait_send()


def gather_weights(in_shard, out_shard, part, expert):
    owners = lax.axis_size("dp")
    (rows, a_cols), b_cols = in_shard.shape, out_shard.shape[1]
    dma = pltpu.SemaphoreType.DMA
    in_full, out_full, whole, *other = pl.pallas_call(
        gather_kernel,
        out_shape=(
            jax.ShapeDtypeStruct((4, 2, 4, 2, rows, a_cols), BF16),
            jax.ShapeDtypeStruct((4, 2, 4, 2, rows, b_cols), BF16),
            jax.ShapeDtypeStruct((2,) + part.shape, BF16),
            *[jax.ShapeDtypeStruct(w.shape, BF16) for w in expert],
        ),
        in_specs=[ANY_SPEC] * 5,
        out_specs=[ANY_SPEC] * 5,
        scratch_shapes=[
            dma((3,)),
            dma((2,)),
            dma((2,)),
            dma((2, 4)),
            dma((2, 4)),
            dma((2, 4)),
            dma((2, 4)),
            dma((8,)),
            dma((8,)),
            dma((4,)),
            dma((4,)),
        ],
        compiler_params=pltpu.CompilerParams(collective_id=2, has_side_effects=True),
        cost_estimate=pl.CostEstimate(flops=0, bytes_accessed=250_000_000, transcendentals=0),
    )(in_shard, out_shard, part, *expert)
    return (
        in_full.reshape(owners * rows, a_cols),
        out_full.reshape(owners * rows, b_cols),
        whole.reshape(-1, part.shape[1]),
        other,
    )


ROWS_FULL, ROWS_PART, CHUNKS = 16, 4, 4


def pack_kernel(weighted, values, place, part, *refs):
    out = refs[-1]
    width = values.shape[1]
    step = width // CHUNKS
    tokens = values.shape[0]
    main = jnp.dot(place[...], values[...], preferred_element_type=F32)
    rest = jnp.zeros((place.shape[0], step), F32)
    for j in range(CHUNKS):
        rest += jnp.dot(
            part[:, j * tokens : (j + 1) * tokens],
            values[:, j * step : (j + 1) * step],
            preferred_element_type=F32,
        )
    if weighted:
        main, rest = main * refs[0][...], rest * refs[1][...]
    out[:, :width] = main.astype(BF16)
    out[:, width:] = rest.astype(BF16)


def pack(values, place, part, weights=()):
    total, tokens = place.shape
    width = values.shape[1]
    block = total // 4
    return pl.pallas_call(
        functools.partial(pack_kernel, bool(weights)),
        grid=(4,),
        out_shape=jax.ShapeDtypeStruct((total, width + width // CHUNKS), BF16),
        in_specs=[
            pl.BlockSpec((tokens, width), lambda g: (0, 0)),
            pl.BlockSpec((block, tokens), lambda g: (g, 0)),
            pl.BlockSpec((block, CHUNKS * tokens), lambda g: (g, 0)),
        ]
        + [pl.BlockSpec((block, 1), lambda g: (g, 0))] * len(weights),
        out_specs=pl.BlockSpec((block, width + width // CHUNKS), lambda g: (g, 0)),
        cost_estimate=pl.CostEstimate(flops=1_000_000_000, bytes_accessed=8_000_000, transcendentals=0),
    )(values, place, part, *weights)


def expert_kernel(
    rows, grads, gate_m, gate_o, up_m, up_o, down_m, down_o,
    result, d_row, rows_out, grads_out, hidden, d_gate, d_up,
    gate_w, up_w, down_w,
):
    units = down_m.shape[0]

    @pl.when(pl.program_id(0) == 0)
    def _():
        gate_w[:, :units] = gate_m[...]
        gate_w[:, units:] = gate_o[...]
        up_w[:, :units] = up_m[...]
        up_w[:, units:] = up_o[...]
        down_w[:units] = down_m[...]
        down_w[units:] = down_o[...]

    block = rows.shape[0]
    width = down_w.shape[1]
    step = width // CHUNKS
    more = block // ROWS_FULL * ROWS_PART

    def picks(shape, axis, j):
        extra = lax.broadcasted_iota(jnp.int32, shape, axis)
        packed = lax.broadcasted_iota(jnp.int32, shape, 1 - axis)
        return (packed == (extra >> 2) * 16 + j * 4 + (extra & 3)).astype(F32).astype(BF16)

    def spread(src, dst):
        dst[:block] = src[:, :width]
        for j in range(CHUNKS):
            dst[block:, j * step : (j + 1) * step] = jnp.dot(
                picks((more, block), 0, j), src[:, width:], preferred_element_type=F32
            ).astype(BF16)

    def repack(dst, parts):
        rest = jnp.zeros((block, step), F32)
        for j in range(CHUNKS):
            full = parts(j).astype(BF16)
            dst[:, j * step : (j + 1) * step] = full[:block]
            rest += jnp.dot(picks((block, more), 1, j), full[block:], preferred_element_type=F32)
        dst[:, width:] = rest.astype(BF16)

    spread(rows, rows_out)
    gate = jnp.dot(rows_out[...], gate_w[...], preferred_element_type=F32)
    up = jnp.dot(rows_out[...], up_w[...], preferred_element_type=F32)
    sigma = jax.nn.sigmoid(gate)
    activated = gate * sigma
    hidden[...] = (activated * up).astype(BF16)
    spread(grads, grads_out)
    d_hidden = dot(grads_out[...], down_w[...], ((1,), (1,)))
    d_gate[...] = (d_hidden * up * (sigma * (1.0 + gate * (1.0 - sigma)))).astype(BF16)
    d_up[...] = (d_hidden * activated).astype(BF16)
    repack(
        d_row,
        lambda j: dot(d_gate[...], gate_w[j * step : (j + 1) * step], ((1,), (1,)))
        + dot(d_up[...], up_w[j * step : (j + 1) * step], ((1,), (1,))),
    )
    repack(
        result,
        lambda j: jnp.dot(hidden[...], down_w[:, j * step : (j + 1) * step], preferred_element_type=F32),
    )


def run_expert(rows, grads, gate_w, up_w, down_w):
    total, packed = rows.shape
    units, width = 2 * down_w[0].shape[0], down_w[0].shape[1]
    groups = 4
    block = total // groups
    full = block // ROWS_FULL * (ROWS_FULL + ROWS_PART)

    def whole_of(w):
        return pl.BlockSpec(w.shape, lambda g: (0, 0), pipeline_mode=pl.Buffered(1))

    def cut(rows, cols):
        return pl.BlockSpec((rows, cols), lambda g: (g, 0))

    def shape(cols):
        return jax.ShapeDtypeStruct((full * groups, cols), BF16)

    return pl.pallas_call(
        expert_kernel,
        grid=(groups,),
        out_shape=(
            jax.ShapeDtypeStruct((total, packed), BF16),
            jax.ShapeDtypeStruct((total, packed), BF16),
            shape(width),
            shape(width),
            shape(units),
            shape(units),
            shape(units),
        ),
        in_specs=[cut(block, packed)] * 2 + [whole_of(w) for w in (*gate_w, *up_w, *down_w)],
        out_specs=[cut(block, packed)] * 2 + [cut(full, width)] * 2 + [cut(full, units)] * 3,
        scratch_shapes=[
            pltpu.VMEM((width, units), BF16),
            pltpu.VMEM((width, units), BF16),
            pltpu.VMEM((units, width), BF16),
        ],
        compiler_params=pltpu.CompilerParams(vmem_limit_bytes=56 * 1024 * 1024),
        cost_estimate=pl.CostEstimate(
            flops=12 * full * groups * width * units, bytes_accessed=45_000_000, transcendentals=full * groups * units
        ),
    )(rows, grads, *gate_w, *up_w, *down_w)


def dot(left, right, contract):
    return lax.dot_general(left, right, (contract, ((), ())), preferred_element_type=F32)


def rms_scale(values):
    return lax.rsqrt(jnp.mean(values * values, axis=-1, keepdims=True) + EPS)


def norm_back(values, scale, gain, grad):
    scaled = gain * grad
    inner = jnp.mean(scaled * values, axis=-1, keepdims=True)
    d_values = scale * scaled - values * (scale * scale * scale) * inner
    axes = tuple(range(grad.ndim - 1))
    return (d_values, jnp.sum(grad * values * scale, axis=axes))


def head_columns(at):
    return pl.ds(pl.multiple_of(at * HD, HD), HD)


def head_probs(query, key):
    scores = dot(query, key, ((1,), (1,))) * HD ** (-0.5)
    shape = scores.shape
    causal = lax.broadcasted_iota(jnp.int32, shape, 0) >= lax.broadcasted_iota(jnp.int32, shape, 1)
    scores = jnp.where(causal, scores, -1e30)
    powers = jnp.exp(scores - jnp.max(scores, axis=-1, keepdims=True))
    return powers / jnp.sum(powers, axis=-1, keepdims=True)


def attend_kernel(query_heads, key_heads, raw, cosine, sine, query_gain, key_gain, query, key, value, mixed):
    group = query_heads // key_heads

    def turned(values, gain):
        values = values * rms_scale(values) * gain[...]
        return (values * cosine[...] - pltpu.roll(values, HD // 2, 1) * sine[...]).astype(BF16)

    for g in range(key_heads):
        own = head_columns(g)
        key[:, own] = turned(raw[:, head_columns(query_heads + g)], key_gain)
        value[:, own] = raw[:, head_columns(query_heads + key_heads + g)].astype(BF16)

        @pl.loop(g * group, (g + 1) * group)
        def _(h):
            at = head_columns(h)
            query[:, at] = turned(raw[:, at], query_gain)
            probs = head_probs(query[:, at], key[:, own])
            mixed[:, at] = dot(probs.astype(BF16), value[:, own], ((1,), (0,))).astype(BF16)


def attend(raw, cosine, sine, query_gain, key_gain, query_heads, key_heads):
    length = raw.shape[0]
    cols = [query_heads * HD, key_heads * HD, key_heads * HD, query_heads * HD]
    return pl.pallas_call(
        functools.partial(attend_kernel, query_heads, key_heads),
        out_shape=[jax.ShapeDtypeStruct((length, c), BF16) for c in cols],
        in_specs=[VMEM_SPEC] * 5,
        out_specs=[VMEM_SPEC] * 4,
        compiler_params=pltpu.CompilerParams(vmem_limit_bytes=48 * 1024 * 1024),
        cost_estimate=pl.CostEstimate(flops=600_000_000, bytes_accessed=6_000_000, transcendentals=1_100_000),
    )(raw, cosine, sine, query_gain[None], key_gain[None])


def attend_back_kernel(
    query_heads, key_heads, raw, cosine, sine, query_gain, key_gain, query, key, value, d_mixed,
    d_raw, gain_sums, d_key, d_value,
):
    group = query_heads // key_heads
    scale = HD ** (-0.5)

    def through_norm(values, gain, d_turned, row):
        d_out = d_turned * cosine[...] + pltpu.roll(d_turned, HD // 2, 1) * sine[...]
        norm = rms_scale(values)
        scaled = gain[...] * d_out
        inner = jnp.mean(scaled * values, axis=-1, keepdims=True)
        gain_sums[row : row + 1] += jnp.sum(d_out * values * norm, axis=0, keepdims=True)
        return (norm * scaled - values * (norm * norm * norm) * inner).astype(BF16)

    gain_sums[...] = jnp.zeros_like(gain_sums)
    for g in range(key_heads):
        own = head_columns(g)
        d_key[...] = jnp.zeros_like(d_key)
        d_value[...] = jnp.zeros_like(d_value)

        @pl.loop(g * group, (g + 1) * group)
        def _(h):
            at = head_columns(h)
            probs = head_probs(query[:, at], key[:, own])
            d_probs = dot(d_mixed[:, at], value[:, own], ((1,), (1,)))
            d_value[...] += dot(probs.astype(BF16), d_mixed[:, at], ((0,), (0,)))
            delta = jnp.sum(probs * d_probs, axis=-1, keepdims=True)
            d_scores = (probs * (d_probs - delta)).astype(BF16)
            d_key[...] += dot(d_scores, query[:, at], ((0,), (0,)))
            d_query = dot(d_scores, key[:, own], ((1,), (0,))) * scale
            d_raw[:, at] = through_norm(raw[:, at], query_gain, d_query, 0)

        at = head_columns(query_heads + g)
        d_raw[:, at] = through_norm(raw[:, at], key_gain, d_key[...] * scale, 1)
        d_raw[:, head_columns(query_heads + key_heads + g)] = d_value[...].astype(BF16)


def attend_back(raw, cosine, sine, query_gain, key_gain, query, key, value, d_mixed):
    length = raw.shape[0]
    query_heads, key_heads = query.shape[1] // HD, key.shape[1] // HD
    return pl.pallas_call(
        functools.partial(attend_back_kernel, query_heads, key_heads),
        out_shape=(
            jax.ShapeDtypeStruct(raw.shape, BF16),
            jax.ShapeDtypeStruct((8, HD), F32),
        ),
        in_specs=[VMEM_SPEC] * 9,
        out_specs=[VMEM_SPEC] * 2,
        scratch_shapes=[pltpu.VMEM((length, HD), F32), pltpu.VMEM((length, HD), F32)],
        compiler_params=pltpu.CompilerParams(vmem_limit_bytes=48 * 1024 * 1024),
        cost_estimate=pl.CostEstimate(flops=1_000_000, bytes_accessed=1_000_000, transcendentals=0),
    )(raw, cosine, sine, query_gain[None], key_gain[None], query, key, value, d_mixed)


def output_kernel(returned, place, part, place_weight, part_weight, grad, base, out, of_expert, total):
    step = pl.program_id(0)
    width = grad.shape[1]
    tokens = grad.shape[0]
    cut = width // CHUNKS

    @pl.when(step == 0)
    def _():
        total[...] = base[...]

    def combine(weights, values):
        high = weights.astype(BF16)
        low = (weights - high.astype(F32)).astype(BF16)
        return dot(high, values, ((0,), (0,))) + dot(low, values, ((0,), (0,)))

    main, rest = returned[:, :width], returned[:, width:]
    total[...] += combine(place[...].astype(F32) * place_weight[...], main)
    products = dot(main, grad[...], ((1,), (1,))) * place[...].astype(F32)
    for j in range(CHUNKS):
        chosen = part[:, j * tokens : (j + 1) * tokens].astype(F32)
        at = slice(j * cut, (j + 1) * cut)
        total[:, at] += combine(chosen * part_weight[...], rest)
        products += dot(rest, grad[:, at], ((1,), (1,))) * chosen
    of_expert[...] = jnp.sum(products.reshape(-1, ROWS_FULL, tokens), axis=1)

    @pl.when(step == pl.num_programs(0) - 1)
    def _():
        out[...] = total[...].astype(BF16)


def finish_output(returned, place, part, place_weight, part_weight, grad, base):
    total, packed = returned.shape
    tokens, width = grad.shape
    groups = 4
    block = total // groups

    def cut(rows, cols):
        return pl.BlockSpec((rows, cols), lambda g: (g, 0))

    def fixed(cols):
        return pl.BlockSpec((tokens, cols), lambda g: (0, 0))

    return pl.pallas_call(
        output_kernel,
        grid=(groups,),
        out_shape=(
            jax.ShapeDtypeStruct((tokens, width), BF16),
            jax.ShapeDtypeStruct((total // ROWS_FULL, tokens), F32),
        ),
        in_specs=[cut(block, packed), cut(block, tokens), cut(block, CHUNKS * tokens), cut(block, 1), cut(block, 1)]
        + [fixed(width), fixed(width)],
        out_specs=[fixed(width), cut(block // ROWS_FULL, tokens)],
        scratch_shapes=[pltpu.VMEM((tokens, width), F32)],
        cost_estimate=pl.CostEstimate(flops=3_000_000_000, bytes_accessed=10_000_000, transcendentals=0),
    )(returned, place, part, place_weight, part_weight, grad, base)


def rope_tables(positions, head_size):
    half = head_size // 2
    freqs = jnp.exp(jnp.arange(half, dtype=F32) * (-2.0 * math.log(THETA) / head_size))
    angles = positions.astype(F32)[:, None] * freqs[None, :]
    cosine, sine = jnp.cos(angles), jnp.sin(angles)
    return jnp.concatenate([cosine, cosine], axis=1), jnp.concatenate([sine, -sine], axis=1)


def swap(values):
    return lax.ppermute(values, "tensor", [(0, 1), (1, 0)])


def share_sequence(values):
    other = swap(values)
    first = lax.axis_index("tensor") == 0
    return jnp.concatenate(
        [jnp.where(first, values, other), jnp.where(first, other, values)], axis=0
    )


def halves_of(total, rows):
    mine = lax.axis_index("tensor") * rows
    return (
        lax.dynamic_slice_in_dim(total, mine, rows, 0),
        lax.dynamic_slice_in_dim(total, rows - mine, rows, 0),
    )


def sum_sequence(total, rows):
    own, sent = halves_of(total, rows)
    return own + swap(sent.astype(BF16)).astype(F32)


def exchange(buffer):
    groups = [[dp * 2 + (dp // 8 % 2 ^ g) for dp in range(64)] for g in range(2)]
    return lax.all_to_all(
        buffer, ("dp", "tensor"), split_axis=0, concat_axis=0, tiled=True, axis_index_groups=groups
    )


def per_device(
    tokens,
    positions,
    norm_in,
    query_weight,
    key_weight,
    value_weight,
    query_gain,
    key_gain,
    out_weight,
    norm_mid,
    routed_experts,
    route_weight,
    gate_weight,
    up_weight,
    down_weight,
    out_grad,
):
    rows, width = tokens.shape
    owners = lax.axis_size("dp")
    experts = owners
    scale = HD ** (-0.5)

    inputs = tokens.astype(F32)
    in_scale = rms_scale(inputs)
    normed = (inputs * in_scale * norm_in).astype(BF16)
    gate_w, up_w, down_w = gate_weight[0], up_weight[0], down_weight[0]
    in_full, out_full, whole, (down_o, gate_o) = gather_weights(
        jnp.concatenate([query_weight, key_weight, value_weight], axis=1),
        out_weight.T,
        normed,
        (down_w, gate_w),
    )
    q_cols, k_cols = query_weight.shape[1], key_weight.shape[1]
    query_heads, key_heads = q_cols // HD, k_cols // HD

    names = routed_experts[:, :, None] == jnp.arange(experts, dtype=jnp.int32)
    chosen = jnp.any(names, axis=1)
    weight_of = jnp.sum(jnp.where(names, route_weight[:, :, None], 0.0), axis=1)
    below = jnp.arange(rows)[:, None] > jnp.arange(rows)[None, :]
    rank = dot(below.astype(BF16), chosen.astype(BF16), ((1,), (0,))).astype(jnp.int32)
    rank = jnp.where(chosen, rank, -1).T
    spot = jnp.arange(ROWS_FULL, dtype=jnp.int32)
    in_place = rank[:, None, :] == spot[None, :, None]
    extra = rank[:, None, :] == ROWS_FULL + (spot % ROWS_PART)[None, :, None]
    quarter = jnp.arange(CHUNKS, dtype=jnp.int32)
    in_part = extra[:, :, None, :] & (
        (spot // ROWS_PART)[None, :, None, None] == quarter[None, None, :, None]
    )
    packed_rows = experts * ROWS_FULL
    place = in_place.reshape(packed_rows, rows).astype(BF16)
    part = in_part.reshape(packed_rows, CHUNKS * rows).astype(BF16)
    weight_t = weight_of.T
    place_weight = jnp.sum(jnp.where(in_place, weight_t[:, None, :], 0.0), axis=2).reshape(packed_rows, 1)
    part_weight = jnp.sum(jnp.where(extra, weight_t[:, None, :], 0.0), axis=2).reshape(packed_rows, 1)

    def to_experts(packed):
        return exchange(packed.reshape(experts, ROWS_FULL, -1)).reshape(packed_rows, -1)

    def to_tokens(packed, place, part):
        first = dot(place, packed[:, :width], ((0,), (0,)))
        rest = dot(part, packed[:, width:], ((0,), (0,)))
        return first + rest.reshape(CHUNKS, rows, -1).transpose(1, 0, 2).reshape(rows, width)

    grad = out_grad.astype(F32)
    d_rows = pack(out_grad, place, part, (place_weight, part_weight))
    d_rows, whole = lax.optimization_barrier((d_rows, whole))
    expert_grads = to_experts(d_rows)

    cosine, sine = rope_tables(positions, HD)
    raw = dot(whole, in_full, ((1,), (0,)))
    query, key, value, mixed = attend(
        raw, cosine, sine, query_gain, key_gain, query_heads, key_heads
    )
    attended = sum_sequence(dot(mixed, out_full, ((1,), (1,))), rows)
    hidden_in = inputs + attended
    mid_scale = rms_scale(hidden_in)
    normed_mid = (hidden_in * mid_scale * norm_mid).astype(BF16)

    send_rows = pack(normed_mid, place, part)
    send_rows, expert_grads, up_s = lax.optimization_barrier((send_rows, expert_grads, up_w))
    up_o = swap(up_s)
    result, d_row, rows_in, grads_in, hidden, d_gate, d_up = run_expert(
        to_experts(send_rows), expert_grads, (gate_w, gate_o), (up_w, up_o), (down_w, down_o)
    )
    back_rows = to_experts(d_row)
    units = down_w.shape[0]
    halves, others = [
        ((hidden[:, of], grads_in), (rows_in, d_gate[:, of]), (rows_in, d_up[:, of]))
        for of in (slice(0, units), slice(units, 2 * units))
    ]
    sent = [dot(left, right, ((0,), (0,))).astype(BF16) for left, right in others]
    kept = [dot(left, right, ((0,), (0,))) for left, right in halves]
    gate_came = swap(sent[1])

    back_rows, result, gate_came, *kept = lax.optimization_barrier((back_rows, result, gate_came, *kept))
    d_mid = to_tokens(back_rows, place, part)
    d_mid_in, grad_norm_mid = norm_back(hidden_in, mid_scale, norm_mid, d_mid)
    d_hidden_in = grad + d_mid_in
    d_attended = d_hidden_in.astype(BF16)
    d_whole = share_sequence(d_attended)
    d_mixed = dot(d_whole, out_full, ((1,), (0,))).astype(BF16)
    d_raw, gain_sums = attend_back(
        raw, cosine, sine, query_gain, key_gain, query, key, value, d_mixed
    )
    d_total = dot(d_raw, in_full, ((1,), (1,)))
    d_own, d_sent = halves_of(d_total, rows)

    returned = to_experts(result)
    in_grads = dot(whole, d_raw, ((0,), (0,))).astype(BF16)
    out_grads = dot(d_whole, mixed, ((0,), (0,))).astype(BF16)
    gain_row = jnp.pad(gain_sums[:2].reshape(1, -1), ((0, 0), (0, width - 2 * HD)))
    gains = jnp.pad(jnp.concatenate([grad_norm_mid[None], gain_row]), ((1, 5), (0, 0)))
    in_grads, returned = lax.optimization_barrier((in_grads, returned))
    in_total, out_total, gains, d_came, down_came, up_came = reduce_grads(
        in_grads, out_grads, gains, d_own, d_sent.astype(BF16), inputs * in_scale, (sent[0], sent[2])
    )
    output, of_expert = finish_output(
        returned, place, part, place_weight, part_weight, out_grad, hidden_in
    )
    of_expert = of_expert.T
    grad_route = jnp.sum(jnp.where(names, of_expert[:, None, :], 0.0), axis=2)
    d_normed = d_own + d_came.astype(F32)
    d_inputs, _ = norm_back(inputs, in_scale, norm_in, d_normed)
    grad_tokens = (d_hidden_in + d_inputs).astype(BF16)
    grad_down, grad_gate, grad_up = [
        (own + half.astype(F32))[None] for own, half in zip(kept, (down_came, gate_came, up_came))
    ]
    grad_norm_in, grad_norm_mid = gains[0], gains[1]
    grad_query_gain, grad_key_gain = gains[2, :HD], gains[2, HD : 2 * HD]
    return (
        output,
        grad_tokens,
        grad_norm_in,
        in_total[:, :q_cols],
        in_total[:, q_cols : q_cols + k_cols],
        in_total[:, q_cols + k_cols :],
        grad_query_gain,
        grad_key_gain,
        out_total.T,
        grad_norm_mid,
        grad_route,
        grad_gate,
        grad_up,
        grad_down,
    )


def solution(mesh):
    tokens_spec = P(("dp", "tensor"), None)
    columns, rows = P("dp", None, "tensor"), P("dp", "tensor", None)
    proj = P("dp", "tensor")
    return jax.shard_map(
        per_device,
        mesh=mesh,
        in_specs=(
            tokens_spec,
            P("dp"),
            P(),
            proj,
            proj,
            proj,
            P(),
            P(),
            P("tensor", "dp"),
            P(),
            tokens_spec,
            tokens_spec,
            columns,
            columns,
            rows,
            tokens_spec,
        ),
        out_specs=(
            tokens_spec,
            tokens_spec,
            P(),
            proj,
            proj,
            proj,
            P(),
            P(),
            P("tensor", "dp"),
            P(),
            tokens_spec,
            columns,
            columns,
            rows,
        ),
        check_vma=False,
    )
```

```python
import functools
import math

import jax
import jax.numpy as jnp
from jax import lax
from jax.experimental import pallas as pl
from jax.experimental.pallas import tpu as pltpu
from jax.sharding import PartitionSpec as P

HD = 128
TOP = 8
EPS = 1e-06
THETA = 1000000.0
BF16 = jnp.bfloat16
F32 = jnp.float32
MESH_ID = pl.DeviceIdType.MESH
ANY_SPEC = pl.BlockSpec(memory_space=pl.ANY)
VMEM_SPEC = pl.BlockSpec(memory_space=pltpu.VMEM)


def coordinates():
    dp = lax.axis_index("dp")
    return lax.div(dp, 16), lax.rem(lax.div(dp, 8), 2), lax.rem(lax.div(dp, 2), 4), lax.rem(dp, 2)


def device(z, x, y, core, tensor):
    return (((z * 2 + x) * 4 + y) * 2 + core, tensor)


def turn(at, step):
    return lax.rem(at + step, 4)


def send(src, dst, send_sem, recv_sem, to):
    copy = pltpu.make_async_remote_copy(
        src_ref=src,
        dst_ref=dst,
        send_sem=send_sem,
        recv_sem=recv_sem,
        device_id=to,
        device_id_type=MESH_ID,
    )
    copy.start()
    return copy


def greet(peers):
    barrier = pltpu.get_barrier_semaphore()
    for peer in peers:
        pl.semaphore_signal(barrier, inc=1, device_id=peer, device_id_type=MESH_ID)
    pl.semaphore_wait(barrier, len(peers))


STEPS = (1, 3, 2)


def combine_rows(weights, values):
    high = weights.astype(BF16)
    low = (weights - high.astype(F32)).astype(BF16)
    return dot(high, values, ((0,), (0,))) + dot(low, values, ((0,), (0,)))


def output_rows(at, returned, place, part, place_weight, part_weight, grad, total):
    tokens, width = grad.shape
    step = width // CHUNKS
    main, rest, picked = returned[at, :width], returned[at, width:], place[at].astype(F32)
    total[...] += combine_rows(picked * place_weight[at], main)
    products = dot(main, grad[...], ((1,), (1,))) * picked
    for j in range(CHUNKS):
        picked = part[at, j * tokens : (j + 1) * tokens].astype(F32)
        columns = slice(j * step, (j + 1) * step)
        total[:, columns] += combine_rows(picked * part_weight[at], rest)
        products += dot(rest, grad[:, columns], ((1,), (1,))) * picked
    return jnp.sum(products.reshape(-1, ROWS_FULL, tokens), axis=1)


def reduce_kernel(
    ga, gb, gain, d_own, d_sent, x_hat,
    returned, place, part, place_weight, part_weight, grad, base, down, gate,
    oa, ob, og, d_came, output, of_expert, down_c, gate_c,
    own_a, got_a, one_a, via_a, two_a, sum_a, three_a,
    own_b, got_b, one_b, via_b, two_b, sum_b, three_b,
    vec, vecs,
    load_sem, core_send, core_recv, one_send, one_recv, two_send, two_recv,
    three_send, three_recv, vec_send, vec_recv, pair_send, pair_recv, total,
):
    z, x, y, core = coordinates()
    tensor = lax.axis_index("tensor")
    sibling = device(z, x, y, 1 - core, tensor)
    along_z = [device(turn(z, s), x, y, core, tensor) for s in STEPS]
    along_y = [device(z, x, turn(y, s), core, tensor) for s in STEPS]
    across = device(z, 1 - x, y, core, tensor)
    near = [
        device(z, x, y, 1 - core, tensor),
        device(z, x, y, core, 1 - tensor),
        device(z, x, y, 1 - core, 1 - tensor),
    ]
    greet(along_z + along_y + [across] + near)

    vec_groups = (
        (near, core * 2 + tensor, 4),
        (along_z, z, 4),
        (along_y, y, 4),
        ([across], x, 2),
    )
    vec_copies = {}

    def vec_start(stage):
        peers, mine, _ = vec_groups[stage]
        if stage == 0:
            vec[0] = gain[...]
            vec[0, 0:1] = jnp.sum(
                (d_own[...] + d_came[...].astype(F32)) * x_hat[...], axis=0, keepdims=True
            )
        vecs[stage, mine] = vec[stage]
        vec_copies[stage] = [
            send(vec.at[stage], vecs.at[stage, mine], vec_send.at[stage, i], vec_recv.at[stage, i], peer)
            for i, peer in enumerate(peers)
        ]

    def vec_finish(stage):
        for copy in vec_copies[stage]:
            copy.wait()
        count = vec_groups[stage][2]
        added = vecs[stage, 0]
        for i in range(1, count):
            added = added + vecs[stage, i]
        if stage == 3:
            og[...] = added
        else:
            vec[stage + 1] = added

    partner = near[1]
    d_copy = send(d_sent, d_came, pair_send.at[0], pair_recv.at[0], partner)

    loads, swaps = {}, {}
    order = (2, 1, 3, 0)
    for i, s in enumerate(order):
        to = turn(z, s)
        swaps["a", s] = send(ga.at[to, :, :, 1 - core], got_a.at[to], core_send.at[0, i], core_recv.at[0, i], sibling)
        loads["a", s] = pltpu.make_async_copy(ga.at[to, :, :, core], own_a.at[to], load_sem.at[0, i])
        loads["a", s].start()
        to = turn(y, s)
        swaps["b", s] = send(gb.at[:, :, to, 1 - core], got_b.at[to], core_send.at[1, i], core_recv.at[1, i], sibling)
        loads["b", s] = pltpu.make_async_copy(gb.at[:, :, to, core], own_b.at[to], load_sem.at[1, i])
        loads["b", s].start()

    def add_cores(own, got, to):
        shape = own.shape

        @pl.loop(0, shape[1])
        def _(i):
            @pl.loop(0, shape[2])
            def _(j):
                own[to, i, j] += got[to, i, j]

    def round_ring(own, got, via, one, at, up, down, name, row):
        n = own.shape[1] // 2
        halves = pl.ds(0, n), pl.ds(n, n)
        above, far, below = turn(at, 1), turn(at, 2), turn(at, 3)

        def step(src, dst, i, to):
            return send(src, dst, one_send.at[row, i], one_recv.at[row, i], to)

        def ready(s):
            loads[name, s].wait()
            swaps[name, s].wait_recv()
            add_cores(own, got, turn(at, s))

        def pass_on(k, to):
            first = k * n

            @pl.loop(0, n)
            def _(i):
                @pl.loop(0, own.shape[2])
                def _(j):
                    own[to, first + i, j] += via[k, i, j]

        ready(2)
        copies = [step(own.at[far, halves[0]], via.at[0], 0, up), step(own.at[far, halves[1]], via.at[1], 1, down)]
        yield copies
        ready(1)
        copies.append(step(own.at[above, halves[1]], one.at[0, halves[1]], 2, up))
        yield
        ready(3)
        copies.append(step(own.at[below, halves[0]], one.at[1, halves[0]], 3, down))
        yield
        copies[0].wait_recv()
        pass_on(0, above)
        copies.append(step(own.at[above, halves[0]], one.at[0, halves[0]], 4, up))
        yield
        copies[1].wait_recv()
        pass_on(1, below)
        copies.append(step(own.at[below, halves[1]], one.at[1, halves[1]], 5, down))
        yield
        ready(0)
        yield

    rings = [
        round_ring(own_a, got_a, via_a, one_a, z, along_z[0], along_z[1], "a", 0),
        round_ring(own_b, got_b, via_b, one_b, y, along_y[0], along_y[1], "b", 1),
    ]
    firsts = [next(r) for r in rings]
    expert = [send(down, down_c, pair_send.at[1], pair_recv.at[1], partner)]
    for i in range(5):
        for r in rings:
            next(r)
        if i == 1:
            d_copy.wait_recv()
            vec_start(0)
            expert.append(send(gate, gate_c, pair_send.at[2], pair_recv.at[2], partner))
            total[...] = base[...]

            @pl.loop(0, returned.shape[0] // 256)
            def _(i):
                rows = pl.ds(pl.multiple_of(i * 256, 256), 256)
                experts = pl.ds(pl.multiple_of(i * 16, 16), 16)
                of_expert[experts] = output_rows(
                    rows, returned, place, part, place_weight, part_weight, grad, total
                )

            output[...] = total[...].astype(BF16)
    ones = firsts[0] + firsts[1]
    vec_finish(0)
    vec_start(1)

    for copy in firsts[0][2:] + firsts[1][2:]:
        copy.wait_recv()
    vec_finish(1)
    vec_start(2)
    twos = []
    for i, s in enumerate(STEPS + (0,)):
        to = turn(y, s)
        for k in range(2):
            sum_a[to, k] = (
                own_a[z, k, to].astype(F32) + one_a[0, k, to].astype(F32) + one_a[1, k, to].astype(F32)
            ).astype(BF16)
        if s:
            twos.append(send(sum_a.at[to], two_a.at[i], two_send.at[0, i], two_recv.at[0, i], along_y[i]))
        to = turn(z, s)
        for k in range(2):
            sum_b[to, k] = (
                own_b[y, to, k].astype(F32) + one_b[0, to, k].astype(F32) + one_b[1, to, k].astype(F32)
            ).astype(BF16)
        if s:
            twos.append(send(sum_b.at[to], two_b.at[i], two_send.at[1, i], two_recv.at[1, i], along_z[i]))

    for copy in twos:
        copy.wait_recv()
    vec_finish(2)
    vec_start(3)

    def last(sums, two, at, k):
        return (
            sums[at, k].astype(F32) + two[0, k].astype(F32) + two[1, k].astype(F32) + two[2, k].astype(F32)
        )

    three_a[0] = last(sum_a, two_a, y, 1 - x).astype(BF16)
    final_a = send(three_a.at[0], three_a.at[1], three_send.at[0], three_recv.at[0], across)
    three_b[0] = last(sum_b, two_b, z, 1 - x).astype(BF16)
    final_b = send(three_b.at[0], three_b.at[1], three_send.at[1], three_recv.at[1], across)
    mine_a = last(sum_a, two_a, y, x)
    final_a.wait_recv()
    oa[...] = mine_a + three_a[1].astype(F32)
    mine_b = last(sum_b, two_b, z, x)
    final_b.wait_recv()
    ob[...] = mine_b + three_b[1].astype(F32)
    vec_finish(3)
    for copy in expert:
        copy.wait_recv()
    for copy in list(swaps.values()) + ones + twos + [final_a, final_b, d_copy] + expert:
        copy.wait_send()


def reduce_grads(in_grads, out_grads, gains, d_own, d_sent, x_hat, routed, expert):
    owners = lax.axis_size("dp")
    rows = in_grads.shape[0] // owners
    a_cols, b_cols = in_grads.shape[1], out_grads.shape[1]
    dma = pltpu.SemaphoreType.DMA
    vmem = pltpu.VMEM

    def scratch(cols, inner):
        return [
            vmem((4,) + inner + (rows, cols), BF16),
            vmem((4,) + inner + (rows, cols), BF16),
            vmem((2,) + inner + (rows, cols), BF16),
            vmem((2, inner[0] // 2, inner[1], rows, cols), BF16),
            vmem((3, 2, rows, cols), BF16),
            vmem((4, 2, rows, cols), BF16),
            vmem((2, rows, cols), BF16),
        ]

    return pl.pallas_call(
        reduce_kernel,
        out_shape=(
            jax.ShapeDtypeStruct((rows, a_cols), F32),
            jax.ShapeDtypeStruct((rows, b_cols), F32),
            jax.ShapeDtypeStruct(gains.shape, F32),
            jax.ShapeDtypeStruct(d_sent.shape, BF16),
            jax.ShapeDtypeStruct(d_sent.shape, BF16),
            jax.ShapeDtypeStruct((owners, d_sent.shape[0]), F32),
            *[jax.ShapeDtypeStruct(half.shape, BF16) for half in expert],
        ),
        in_specs=[ANY_SPEC] * 2 + [VMEM_SPEC] * 11 + [ANY_SPEC] * 2,
        out_specs=[VMEM_SPEC] * 6 + [ANY_SPEC] * 2,
        scratch_shapes=scratch(a_cols, (2, 4))
        + scratch(b_cols, (4, 2))
        + [
            vmem((4,) + gains.shape, F32),
            vmem((4, 4) + gains.shape, F32),
            dma((2, 4)),
            dma((2, 4)),
            dma((2, 4)),
            dma((2, 6)),
            dma((2, 6)),
            dma((2, 3)),
            dma((2, 3)),
            dma((2,)),
            dma((2,)),
            dma((4, 3)),
            dma((4, 3)),
            dma((3,)),
            dma((3,)),
            vmem(d_sent.shape, F32),
        ],
        compiler_params=pltpu.CompilerParams(
            collective_id=1, has_side_effects=True, vmem_limit_bytes=56 * 1024 * 1024
        ),
        cost_estimate=pl.CostEstimate(flops=10_000_000, bytes_accessed=300_000_000, transcendentals=0),
    )(
        in_grads.reshape(4, 2, 4, 2, rows, a_cols),
        out_grads.reshape(4, 2, 4, 2, rows, b_cols),
        gains,
        d_own,
        d_sent,
        x_hat,
        *routed,
        *expert,
    )


def ring(view, at, up, down, sends, recvs, arrived):
    both = pl.ds(0, 2)

    def start(place, half, i, to):
        block = view(place, half)
        return send(block, block, sends.at[i], recvs.at[i], to)

    copies = [start(at, both, 0, up), start(at, both, 1, down)]
    yield copies
    copies[0].wait_recv()
    copies.append(start(turn(at, 3), 0, 2, up))
    arrived(turn(at, 3))
    yield
    copies[1].wait_recv()
    copies.append(start(turn(at, 1), 1, 3, down))
    arrived(turn(at, 1))
    yield
    copies[2].wait_recv()
    copies[3].wait_recv()
    arrived(turn(at, 2))
    yield
    yield copies


def gather_kernel(
    sa, sb, part, values, place, pieces, place_weight, piece_weight, down,
    fa, fb, whole, packed, down_o,
    keep_sem, x_send, x_recv, one_send, one_recv, two_send, two_recv, core_send, core_recv, pair_send, pair_recv,
):
    z, x, y, core = coordinates()
    tensor = lax.axis_index("tensor")
    sibling = device(z, x, y, 1 - core, tensor)
    across = device(z, 1 - x, y, core, tensor)
    partner = device(z, x, y, core, 1 - tensor)
    around_z = device(turn(z, 1), x, y, core, tensor), device(turn(z, 3), x, y, core, tensor)
    around_y = device(z, x, turn(y, 1), core, tensor), device(z, x, turn(y, 3), core, tensor)
    greet([sibling, across, partner, *around_z, *around_y])

    a_own, b_own = fa.at[z, x, y, core], fb.at[z, x, y, core]
    over = [
        send(sa, a_own, x_send.at[0], x_recv.at[0], across),
        send(sb, b_own, x_send.at[1], x_recv.at[1], across),
    ]
    pair = send(part, whole.at[tensor], pair_send.at[0], pair_recv.at[0], partner)
    expert = [send(down, down_o, pair_send.at[1], pair_recv.at[1], partner)]
    keep = [
        pltpu.make_async_copy(part, whole.at[tensor], keep_sem.at[0]),
        pltpu.make_async_copy(sa, a_own, keep_sem.at[1]),
        pltpu.make_async_copy(sb, b_own, keep_sem.at[2]),
    ]
    for copy in keep:
        copy.start()
    keep[1].wait()
    keep[2].wait()
    over[0].wait_recv()
    over[1].wait_recv()

    cores = []

    def hand_on(view):
        def arrived(place):
            block, k = view(place, pl.ds(0, 2)), len(cores)
            cores.append(send(block, block, core_send.at[k], core_recv.at[k], sibling))

        return arrived

    large = []

    def spread(kind, place):
        if kind == 0:
            view, at, around = (lambda i, h: fa.at[i, h, place, core]), z, around_z
        else:
            view, at, around = (lambda i, h: fb.at[place, h, i, core]), y, around_y
        k = len(large) // 2
        arrived = hand_on(view)
        steps = ring(view, at, *around, two_send.at[kind, k], two_recv.at[kind, k], arrived)
        large.append(steps)
        next(steps)
        arrived(at)

    small = [
        ring(
            lambda i, h: fa.at[z, h, i, core], y, *around_y, one_send.at[0], one_recv.at[0],
            lambda place: spread(0, place),
        ),
        ring(
            lambda i, h: fb.at[i, h, y, core], z, *around_z, one_send.at[1], one_recv.at[1],
            lambda place: spread(1, place),
        ),
    ]
    firsts = [next(r) for r in small]
    spread(0, y)
    spread(1, z)

    width = values.shape[1]

    @pl.loop(0, packed.shape[0] // 256)
    def _(i):
        at = pl.ds(pl.multiple_of(i * 256, 256), 256)
        main, rest = pack_rows(values, place[at], pieces[at])
        packed[at, :width] = (main * place_weight[at]).astype(BF16)
        packed[at, width:] = (rest * piece_weight[at]).astype(BF16)

    for _ in range(3):
        for r in small:
            next(r)
    for i in range(0, len(large), 2):
        for _ in range(3):
            next(large[i])
            next(large[i + 1])
    keep[0].wait()
    pair.wait_recv()
    for copy in cores + expert:
        copy.wait_recv()
    for copy in expert + [pair] + over + cores:
        copy.wait_send()
    for r in large:
        for copy in next(r):
            copy.wait_send()
    for group in firsts:
        for copy in group:
            copy.wait_send()


def gather_weights(in_shard, out_shard, part, to_pack, expert):
    owners = lax.axis_size("dp")
    (rows, a_cols), b_cols = in_shard.shape, out_shard.shape[1]
    dma = pltpu.SemaphoreType.DMA
    in_full, out_full, whole, packed, *other = pl.pallas_call(
        gather_kernel,
        out_shape=(
            jax.ShapeDtypeStruct((4, 2, 4, 2, rows, a_cols), BF16),
            jax.ShapeDtypeStruct((4, 2, 4, 2, rows, b_cols), BF16),
            jax.ShapeDtypeStruct((2,) + part.shape, BF16),
            jax.ShapeDtypeStruct((to_pack[1].shape[0], part.shape[1] * 5 // 4), BF16),
            *[jax.ShapeDtypeStruct(w.shape, BF16) for w in expert],
        ),
        in_specs=[VMEM_SPEC] * 8 + [ANY_SPEC],
        out_specs=[ANY_SPEC] * 3 + [VMEM_SPEC, ANY_SPEC],
        scratch_shapes=[
            dma((3,)),
            dma((2,)),
            dma((2,)),
            dma((2, 4)),
            dma((2, 4)),
            dma((2, 4, 4)),
            dma((2, 4, 4)),
            dma((32,)),
            dma((32,)),
            dma((4,)),
            dma((4,)),
        ],
        compiler_params=pltpu.CompilerParams(
            collective_id=2, has_side_effects=True, vmem_limit_bytes=40 * 1024 * 1024
        ),
        cost_estimate=pl.CostEstimate(flops=0, bytes_accessed=250_000_000, transcendentals=0),
    )(in_shard, out_shard, part, *to_pack, *expert)
    return (
        in_full.reshape(owners * rows, a_cols),
        out_full.reshape(owners * rows, b_cols),
        whole.reshape(-1, part.shape[1]),
        packed,
        other,
    )


ROWS_FULL, ROWS_PART, CHUNKS = 16, 4, 4


def pack_rows(values, place, part):
    tokens, width = values.shape
    step = width // CHUNKS
    main = jnp.dot(place, values[...], preferred_element_type=F32)
    rest = jnp.zeros((place.shape[0], step), F32)
    for j in range(CHUNKS):
        rest += jnp.dot(
            part[:, j * tokens : (j + 1) * tokens],
            values[:, j * step : (j + 1) * step],
            preferred_element_type=F32,
        )
    return main, rest


def pack_kernel(values, place, part, out):
    width = values.shape[1]
    main, rest = pack_rows(values, place[...], part[...])
    out[:, :width] = main.astype(BF16)
    out[:, width:] = rest.astype(BF16)


def pack(values, place, part):
    total, tokens = place.shape
    width = values.shape[1]
    block = total // 4
    return pl.pallas_call(
        pack_kernel,
        grid=(4,),
        out_shape=jax.ShapeDtypeStruct((total, width + width // CHUNKS), BF16),
        in_specs=[
            pl.BlockSpec((tokens, width), lambda g: (0, 0)),
            pl.BlockSpec((block, tokens), lambda g: (g, 0)),
            pl.BlockSpec((block, CHUNKS * tokens), lambda g: (g, 0)),
        ],
        out_specs=pl.BlockSpec((block, width + width // CHUNKS), lambda g: (g, 0)),
        cost_estimate=pl.CostEstimate(flops=1_000_000_000, bytes_accessed=8_000_000, transcendentals=0),
    )(values, place, part)


def expert_kernel(
    rows, grads, gate_m, gate_o, up_m, up_o, down_m, down_o,
    result, d_row, rows_out, grads_out, hidden, d_gate, d_up,
    gate_w, up_w, down_w,
):
    units = down_m.shape[0]

    @pl.when(pl.program_id(0) == 0)
    def _():
        gate_w[:, :units] = gate_m[...]
        gate_w[:, units:] = gate_o[...]
        up_w[:, :units] = up_m[...]
        up_w[:, units:] = up_o[...]
        down_w[:units] = down_m[...]
        down_w[units:] = down_o[...]

    block = rows.shape[0]
    width = down_w.shape[1]
    step = width // CHUNKS
    more = block // ROWS_FULL * ROWS_PART

    def picks(shape, axis, j):
        extra = lax.broadcasted_iota(jnp.int32, shape, axis)
        packed = lax.broadcasted_iota(jnp.int32, shape, 1 - axis)
        return (packed == (extra >> 2) * 16 + j * 4 + (extra & 3)).astype(F32).astype(BF16)

    def spread(src, dst):
        dst[:block] = src[:, :width]
        for j in range(CHUNKS):
            dst[block:, j * step : (j + 1) * step] = jnp.dot(
                picks((more, block), 0, j), src[:, width:], preferred_element_type=F32
            ).astype(BF16)

    def repack(dst, parts):
        rest = jnp.zeros((block, step), F32)
        for j in range(CHUNKS):
            full = parts(j).astype(BF16)
            dst[:, j * step : (j + 1) * step] = full[:block]
            rest += jnp.dot(picks((block, more), 1, j), full[block:], preferred_element_type=F32)
        dst[:, width:] = rest.astype(BF16)

    spread(rows, rows_out)
    gate = jnp.dot(rows_out[...], gate_w[...], preferred_element_type=F32)
    up = jnp.dot(rows_out[...], up_w[...], preferred_element_type=F32)
    sigma = jax.nn.sigmoid(gate)
    activated = gate * sigma
    hidden[...] = (activated * up).astype(BF16)
    spread(grads, grads_out)
    d_hidden = dot(grads_out[...], down_w[...], ((1,), (1,)))
    d_gate[...] = (d_hidden * up * (sigma * (1.0 + gate * (1.0 - sigma)))).astype(BF16)
    d_up[...] = (d_hidden * activated).astype(BF16)
    repack(
        d_row,
        lambda j: dot(d_gate[...], gate_w[j * step : (j + 1) * step], ((1,), (1,)))
        + dot(d_up[...], up_w[j * step : (j + 1) * step], ((1,), (1,))),
    )
    repack(
        result,
        lambda j: jnp.dot(hidden[...], down_w[:, j * step : (j + 1) * step], preferred_element_type=F32),
    )


def run_expert(rows, grads, gate_w, up_w, down_w):
    total, packed = rows.shape
    units, width = 2 * down_w[0].shape[0], down_w[0].shape[1]
    groups = 4
    block = total // groups
    full = block // ROWS_FULL * (ROWS_FULL + ROWS_PART)

    def whole_of(w):
        return pl.BlockSpec(w.shape, lambda g: (0, 0), pipeline_mode=pl.Buffered(1))

    def cut(rows, cols):
        return pl.BlockSpec((rows, cols), lambda g: (g, 0))

    def shape(cols):
        return jax.ShapeDtypeStruct((full * groups, cols), BF16)

    return pl.pallas_call(
        expert_kernel,
        grid=(groups,),
        out_shape=(
            jax.ShapeDtypeStruct((total, packed), BF16),
            jax.ShapeDtypeStruct((total, packed), BF16),
            shape(width),
            shape(width),
            shape(units),
            shape(units),
            shape(units),
        ),
        in_specs=[cut(block, packed)] * 2 + [whole_of(w) for w in (*gate_w, *up_w, *down_w)],
        out_specs=[cut(block, packed)] * 2 + [cut(full, width)] * 2 + [cut(full, units)] * 3,
        scratch_shapes=[
            pltpu.VMEM((width, units), BF16),
            pltpu.VMEM((width, units), BF16),
            pltpu.VMEM((units, width), BF16),
        ],
        compiler_params=pltpu.CompilerParams(vmem_limit_bytes=56 * 1024 * 1024),
        cost_estimate=pl.CostEstimate(
            flops=12 * full * groups * width * units, bytes_accessed=45_000_000, transcendentals=full * groups * units
        ),
    )(rows, grads, *gate_w, *up_w, *down_w)


def dot(left, right, contract):
    return lax.dot_general(left, right, (contract, ((), ())), preferred_element_type=F32)


def rms_scale(values):
    return lax.rsqrt(jnp.mean(values * values, axis=-1, keepdims=True) + EPS)


def norm_back(values, scale, gain, grad):
    scaled = gain * grad
    inner = jnp.mean(scaled * values, axis=-1, keepdims=True)
    d_values = scale * scaled - values * (scale * scale * scale) * inner
    axes = tuple(range(grad.ndim - 1))
    return (d_values, jnp.sum(grad * values * scale, axis=axes))


def head_columns(at):
    return pl.ds(pl.multiple_of(at * HD, HD), HD)


def head_probs(query, key):
    scores = dot(query, key, ((1,), (1,))) * HD ** (-0.5)
    shape = scores.shape
    causal = lax.broadcasted_iota(jnp.int32, shape, 0) >= lax.broadcasted_iota(jnp.int32, shape, 1)
    scores = jnp.where(causal, scores, -1e30)
    powers = jnp.exp(scores - jnp.max(scores, axis=-1, keepdims=True))
    return powers / jnp.sum(powers, axis=-1, keepdims=True)


def attend_kernel(query_heads, key_heads, raw, cosine, sine, query_gain, key_gain, query, key, value, mixed):
    group = query_heads // key_heads

    def turned(values, gain):
        values = values * rms_scale(values) * gain[...]
        return (values * cosine[...] - pltpu.roll(values, HD // 2, 1) * sine[...]).astype(BF16)

    for g in range(key_heads):
        own = head_columns(g)
        key[:, own] = turned(raw[:, head_columns(query_heads + g)], key_gain)
        value[:, own] = raw[:, head_columns(query_heads + key_heads + g)].astype(BF16)

        @pl.loop(g * group, (g + 1) * group)
        def _(h):
            at = head_columns(h)
            query[:, at] = turned(raw[:, at], query_gain)
            probs = head_probs(query[:, at], key[:, own])
            mixed[:, at] = dot(probs.astype(BF16), value[:, own], ((1,), (0,))).astype(BF16)


def attend(raw, cosine, sine, query_gain, key_gain, query_heads, key_heads):
    length = raw.shape[0]
    cols = [query_heads * HD, key_heads * HD, key_heads * HD, query_heads * HD]
    return pl.pallas_call(
        functools.partial(attend_kernel, query_heads, key_heads),
        out_shape=[jax.ShapeDtypeStruct((length, c), BF16) for c in cols],
        in_specs=[VMEM_SPEC] * 5,
        out_specs=[VMEM_SPEC] * 4,
        compiler_params=pltpu.CompilerParams(vmem_limit_bytes=48 * 1024 * 1024),
        cost_estimate=pl.CostEstimate(flops=600_000_000, bytes_accessed=6_000_000, transcendentals=1_100_000),
    )(raw, cosine, sine, query_gain[None], key_gain[None])


def attend_back_kernel(
    query_heads, key_heads, raw, cosine, sine, query_gain, key_gain, query, key, value, d_mixed,
    d_raw, gain_sums, d_key, d_value,
):
    group = query_heads // key_heads
    scale = HD ** (-0.5)

    def through_norm(values, gain, d_turned, row):
        d_out = d_turned * cosine[...] + pltpu.roll(d_turned, HD // 2, 1) * sine[...]
        norm = rms_scale(values)
        scaled = gain[...] * d_out
        inner = jnp.mean(scaled * values, axis=-1, keepdims=True)
        gain_sums[row : row + 1] += jnp.sum(d_out * values * norm, axis=0, keepdims=True)
        return (norm * scaled - values * (norm * norm * norm) * inner).astype(BF16)

    gain_sums[...] = jnp.zeros_like(gain_sums)
    for g in range(key_heads):
        own = head_columns(g)
        d_key[...] = jnp.zeros_like(d_key)
        d_value[...] = jnp.zeros_like(d_value)

        @pl.loop(g * group, (g + 1) * group)
        def _(h):
            at = head_columns(h)
            probs = head_probs(query[:, at], key[:, own])
            d_probs = dot(d_mixed[:, at], value[:, own], ((1,), (1,)))
            d_value[...] += dot(probs.astype(BF16), d_mixed[:, at], ((0,), (0,)))
            delta = jnp.sum(probs * d_probs, axis=-1, keepdims=True)
            d_scores = (probs * (d_probs - delta)).astype(BF16)
            d_key[...] += dot(d_scores, query[:, at], ((0,), (0,)))
            d_query = dot(d_scores, key[:, own], ((1,), (0,))) * scale
            d_raw[:, at] = through_norm(raw[:, at], query_gain, d_query, 0)

        at = head_columns(query_heads + g)
        d_raw[:, at] = through_norm(raw[:, at], key_gain, d_key[...] * scale, 1)
        d_raw[:, head_columns(query_heads + key_heads + g)] = d_value[...].astype(BF16)


def attend_back(raw, cosine, sine, query_gain, key_gain, query, key, value, d_mixed):
    length = raw.shape[0]
    query_heads, key_heads = query.shape[1] // HD, key.shape[1] // HD
    return pl.pallas_call(
        functools.partial(attend_back_kernel, query_heads, key_heads),
        out_shape=(
            jax.ShapeDtypeStruct(raw.shape, BF16),
            jax.ShapeDtypeStruct((8, HD), F32),
        ),
        in_specs=[VMEM_SPEC] * 9,
        out_specs=[VMEM_SPEC] * 2,
        scratch_shapes=[pltpu.VMEM((length, HD), F32), pltpu.VMEM((length, HD), F32)],
        compiler_params=pltpu.CompilerParams(vmem_limit_bytes=48 * 1024 * 1024),
        cost_estimate=pl.CostEstimate(flops=1_000_000, bytes_accessed=1_000_000, transcendentals=0),
    )(raw, cosine, sine, query_gain[None], key_gain[None], query, key, value, d_mixed)


def rope_tables(positions, head_size):
    half = head_size // 2
    freqs = jnp.exp(jnp.arange(half, dtype=F32) * (-2.0 * math.log(THETA) / head_size))
    angles = positions.astype(F32)[:, None] * freqs[None, :]
    cosine, sine = jnp.cos(angles), jnp.sin(angles)
    return jnp.concatenate([cosine, cosine], axis=1), jnp.concatenate([sine, -sine], axis=1)


def swap(values):
    return lax.ppermute(values, "tensor", [(0, 1), (1, 0)])


def share_sequence(values):
    other = swap(values)
    first = lax.axis_index("tensor") == 0
    return jnp.concatenate(
        [jnp.where(first, values, other), jnp.where(first, other, values)], axis=0
    )


def halves_of(total, rows):
    mine = lax.axis_index("tensor") * rows
    return (
        lax.dynamic_slice_in_dim(total, mine, rows, 0),
        lax.dynamic_slice_in_dim(total, rows - mine, rows, 0),
    )


def sum_sequence(total, rows):
    own, sent = halves_of(total, rows)
    return own + swap(sent.astype(BF16)).astype(F32)


def exchange(buffer):
    groups = [[dp * 2 + (dp // 8 % 2 ^ g) for dp in range(64)] for g in range(2)]
    return lax.all_to_all(
        buffer, ("dp", "tensor"), split_axis=0, concat_axis=0, tiled=True, axis_index_groups=groups
    )


def per_device(
    tokens,
    positions,
    norm_in,
    query_weight,
    key_weight,
    value_weight,
    query_gain,
    key_gain,
    out_weight,
    norm_mid,
    routed_experts,
    route_weight,
    gate_weight,
    up_weight,
    down_weight,
    out_grad,
):
    rows, width = tokens.shape
    owners = lax.axis_size("dp")
    experts = owners
    scale = HD ** (-0.5)

    inputs = tokens.astype(F32)
    in_scale = rms_scale(inputs)
    normed = (inputs * in_scale * norm_in).astype(BF16)
    gate_w, up_w, down_w = gate_weight[0], up_weight[0], down_weight[0]
    q_cols, k_cols = query_weight.shape[1], key_weight.shape[1]
    query_heads, key_heads = q_cols // HD, k_cols // HD

    names = routed_experts[:, :, None] == jnp.arange(experts, dtype=jnp.int32)
    chosen = jnp.any(names, axis=1)
    weight_of = jnp.sum(jnp.where(names, route_weight[:, :, None], 0.0), axis=1)
    below = jnp.arange(rows)[:, None] > jnp.arange(rows)[None, :]
    rank = dot(below.astype(BF16), chosen.astype(BF16), ((1,), (0,))).astype(jnp.int32)
    rank = jnp.where(chosen, rank, -1).T
    spot = jnp.arange(ROWS_FULL, dtype=jnp.int32)
    in_place = rank[:, None, :] == spot[None, :, None]
    extra = rank[:, None, :] == ROWS_FULL + (spot % ROWS_PART)[None, :, None]
    quarter = jnp.arange(CHUNKS, dtype=jnp.int32)
    in_part = extra[:, :, None, :] & (
        (spot // ROWS_PART)[None, :, None, None] == quarter[None, None, :, None]
    )
    packed_rows = experts * ROWS_FULL
    place = in_place.reshape(packed_rows, rows).astype(BF16)
    part = in_part.reshape(packed_rows, CHUNKS * rows).astype(BF16)
    weight_t = weight_of.T
    place_weight = jnp.sum(jnp.where(in_place, weight_t[:, None, :], 0.0), axis=2).reshape(packed_rows, 1)
    part_weight = jnp.sum(jnp.where(extra, weight_t[:, None, :], 0.0), axis=2).reshape(packed_rows, 1)

    def to_experts(packed):
        return exchange(packed.reshape(experts, ROWS_FULL, -1)).reshape(packed_rows, -1)

    def to_tokens(packed, place, part):
        first = dot(place, packed[:, :width], ((0,), (0,)))
        rest = dot(part, packed[:, width:], ((0,), (0,)))
        return first + rest.reshape(CHUNKS, rows, -1).transpose(1, 0, 2).reshape(rows, width)

    grad = out_grad.astype(F32)
    in_full, out_full, whole, d_rows, (down_o,) = gather_weights(
        jnp.concatenate([query_weight, key_weight, value_weight], axis=1),
        out_weight.T,
        normed,
        (out_grad, place, part, place_weight, part_weight),
        (down_w,),
    )
    d_rows, whole, gate_s = lax.optimization_barrier((d_rows, whole, gate_w))
    gate_o = swap(gate_s)
    expert_grads = to_experts(d_rows)

    cosine, sine = rope_tables(positions, HD)
    raw = dot(whole, in_full, ((1,), (0,)))
    query, key, value, mixed = attend(
        raw, cosine, sine, query_gain, key_gain, query_heads, key_heads
    )
    attended, gate_o = lax.optimization_barrier((dot(mixed, out_full, ((1,), (1,))), gate_o))
    attended = sum_sequence(attended, rows)
    hidden_in = inputs + attended
    mid_scale = rms_scale(hidden_in)
    normed_mid = (hidden_in * mid_scale * norm_mid).astype(BF16)

    send_rows = pack(normed_mid, place, part)
    send_rows, expert_grads, up_s = lax.optimization_barrier((send_rows, expert_grads, up_w))
    up_o = swap(up_s)
    result, d_row, rows_in, grads_in, hidden, d_gate, d_up = run_expert(
        to_experts(send_rows), expert_grads, (gate_w, gate_o), (up_w, up_o), (down_w, down_o)
    )
    back_rows = to_experts(d_row)
    units = down_w.shape[0]
    others = ((hidden[:, units:], grads_in), (rows_in, d_gate[:, units:]), (rows_in, d_up[:, units:]))
    sent = [dot(left, right, ((0,), (0,))).astype(BF16) for left, right in others]
    gate_came = swap(sent[1])
    *sent, rows_k, grads_k = lax.optimization_barrier((*sent, rows_in, grads_in))
    kept = [
        dot(left, right, ((0,), (0,)))
        for left, right in (
            (hidden[:, :units], grads_k), (rows_k, d_gate[:, :units]), (rows_k, d_up[:, :units])
        )
    ]

    back_rows, result, gate_came, *kept = lax.optimization_barrier((back_rows, result, gate_came, *kept))
    d_mid = to_tokens(back_rows, place, part)
    d_mid_in, grad_norm_mid = norm_back(hidden_in, mid_scale, norm_mid, d_mid)
    d_hidden_in = grad + d_mid_in
    d_attended = d_hidden_in.astype(BF16)
    d_whole = share_sequence(d_attended)
    d_mixed = dot(d_whole, out_full, ((1,), (0,))).astype(BF16)
    d_raw, gain_sums = attend_back(
        raw, cosine, sine, query_gain, key_gain, query, key, value, d_mixed
    )
    d_total = dot(d_raw, in_full, ((1,), (1,)))
    d_own, d_sent = halves_of(d_total, rows)

    returned = to_experts(result)
    in_grads = dot(whole, d_raw, ((0,), (0,))).astype(BF16)
    out_grads = dot(d_whole, mixed, ((0,), (0,))).astype(BF16)
    gain_row = jnp.pad(gain_sums[:2].reshape(1, -1), ((0, 0), (0, width - 2 * HD)))
    gains = jnp.pad(jnp.concatenate([grad_norm_mid[None], gain_row]), ((1, 5), (0, 0)))
    in_grads, returned = lax.optimization_barrier((in_grads, returned))
    in_total, out_total, gains, d_came, output, of_expert, down_came, up_came = reduce_grads(
        in_grads, out_grads, gains, d_own, d_sent.astype(BF16), inputs * in_scale,
        (returned, place, part, place_weight, part_weight, out_grad, hidden_in),
        (sent[0], sent[2]),
    )
    grad_route = jnp.sum(jnp.where(names, of_expert.T[:, None, :], 0.0), axis=2)
    d_normed = d_own + d_came.astype(F32)
    d_inputs, _ = norm_back(inputs, in_scale, norm_in, d_normed)
    grad_tokens = (d_hidden_in + d_inputs).astype(BF16)
    grad_down, grad_gate, grad_up = [
        (own + half.astype(F32))[None] for own, half in zip(kept, (down_came, gate_came, up_came))
    ]
    grad_norm_in, grad_norm_mid = gains[0], gains[1]
    grad_query_gain, grad_key_gain = gains[2, :HD], gains[2, HD : 2 * HD]
    return (
        output,
        grad_tokens,
        grad_norm_in,
        in_total[:, :q_cols],
        in_total[:, q_cols : q_cols + k_cols],
        in_total[:, q_cols + k_cols :],
        grad_query_gain,
        grad_key_gain,
        out_total.T,
        grad_norm_mid,
        grad_route,
        grad_gate,
        grad_up,
        grad_down,
    )


def solution(mesh):
    tokens_spec = P(("dp", "tensor"), None)
    columns, rows = P("dp", None, "tensor"), P("dp", "tensor", None)
    proj = P("dp", "tensor")
    return jax.shard_map(
        per_device,
        mesh=mesh,
        in_specs=(
            tokens_spec,
            P("dp"),
            P(),
            proj,
            proj,
            proj,
            P(),
            P(),
            P("tensor", "dp"),
            P(),
            tokens_spec,
            tokens_spec,
            columns,
            columns,
            rows,
            tokens_spec,
        ),
        out_specs=(
            tokens_spec,
            tokens_spec,
            P(),
            proj,
            proj,
            proj,
            P(),
            P(),
            P("tensor", "dp"),
            P(),
            tokens_spec,
            columns,
            columns,
            rows,
        ),
        check_vma=False,
    )
```

```python
import functools
import math

import jax
import jax.numpy as jnp
from jax import lax
from jax.experimental import pallas as pl
from jax.experimental.pallas import tpu as pltpu
from jax.sharding import PartitionSpec as P

HD = 128
TOP = 8
EPS = 1e-06
THETA = 1000000.0
BF16 = jnp.bfloat16
F32 = jnp.float32
MESH_ID = pl.DeviceIdType.MESH
ANY_SPEC = pl.BlockSpec(memory_space=pl.ANY)
VMEM_SPEC = pl.BlockSpec(memory_space=pltpu.VMEM)


def coordinates():
    dp = lax.axis_index("dp")
    return lax.div(dp, 16), lax.rem(lax.div(dp, 8), 2), lax.rem(lax.div(dp, 2), 4), lax.rem(dp, 2)


def device(z, x, y, core, tensor):
    return (((z * 2 + x) * 4 + y) * 2 + core, tensor)


def turn(at, step):
    return lax.rem(at + step, 4)


def send(src, dst, send_sem, recv_sem, to):
    copy = pltpu.make_async_remote_copy(
        src_ref=src,
        dst_ref=dst,
        send_sem=send_sem,
        recv_sem=recv_sem,
        device_id=to,
        device_id_type=MESH_ID,
    )
    copy.start()
    return copy


def greet(peers):
    barrier = pltpu.get_barrier_semaphore()
    for peer in peers:
        pl.semaphore_signal(barrier, inc=1, device_id=peer, device_id_type=MESH_ID)
    pl.semaphore_wait(barrier, len(peers))


STEPS = (1, 3, 2)


def combine_rows(weights, values):
    high = weights.astype(BF16)
    low = (weights - high.astype(F32)).astype(BF16)
    return dot(high, values, ((0,), (0,))) + dot(low, values, ((0,), (0,)))


def output_rows(at, returned, place, part, place_weight, part_weight, grad, total):
    tokens, width = grad.shape
    step = width // CHUNKS
    main, rest, picked = returned[at, :width], returned[at, width:], place[at].astype(F32)
    total[...] += combine_rows(picked * place_weight[at], main)
    products = dot(main, grad[...], ((1,), (1,))) * picked
    for j in range(CHUNKS):
        picked = part[at, j * tokens : (j + 1) * tokens].astype(F32)
        columns = slice(j * step, (j + 1) * step)
        total[:, columns] += combine_rows(picked * part_weight[at], rest)
        products += dot(rest, grad[:, columns], ((1,), (1,))) * picked
    return jnp.sum(products.reshape(-1, ROWS_FULL, tokens), axis=1)


def reduce_kernel(
    ga, gb, gain, d_own, d_sent, x_hat,
    returned, place, part, place_weight, part_weight, grad, base, down, gate,
    oa, ob, og, d_came, output, of_expert, down_c, gate_c,
    own_a, got_a, one_a, via_a, two_a, sum_a, three_a,
    own_b, got_b, one_b, via_b, two_b, sum_b, three_b,
    vec, vecs,
    load_sem, core_send, core_recv, one_send, one_recv, two_send, two_recv,
    three_send, three_recv, vec_send, vec_recv, pair_send, pair_recv, total,
):
    z, x, y, core = coordinates()
    tensor = lax.axis_index("tensor")
    sibling = device(z, x, y, 1 - core, tensor)
    along_z = [device(turn(z, s), x, y, core, tensor) for s in STEPS]
    along_y = [device(z, x, turn(y, s), core, tensor) for s in STEPS]
    across = device(z, 1 - x, y, core, tensor)
    near = [
        device(z, x, y, 1 - core, tensor),
        device(z, x, y, core, 1 - tensor),
        device(z, x, y, 1 - core, 1 - tensor),
    ]
    greet(along_z + along_y + [across] + near)

    vec_groups = (
        (near, core * 2 + tensor, 4),
        (along_z, z, 4),
        (along_y, y, 4),
        ([across], x, 2),
    )
    vec_copies = {}

    def vec_start(stage):
        peers, mine, _ = vec_groups[stage]
        if stage == 0:
            vec[0] = gain[...]
            vec[0, 0:1] = jnp.sum(
                (d_own[...] + d_came[...].astype(F32)) * x_hat[...], axis=0, keepdims=True
            )
        vecs[stage, mine] = vec[stage]
        vec_copies[stage] = [
            send(vec.at[stage], vecs.at[stage, mine], vec_send.at[stage, i], vec_recv.at[stage, i], peer)
            for i, peer in enumerate(peers)
        ]

    def vec_finish(stage):
        for copy in vec_copies[stage]:
            copy.wait()
        count = vec_groups[stage][2]
        added = vecs[stage, 0]
        for i in range(1, count):
            added = added + vecs[stage, i]
        if stage == 3:
            og[...] = added
        else:
            vec[stage + 1] = added

    partner = near[1]
    d_copy = send(d_sent, d_came, pair_send.at[0], pair_recv.at[0], partner)

    loads, swaps = {}, {}
    order = (2, 1, 3, 0)
    for i, s in enumerate(order):
        to = turn(z, s)
        swaps["a", s] = send(ga.at[to, :, :, 1 - core], got_a.at[to], core_send.at[0, i], core_recv.at[0, i], sibling)
        loads["a", s] = pltpu.make_async_copy(ga.at[to, :, :, core], own_a.at[to], load_sem.at[0, i])
        loads["a", s].start()
        to = turn(y, s)
        swaps["b", s] = send(gb.at[:, :, to, 1 - core], got_b.at[to], core_send.at[1, i], core_recv.at[1, i], sibling)
        loads["b", s] = pltpu.make_async_copy(gb.at[:, :, to, core], own_b.at[to], load_sem.at[1, i])
        loads["b", s].start()

    def add_cores(own, got, to):
        shape = own.shape

        @pl.loop(0, shape[1])
        def _(i):
            @pl.loop(0, shape[2])
            def _(j):
                own[to, i, j] += got[to, i, j]

    def round_ring(own, got, via, one, at, up, down, name, row):
        n = own.shape[1] // 2
        halves = pl.ds(0, n), pl.ds(n, n)
        above, far, below = turn(at, 1), turn(at, 2), turn(at, 3)

        def step(src, dst, i, to):
            return send(src, dst, one_send.at[row, i], one_recv.at[row, i], to)

        def ready(s):
            loads[name, s].wait()
            swaps[name, s].wait_recv()
            add_cores(own, got, turn(at, s))

        def pass_on(k, to):
            first = k * n

            @pl.loop(0, n)
            def _(i):
                @pl.loop(0, own.shape[2])
                def _(j):
                    own[to, first + i, j] += via[k, i, j]

        ready(2)
        copies = [step(own.at[far, halves[0]], via.at[0], 0, up), step(own.at[far, halves[1]], via.at[1], 1, down)]
        yield copies
        ready(1)
        copies.append(step(own.at[above, halves[1]], one.at[0, halves[1]], 2, up))
        yield
        ready(3)
        copies.append(step(own.at[below, halves[0]], one.at[1, halves[0]], 3, down))
        yield
        copies[0].wait_recv()
        pass_on(0, above)
        copies.append(step(own.at[above, halves[0]], one.at[0, halves[0]], 4, up))
        yield
        copies[1].wait_recv()
        pass_on(1, below)
        copies.append(step(own.at[below, halves[1]], one.at[1, halves[1]], 5, down))
        yield
        ready(0)
        yield

    rings = [
        round_ring(own_a, got_a, via_a, one_a, z, along_z[0], along_z[1], "a", 0),
        round_ring(own_b, got_b, via_b, one_b, y, along_y[0], along_y[1], "b", 1),
    ]
    firsts = [next(r) for r in rings]
    expert = [send(down, down_c, pair_send.at[1], pair_recv.at[1], partner)]
    for i in range(5):
        for r in rings:
            next(r)
        if i == 1:
            d_copy.wait_recv()
            vec_start(0)
            expert.append(send(gate, gate_c, pair_send.at[2], pair_recv.at[2], partner))
            total[...] = base[...]

            @pl.loop(0, returned.shape[0] // 256)
            def _(i):
                rows = pl.ds(pl.multiple_of(i * 256, 256), 256)
                experts = pl.ds(pl.multiple_of(i * 16, 16), 16)
                of_expert[experts] = output_rows(
                    rows, returned, place, part, place_weight, part_weight, grad, total
                )

            output[...] = total[...].astype(BF16)
    ones = firsts[0] + firsts[1]
    vec_finish(0)
    vec_start(1)

    for copy in firsts[0][2:] + firsts[1][2:]:
        copy.wait_recv()
    vec_finish(1)
    vec_start(2)
    twos = []
    for i, s in enumerate(STEPS + (0,)):
        to = turn(y, s)
        for k in range(2):
            sum_a[to, k] = (
                own_a[z, k, to].astype(F32) + one_a[0, k, to].astype(F32) + one_a[1, k, to].astype(F32)
            ).astype(BF16)
        if s:
            twos.append(send(sum_a.at[to], two_a.at[i], two_send.at[0, i], two_recv.at[0, i], along_y[i]))
        to = turn(z, s)
        for k in range(2):
            sum_b[to, k] = (
                own_b[y, to, k].astype(F32) + one_b[0, to, k].astype(F32) + one_b[1, to, k].astype(F32)
            ).astype(BF16)
        if s:
            twos.append(send(sum_b.at[to], two_b.at[i], two_send.at[1, i], two_recv.at[1, i], along_z[i]))

    for copy in twos:
        copy.wait_recv()
    vec_finish(2)
    vec_start(3)

    def last(sums, two, at, k):
        return (
            sums[at, k].astype(F32) + two[0, k].astype(F32) + two[1, k].astype(F32) + two[2, k].astype(F32)
        )

    three_a[0] = last(sum_a, two_a, y, 1 - x).astype(BF16)
    final_a = send(three_a.at[0], three_a.at[1], three_send.at[0], three_recv.at[0], across)
    three_b[0] = last(sum_b, two_b, z, 1 - x).astype(BF16)
    final_b = send(three_b.at[0], three_b.at[1], three_send.at[1], three_recv.at[1], across)
    mine_a = last(sum_a, two_a, y, x)
    final_a.wait_recv()
    oa[...] = mine_a + three_a[1].astype(F32)
    mine_b = last(sum_b, two_b, z, x)
    final_b.wait_recv()
    ob[...] = mine_b + three_b[1].astype(F32)
    vec_finish(3)
    for copy in expert:
        copy.wait_recv()
    for copy in list(swaps.values()) + ones + twos + [final_a, final_b, d_copy] + expert:
        copy.wait_send()


def reduce_grads(in_grads, out_grads, gains, d_own, d_sent, x_hat, routed, expert):
    owners = lax.axis_size("dp")
    rows = in_grads.shape[0] // owners
    a_cols, b_cols = in_grads.shape[1], out_grads.shape[1]
    dma = pltpu.SemaphoreType.DMA
    vmem = pltpu.VMEM

    def scratch(cols, inner):
        return [
            vmem((4,) + inner + (rows, cols), BF16),
            vmem((4,) + inner + (rows, cols), BF16),
            vmem((2,) + inner + (rows, cols), BF16),
            vmem((2, inner[0] // 2, inner[1], rows, cols), BF16),
            vmem((3, 2, rows, cols), BF16),
            vmem((4, 2, rows, cols), BF16),
            vmem((2, rows, cols), BF16),
        ]

    return pl.pallas_call(
        reduce_kernel,
        out_shape=(
            jax.ShapeDtypeStruct((rows, a_cols), F32),
            jax.ShapeDtypeStruct((rows, b_cols), F32),
            jax.ShapeDtypeStruct(gains.shape, F32),
            jax.ShapeDtypeStruct(d_sent.shape, BF16),
            jax.ShapeDtypeStruct(d_sent.shape, BF16),
            jax.ShapeDtypeStruct((owners, d_sent.shape[0]), F32),
            *[jax.ShapeDtypeStruct(half.shape, BF16) for half in expert],
        ),
        in_specs=[ANY_SPEC] * 2 + [VMEM_SPEC] * 11 + [ANY_SPEC] * 2,
        out_specs=[VMEM_SPEC] * 6 + [ANY_SPEC] * 2,
        scratch_shapes=scratch(a_cols, (2, 4))
        + scratch(b_cols, (4, 2))
        + [
            vmem((4,) + gains.shape, F32),
            vmem((4, 4) + gains.shape, F32),
            dma((2, 4)),
            dma((2, 4)),
            dma((2, 4)),
            dma((2, 6)),
            dma((2, 6)),
            dma((2, 3)),
            dma((2, 3)),
            dma((2,)),
            dma((2,)),
            dma((4, 3)),
            dma((4, 3)),
            dma((3,)),
            dma((3,)),
            vmem(d_sent.shape, F32),
        ],
        compiler_params=pltpu.CompilerParams(
            collective_id=1, has_side_effects=True, vmem_limit_bytes=56 * 1024 * 1024
        ),
        cost_estimate=pl.CostEstimate(flops=10_000_000, bytes_accessed=300_000_000, transcendentals=0),
    )(
        in_grads.reshape(4, 2, 4, 2, rows, a_cols),
        out_grads.reshape(4, 2, 4, 2, rows, b_cols),
        gains,
        d_own,
        d_sent,
        x_hat,
        *routed,
        *expert,
    )


def ring(view, at, up, down, sends, recvs, arrived):
    both = pl.ds(0, 2)

    def start(place, half, i, to):
        block = view(place, half)
        return send(block, block, sends.at[i], recvs.at[i], to)

    copies = [start(at, both, 0, up), start(at, both, 1, down)]
    yield copies
    copies[0].wait_recv()
    copies.append(start(turn(at, 3), 0, 2, up))
    arrived(turn(at, 3))
    yield
    copies[1].wait_recv()
    copies.append(start(turn(at, 1), 1, 3, down))
    arrived(turn(at, 1))
    yield
    copies[2].wait_recv()
    copies[3].wait_recv()
    arrived(turn(at, 2))
    yield
    yield copies


def gather_kernel(
    sa, sb, part, values, place, pieces, place_weight, piece_weight, down,
    fa, fb, whole, packed, down_o,
    keep_sem, x_send, x_recv, one_send, one_recv, two_send, two_recv, core_send, core_recv, pair_send, pair_recv,
):
    z, x, y, core = coordinates()
    tensor = lax.axis_index("tensor")
    sibling = device(z, x, y, 1 - core, tensor)
    across = device(z, 1 - x, y, core, tensor)
    partner = device(z, x, y, core, 1 - tensor)
    around_z = device(turn(z, 1), x, y, core, tensor), device(turn(z, 3), x, y, core, tensor)
    around_y = device(z, x, turn(y, 1), core, tensor), device(z, x, turn(y, 3), core, tensor)
    greet([sibling, across, partner, *around_z, *around_y])

    a_own, b_own = fa.at[z, x, y, core], fb.at[z, x, y, core]
    over = [
        send(sa, a_own, x_send.at[0], x_recv.at[0], across),
        send(sb, b_own, x_send.at[1], x_recv.at[1], across),
    ]
    pair = send(part, whole.at[tensor], pair_send.at[0], pair_recv.at[0], partner)
    expert = [send(down, down_o, pair_send.at[1], pair_recv.at[1], partner)]
    keep = [
        pltpu.make_async_copy(part, whole.at[tensor], keep_sem.at[0]),
        pltpu.make_async_copy(sa, a_own, keep_sem.at[1]),
        pltpu.make_async_copy(sb, b_own, keep_sem.at[2]),
    ]
    for copy in keep:
        copy.start()
    keep[1].wait()
    keep[2].wait()
    over[0].wait_recv()
    over[1].wait_recv()

    cores = []

    def hand_on(view):
        def arrived(place):
            block, k = view(place, pl.ds(0, 2)), len(cores)
            cores.append(send(block, block, core_send.at[k], core_recv.at[k], sibling))

        return arrived

    large = []

    def spread(kind, place):
        if kind == 0:
            view, at, around = (lambda i, h: fa.at[i, h, place, core]), z, around_z
        else:
            view, at, around = (lambda i, h: fb.at[place, h, i, core]), y, around_y
        k = len(large) // 2
        arrived = hand_on(view)
        steps = ring(view, at, *around, two_send.at[kind, k], two_recv.at[kind, k], arrived)
        large.append(steps)
        next(steps)
        arrived(at)

    small = [
        ring(
            lambda i, h: fa.at[z, h, i, core], y, *around_y, one_send.at[0], one_recv.at[0],
            lambda place: spread(0, place),
        ),
        ring(
            lambda i, h: fb.at[i, h, y, core], z, *around_z, one_send.at[1], one_recv.at[1],
            lambda place: spread(1, place),
        ),
    ]
    firsts = [next(r) for r in small]
    spread(0, y)
    spread(1, z)

    width = values.shape[1]

    @pl.loop(0, packed.shape[0] // 256)
    def _(i):
        at = pl.ds(pl.multiple_of(i * 256, 256), 256)
        main, rest = pack_rows(values, place[at], pieces[at])
        packed[at, :width] = (main * place_weight[at]).astype(BF16)
        packed[at, width:] = (rest * piece_weight[at]).astype(BF16)

    for _ in range(3):
        for r in small:
            next(r)
    for i in range(0, len(large), 2):
        for _ in range(3):
            next(large[i])
            next(large[i + 1])
    keep[0].wait()
    pair.wait_recv()
    for copy in cores + expert:
        copy.wait_recv()
    for copy in expert + [pair] + over + cores:
        copy.wait_send()
    for r in large:
        for copy in next(r):
            copy.wait_send()
    for group in firsts:
        for copy in group:
            copy.wait_send()


def gather_weights(in_shard, out_shard, part, to_pack, expert):
    owners = lax.axis_size("dp")
    (rows, a_cols), b_cols = in_shard.shape, out_shard.shape[1]
    dma = pltpu.SemaphoreType.DMA
    in_full, out_full, whole, packed, *other = pl.pallas_call(
        gather_kernel,
        out_shape=(
            jax.ShapeDtypeStruct((4, 2, 4, 2, rows, a_cols), BF16),
            jax.ShapeDtypeStruct((4, 2, 4, 2, rows, b_cols), BF16),
            jax.ShapeDtypeStruct((2,) + part.shape, BF16),
            jax.ShapeDtypeStruct((to_pack[1].shape[0], part.shape[1] * 5 // 4), BF16),
            *[jax.ShapeDtypeStruct(w.shape, BF16) for w in expert],
        ),
        in_specs=[VMEM_SPEC] * 8 + [ANY_SPEC],
        out_specs=[ANY_SPEC] * 3 + [VMEM_SPEC, ANY_SPEC],
        scratch_shapes=[
            dma((3,)),
            dma((2,)),
            dma((2,)),
            dma((2, 4)),
            dma((2, 4)),
            dma((2, 4, 4)),
            dma((2, 4, 4)),
            dma((32,)),
            dma((32,)),
            dma((4,)),
            dma((4,)),
        ],
        compiler_params=pltpu.CompilerParams(
            collective_id=2, has_side_effects=True, vmem_limit_bytes=40 * 1024 * 1024
        ),
        cost_estimate=pl.CostEstimate(flops=0, bytes_accessed=250_000_000, transcendentals=0),
    )(in_shard, out_shard, part, *to_pack, *expert)
    return (
        in_full.reshape(owners * rows, a_cols),
        out_full.reshape(owners * rows, b_cols),
        whole.reshape(-1, part.shape[1]),
        packed,
        other,
    )


ROWS_FULL, ROWS_PART, CHUNKS = 16, 4, 4


def pack_rows(values, place, part):
    tokens, width = values.shape
    step = width // CHUNKS
    main = jnp.dot(place, values[...], preferred_element_type=F32)
    rest = jnp.zeros((place.shape[0], step), F32)
    for j in range(CHUNKS):
        rest += jnp.dot(
            part[:, j * tokens : (j + 1) * tokens],
            values[:, j * step : (j + 1) * step],
            preferred_element_type=F32,
        )
    return main, rest


def pack_kernel(values, place, part, out):
    width = values.shape[1]
    main, rest = pack_rows(values, place[...], part[...])
    out[:, :width] = main.astype(BF16)
    out[:, width:] = rest.astype(BF16)


def pack(values, place, part):
    total, tokens = place.shape
    width = values.shape[1]
    block = total // 4
    return pl.pallas_call(
        pack_kernel,
        grid=(4,),
        out_shape=jax.ShapeDtypeStruct((total, width + width // CHUNKS), BF16),
        in_specs=[
            pl.BlockSpec((tokens, width), lambda g: (0, 0)),
            pl.BlockSpec((block, tokens), lambda g: (g, 0)),
            pl.BlockSpec((block, CHUNKS * tokens), lambda g: (g, 0)),
        ],
        out_specs=pl.BlockSpec((block, width + width // CHUNKS), lambda g: (g, 0)),
        cost_estimate=pl.CostEstimate(flops=1_000_000_000, bytes_accessed=8_000_000, transcendentals=0),
    )(values, place, part)


def expert_kernel(
    rows, grads, gate_m, gate_o, up_m, up_o, down_m, down_o,
    result, d_row, rows_out, grads_out, hidden, d_gate, d_up,
    gate_w, up_w, down_w,
):
    units = down_m.shape[0]

    @pl.when(pl.program_id(0) == 0)
    def _():
        gate_w[:, :units] = gate_m[...]
        gate_w[:, units:] = gate_o[...]
        up_w[:, :units] = up_m[...]
        up_w[:, units:] = up_o[...]
        down_w[:units] = down_m[...]
        down_w[units:] = down_o[...]

    block = rows.shape[0]
    width = down_w.shape[1]
    step = width // CHUNKS
    more = block // ROWS_FULL * ROWS_PART

    def picks(shape, axis, j):
        extra = lax.broadcasted_iota(jnp.int32, shape, axis)
        packed = lax.broadcasted_iota(jnp.int32, shape, 1 - axis)
        return (packed == (extra >> 2) * 16 + j * 4 + (extra & 3)).astype(F32).astype(BF16)

    def spread(src, dst):
        dst[:block] = src[:, :width]
        for j in range(CHUNKS):
            dst[block:, j * step : (j + 1) * step] = jnp.dot(
                picks((more, block), 0, j), src[:, width:], preferred_element_type=F32
            ).astype(BF16)

    def repack(dst, parts):
        rest = jnp.zeros((block, step), F32)
        for j in range(CHUNKS):
            full = parts(j).astype(BF16)
            dst[:, j * step : (j + 1) * step] = full[:block]
            rest += jnp.dot(picks((block, more), 1, j), full[block:], preferred_element_type=F32)
        dst[:, width:] = rest.astype(BF16)

    spread(rows, rows_out)
    gate = jnp.dot(rows_out[...], gate_w[...], preferred_element_type=F32)
    up = jnp.dot(rows_out[...], up_w[...], preferred_element_type=F32)
    sigma = jax.nn.sigmoid(gate)
    activated = gate * sigma
    hidden[...] = (activated * up).astype(BF16)
    spread(grads, grads_out)
    d_hidden = dot(grads_out[...], down_w[...], ((1,), (1,)))
    d_gate[...] = (d_hidden * up * (sigma * (1.0 + gate * (1.0 - sigma)))).astype(BF16)
    d_up[...] = (d_hidden * activated).astype(BF16)
    repack(
        d_row,
        lambda j: dot(d_gate[...], gate_w[j * step : (j + 1) * step], ((1,), (1,)))
        + dot(d_up[...], up_w[j * step : (j + 1) * step], ((1,), (1,))),
    )
    repack(
        result,
        lambda j: jnp.dot(hidden[...], down_w[:, j * step : (j + 1) * step], preferred_element_type=F32),
    )


def run_expert(rows, grads, gate_w, up_w, down_w):
    total, packed = rows.shape
    units, width = 2 * down_w[0].shape[0], down_w[0].shape[1]
    groups = 4
    block = total // groups
    full = block // ROWS_FULL * (ROWS_FULL + ROWS_PART)

    def whole_of(w):
        return pl.BlockSpec(w.shape, lambda g: (0, 0), pipeline_mode=pl.Buffered(1))

    def cut(rows, cols):
        return pl.BlockSpec((rows, cols), lambda g: (g, 0))

    def shape(cols):
        return jax.ShapeDtypeStruct((full * groups, cols), BF16)

    return pl.pallas_call(
        expert_kernel,
        grid=(groups,),
        out_shape=(
            jax.ShapeDtypeStruct((total, packed), BF16),
            jax.ShapeDtypeStruct((total, packed), BF16),
            shape(width),
            shape(width),
            shape(units),
            shape(units),
            shape(units),
        ),
        in_specs=[cut(block, packed)] * 2 + [whole_of(w) for w in (*gate_w, *up_w, *down_w)],
        out_specs=[cut(block, packed)] * 2 + [cut(full, width)] * 2 + [cut(full, units)] * 3,
        scratch_shapes=[
            pltpu.VMEM((width, units), BF16),
            pltpu.VMEM((width, units), BF16),
            pltpu.VMEM((units, width), BF16),
        ],
        compiler_params=pltpu.CompilerParams(vmem_limit_bytes=56 * 1024 * 1024),
        cost_estimate=pl.CostEstimate(
            flops=12 * full * groups * width * units, bytes_accessed=45_000_000, transcendentals=full * groups * units
        ),
    )(rows, grads, *gate_w, *up_w, *down_w)


def dot(left, right, contract):
    return lax.dot_general(left, right, (contract, ((), ())), preferred_element_type=F32)


def rms_scale(values):
    return lax.rsqrt(jnp.mean(values * values, axis=-1, keepdims=True) + EPS)


def norm_back(values, scale, gain, grad):
    scaled = gain * grad
    inner = jnp.mean(scaled * values, axis=-1, keepdims=True)
    d_values = scale * scaled - values * (scale * scale * scale) * inner
    axes = tuple(range(grad.ndim - 1))
    return (d_values, jnp.sum(grad * values * scale, axis=axes))


def head_columns(at):
    return pl.ds(pl.multiple_of(at * HD, HD), HD)


def head_probs(query, key):
    scores = dot(query, key, ((1,), (1,))) * HD ** (-0.5)
    shape = scores.shape
    causal = lax.broadcasted_iota(jnp.int32, shape, 0) >= lax.broadcasted_iota(jnp.int32, shape, 1)
    scores = jnp.where(causal, scores, -1e30)
    powers = jnp.exp(scores - jnp.max(scores, axis=-1, keepdims=True))
    return powers / jnp.sum(powers, axis=-1, keepdims=True)


def attend_kernel(query_heads, key_heads, raw, cosine, sine, query_gain, key_gain, query, key, value, mixed):
    group = query_heads // key_heads

    def turned(values, gain):
        values = values * rms_scale(values) * gain[...]
        return (values * cosine[...] - pltpu.roll(values, HD // 2, 1) * sine[...]).astype(BF16)

    for g in range(key_heads):
        own = head_columns(g)
        key[:, own] = turned(raw[:, head_columns(query_heads + g)], key_gain)
        value[:, own] = raw[:, head_columns(query_heads + key_heads + g)].astype(BF16)

        @pl.loop(g * group, (g + 1) * group)
        def _(h):
            at = head_columns(h)
            query[:, at] = turned(raw[:, at], query_gain)
            probs = head_probs(query[:, at], key[:, own])
            mixed[:, at] = dot(probs.astype(BF16), value[:, own], ((1,), (0,))).astype(BF16)


def attend(raw, cosine, sine, query_gain, key_gain, query_heads, key_heads):
    length = raw.shape[0]
    cols = [query_heads * HD, key_heads * HD, key_heads * HD, query_heads * HD]
    return pl.pallas_call(
        functools.partial(attend_kernel, query_heads, key_heads),
        out_shape=[jax.ShapeDtypeStruct((length, c), BF16) for c in cols],
        in_specs=[VMEM_SPEC] * 5,
        out_specs=[VMEM_SPEC] * 4,
        compiler_params=pltpu.CompilerParams(vmem_limit_bytes=48 * 1024 * 1024),
        cost_estimate=pl.CostEstimate(flops=600_000_000, bytes_accessed=6_000_000, transcendentals=1_100_000),
    )(raw, cosine, sine, query_gain[None], key_gain[None])


def attend_back_kernel(
    query_heads, key_heads, raw, cosine, sine, query_gain, key_gain, query, key, value, d_mixed,
    d_raw, gain_sums, d_key, d_value,
):
    group = query_heads // key_heads
    scale = HD ** (-0.5)

    def through_norm(values, gain, d_turned, row):
        d_out = d_turned * cosine[...] + pltpu.roll(d_turned, HD // 2, 1) * sine[...]
        norm = rms_scale(values)
        scaled = gain[...] * d_out
        inner = jnp.mean(scaled * values, axis=-1, keepdims=True)
        gain_sums[row : row + 1] += jnp.sum(d_out * values * norm, axis=0, keepdims=True)
        return (norm * scaled - values * (norm * norm * norm) * inner).astype(BF16)

    gain_sums[...] = jnp.zeros_like(gain_sums)
    for g in range(key_heads):
        own = head_columns(g)
        d_key[...] = jnp.zeros_like(d_key)
        d_value[...] = jnp.zeros_like(d_value)

        @pl.loop(g * group, (g + 1) * group)
        def _(h):
            at = head_columns(h)
            probs = head_probs(query[:, at], key[:, own])
            d_probs = dot(d_mixed[:, at], value[:, own], ((1,), (1,)))
            d_value[...] += dot(probs.astype(BF16), d_mixed[:, at], ((0,), (0,)))
            delta = jnp.sum(probs * d_probs, axis=-1, keepdims=True)
            d_scores = (probs * (d_probs - delta)).astype(BF16)
            d_key[...] += dot(d_scores, query[:, at], ((0,), (0,)))
            d_query = dot(d_scores, key[:, own], ((1,), (0,))) * scale
            d_raw[:, at] = through_norm(raw[:, at], query_gain, d_query, 0)

        at = head_columns(query_heads + g)
        d_raw[:, at] = through_norm(raw[:, at], key_gain, d_key[...] * scale, 1)
        d_raw[:, head_columns(query_heads + key_heads + g)] = d_value[...].astype(BF16)


def attend_back(raw, cosine, sine, query_gain, key_gain, query, key, value, d_mixed):
    length = raw.shape[0]
    query_heads, key_heads = query.shape[1] // HD, key.shape[1] // HD
    return pl.pallas_call(
        functools.partial(attend_back_kernel, query_heads, key_heads),
        out_shape=(
            jax.ShapeDtypeStruct(raw.shape, BF16),
            jax.ShapeDtypeStruct((8, HD), F32),
        ),
        in_specs=[VMEM_SPEC] * 9,
        out_specs=[VMEM_SPEC] * 2,
        scratch_shapes=[pltpu.VMEM((length, HD), F32), pltpu.VMEM((length, HD), F32)],
        compiler_params=pltpu.CompilerParams(vmem_limit_bytes=48 * 1024 * 1024),
        cost_estimate=pl.CostEstimate(flops=1_000_000, bytes_accessed=1_000_000, transcendentals=0),
    )(raw, cosine, sine, query_gain[None], key_gain[None], query, key, value, d_mixed)


def rope_tables(positions, head_size):
    half = head_size // 2
    freqs = jnp.exp(jnp.arange(half, dtype=F32) * (-2.0 * math.log(THETA) / head_size))
    angles = positions.astype(F32)[:, None] * freqs[None, :]
    cosine, sine = jnp.cos(angles), jnp.sin(angles)
    return jnp.concatenate([cosine, cosine], axis=1), jnp.concatenate([sine, -sine], axis=1)


def swap(values):
    return lax.ppermute(values, "tensor", [(0, 1), (1, 0)])


def share_sequence(values):
    other = swap(values)
    first = lax.axis_index("tensor") == 0
    return jnp.concatenate(
        [jnp.where(first, values, other), jnp.where(first, other, values)], axis=0
    )


def halves_of(total, rows):
    mine = lax.axis_index("tensor") * rows
    return (
        lax.dynamic_slice_in_dim(total, mine, rows, 0),
        lax.dynamic_slice_in_dim(total, rows - mine, rows, 0),
    )


def sum_sequence(total, rows):
    own, sent = halves_of(total, rows)
    return own + swap(sent.astype(BF16)).astype(F32)


def exchange(buffer):
    groups = [[dp * 2 + (dp // 8 % 2 ^ g) for dp in range(64)] for g in range(2)]
    return lax.all_to_all(
        buffer, ("dp", "tensor"), split_axis=0, concat_axis=0, tiled=True, axis_index_groups=groups
    )


def per_device(
    tokens,
    positions,
    norm_in,
    query_weight,
    key_weight,
    value_weight,
    query_gain,
    key_gain,
    out_weight,
    norm_mid,
    routed_experts,
    route_weight,
    gate_weight,
    up_weight,
    down_weight,
    out_grad,
):
    rows, width = tokens.shape
    owners = lax.axis_size("dp")
    experts = owners
    scale = HD ** (-0.5)

    inputs = tokens.astype(F32)
    in_scale = rms_scale(inputs)
    normed = (inputs * in_scale * norm_in).astype(BF16)
    gate_w, up_w, down_w = gate_weight[0], up_weight[0], down_weight[0]
    q_cols, k_cols = query_weight.shape[1], key_weight.shape[1]
    query_heads, key_heads = q_cols // HD, k_cols // HD

    names = routed_experts[:, :, None] == jnp.arange(experts, dtype=jnp.int32)
    chosen = jnp.any(names, axis=1)
    weight_of = jnp.sum(jnp.where(names, route_weight[:, :, None], 0.0), axis=1)
    below = jnp.arange(rows)[:, None] > jnp.arange(rows)[None, :]
    rank = dot(below.astype(BF16), chosen.astype(BF16), ((1,), (0,))).astype(jnp.int32)
    rank = jnp.where(chosen, rank, -1).T
    spot = jnp.arange(ROWS_FULL, dtype=jnp.int32)
    in_place = rank[:, None, :] == spot[None, :, None]
    extra = rank[:, None, :] == ROWS_FULL + (spot % ROWS_PART)[None, :, None]
    quarter = jnp.arange(CHUNKS, dtype=jnp.int32)
    in_part = extra[:, :, None, :] & (
        (spot // ROWS_PART)[None, :, None, None] == quarter[None, None, :, None]
    )
    packed_rows = experts * ROWS_FULL
    place = in_place.reshape(packed_rows, rows).astype(BF16)
    part = in_part.reshape(packed_rows, CHUNKS * rows).astype(BF16)
    weight_t = weight_of.T
    place_weight = jnp.sum(jnp.where(in_place, weight_t[:, None, :], 0.0), axis=2).reshape(packed_rows, 1)
    part_weight = jnp.sum(jnp.where(extra, weight_t[:, None, :], 0.0), axis=2).reshape(packed_rows, 1)

    def to_experts(packed):
        return exchange(packed.reshape(experts, ROWS_FULL, -1)).reshape(packed_rows, -1)

    def to_tokens(packed, place, part):
        first = dot(place, packed[:, :width], ((0,), (0,)))
        rest = dot(part, packed[:, width:], ((0,), (0,)))
        return first + rest.reshape(CHUNKS, rows, -1).transpose(1, 0, 2).reshape(rows, width)

    grad = out_grad.astype(F32)
    in_full, out_full, whole, d_rows, (down_o,) = gather_weights(
        jnp.concatenate([query_weight, key_weight, value_weight], axis=1),
        out_weight.T,
        normed,
        (out_grad, place, part, place_weight, part_weight),
        (down_w,),
    )
    d_rows, whole, gate_s = lax.optimization_barrier((d_rows, whole, gate_w))
    gate_o = swap(gate_s)
    expert_grads = to_experts(d_rows)

    cosine, sine = rope_tables(positions, HD)
    raw = dot(whole, in_full, ((1,), (0,)))
    query, key, value, mixed = attend(
        raw, cosine, sine, query_gain, key_gain, query_heads, key_heads
    )
    attended, gate_o = lax.optimization_barrier((dot(mixed, out_full, ((1,), (1,))), gate_o))
    attended = sum_sequence(attended, rows)
    hidden_in = inputs + attended
    mid_scale = rms_scale(hidden_in)
    normed_mid = (hidden_in * mid_scale * norm_mid).astype(BF16)

    send_rows = pack(normed_mid, place, part)
    send_rows, expert_grads, up_s = lax.optimization_barrier((send_rows, expert_grads, up_w))
    up_o = swap(up_s)
    result, d_row, rows_in, grads_in, hidden, d_gate, d_up = run_expert(
        to_experts(send_rows), expert_grads, (gate_w, gate_o), (up_w, up_o), (down_w, down_o)
    )
    back_rows = to_experts(d_row)
    units = down_w.shape[0]
    others = ((hidden[:, units:], grads_in), (rows_in, d_gate[:, units:]), (rows_in, d_up[:, units:]))
    sent = [dot(left, right, ((0,), (0,))).astype(BF16) for left, right in others]
    gate_came, up_first = swap(sent[1]), swap(sent[2][: width // 2])
    *sent, rows_k, grads_k = lax.optimization_barrier((*sent, rows_in, grads_in))
    kept = [
        dot(left, right, ((0,), (0,)))
        for left, right in (
            (hidden[:, :units], grads_k), (rows_k, d_gate[:, :units]), (rows_k, d_up[:, :units])
        )
    ]

    back_rows, result, gate_came, *kept = lax.optimization_barrier((back_rows, result, gate_came, *kept))
    d_mid = to_tokens(back_rows, place, part)
    d_mid_in, grad_norm_mid = norm_back(hidden_in, mid_scale, norm_mid, d_mid)
    d_hidden_in = grad + d_mid_in
    d_attended, up_first = lax.optimization_barrier((d_hidden_in.astype(BF16), up_first))
    d_whole = share_sequence(d_attended)
    d_mixed = dot(d_whole, out_full, ((1,), (0,))).astype(BF16)
    d_raw, gain_sums = attend_back(
        raw, cosine, sine, query_gain, key_gain, query, key, value, d_mixed
    )
    d_total = dot(d_raw, in_full, ((1,), (1,)))
    d_own, d_sent = halves_of(d_total, rows)

    returned = to_experts(result)
    in_grads = dot(whole, d_raw, ((0,), (0,))).astype(BF16)
    out_grads = dot(d_whole, mixed, ((0,), (0,))).astype(BF16)
    gain_row = jnp.pad(gain_sums[:2].reshape(1, -1), ((0, 0), (0, width - 2 * HD)))
    gains = jnp.pad(jnp.concatenate([grad_norm_mid[None], gain_row]), ((1, 5), (0, 0)))
    in_grads, returned = lax.optimization_barrier((in_grads, returned))
    in_total, out_total, gains, d_came, output, of_expert, down_came, up_second = reduce_grads(
        in_grads, out_grads, gains, d_own, d_sent.astype(BF16), inputs * in_scale,
        (returned, place, part, place_weight, part_weight, out_grad, hidden_in),
        (sent[0], sent[2][width // 2 :]),
    )
    grad_route = jnp.sum(jnp.where(names, of_expert.T[:, None, :], 0.0), axis=2)
    d_normed = d_own + d_came.astype(F32)
    d_inputs, _ = norm_back(inputs, in_scale, norm_in, d_normed)
    grad_tokens = (d_hidden_in + d_inputs).astype(BF16)
    grad_down, grad_gate, grad_up = [
        (own + half.astype(F32))[None] for own, half in zip(kept, (down_came, gate_came, jnp.concatenate([up_first, up_second])))
    ]
    grad_norm_in, grad_norm_mid = gains[0], gains[1]
    grad_query_gain, grad_key_gain = gains[2, :HD], gains[2, HD : 2 * HD]
    return (
        output,
        grad_tokens,
        grad_norm_in,
        in_total[:, :q_cols],
        in_total[:, q_cols : q_cols + k_cols],
        in_total[:, q_cols + k_cols :],
        grad_query_gain,
        grad_key_gain,
        out_total.T,
        grad_norm_mid,
        grad_route,
        grad_gate,
        grad_up,
        grad_down,
    )


def solution(mesh):
    tokens_spec = P(("dp", "tensor"), None)
    columns, rows = P("dp", None, "tensor"), P("dp", "tensor", None)
    proj = P("dp", "tensor")
    return jax.shard_map(
        per_device,
        mesh=mesh,
        in_specs=(
            tokens_spec,
            P("dp"),
            P(),
            proj,
            proj,
            proj,
            P(),
            P(),
            P("tensor", "dp"),
            P(),
            tokens_spec,
            tokens_spec,
            columns,
            columns,
            rows,
            tokens_spec,
        ),
        out_specs=(
            tokens_spec,
            tokens_spec,
            P(),
            proj,
            proj,
            proj,
            P(),
            P(),
            P("tensor", "dp"),
            P(),
            tokens_spec,
            columns,
            columns,
            rows,
        ),
        check_vma=False,
    )
```
